32 devices in a mesh: node: 16 (over z, x, core), feat: 2 (over y).
Axes of the slice: x: 2, y: 2, z: 4, core: 2. Of those that a mesh axis runs over, the one named last changes fastest.
Arguments:
- grid_in: bfloat16 [3, 4096, 227], P(None, ('node', 'feat')), may hold values from -6 to 6
- targets: bfloat16 [3, 4096, 83], P(None, ('node', 'feat')), may hold values from -6 to 6
- area: float32 [4096], P(('node', 'feat')), as said below
- row_count: int32 [3, 32], P(None, ('node', 'feat')), may hold values from 64 to 128, as said below
- g2m: int32 [4096, 8], P('node'), may hold values from 0 to 255
- m2g: int32 [4096, 3], P('node'), may hold values from 0 to 255
- senders: int32 [4096, 16], P('node'), may hold values from 0 to 511
- edge_count: int32 [32], P('node'), may hold values from 4 to 16, as said below
- mat_w: float32 [12, 512, 512], P(None, ('node', 'feat')), may hold values from -0.25 to 0.25
- mat_m: float32 [12, 512, 512], P(None, ('node', 'feat')), may hold values from -0.00015258789 to 0.00015258789
- mat_v: float32 [12, 512, 512], P(None, ('node', 'feat')), may hold values from 7.553856e-10 to 3.0215423e-09
- in_w: float32 [227, 512], P(None, ('node', 'feat')), may hold values from -0.375 to 0.375
- in_m: float32 [227, 512], P(None, ('node', 'feat')), may hold values from -0.00015258789 to 0.00015258789
- in_v: float32 [227, 512], P(None, ('node', 'feat')), may hold values from 7.553856e-10 to 3.0215423e-09
- out_w: float32 [512, 83], P(('node', 'feat')), may hold values from -0.25 to 0.25
- out_m: float32 [512, 83], P(('node', 'feat')), may hold values from -0.00015258789 to 0.00015258789
- out_v: float32 [512, 83], P(('node', 'feat')), may hold values from 7.553856e-10 to 3.0215423e-09
- gain_w: float32 [5, 512], P(None, ('node', 'feat')), may hold values from 0.5 to 1.5
- gain_m: float32 [5, 512], P(None, ('node', 'feat')), may hold values from -0.00061035156 to 0.00061035156
- gain_v: float32 [5, 512], P(None, ('node', 'feat')), may hold values from 3.0215423e-09 to 4.8344678e-08
- bias_w: float32 [5, 512], P(None, ('node', 'feat')), may hold values from -2 to 2
- bias_m: float32 [5, 512], P(None, ('node', 'feat')), may hold values from -0.00061035156 to 0.00061035156
- bias_v: float32 [5, 512], P(None, ('node', 'feat')), may hold values from 3.0215423e-09 to 4.8344678e-08
Outputs:
- mat_new: float32 [12, 512, 512], P(None, ('node', 'feat'))
- mat_first: float32 [12, 512, 512], P(None, ('node', 'feat'))
- mat_second: float32 [12, 512, 512], P(None, ('node', 'feat'))
- mat_copy: bfloat16 [12, 512, 512], P(None, ('node', 'feat'))
- in_new: float32 [227, 512], P(None, ('node', 'feat'))
- in_first: float32 [227, 512], P(None, ('node', 'feat'))
- in_second: float32 [227, 512], P(None, ('node', 'feat'))
- in_copy: bfloat16 [227, 512], P(None, ('node', 'feat'))
- out_new: float32 [512, 83], P(('node', 'feat'))
- out_first: float32 [512, 83], P(('node', 'feat'))
- out_second: float32 [512, 83], P(('node', 'feat'))
- out_copy: bfloat16 [512, 83], P(('node', 'feat'))
- gain_new: float32 [5, 512], P(None, ('node', 'feat'))
- gain_first: float32 [5, 512], P(None, ('node', 'feat'))
- gain_second: float32 [5, 512], P(None, ('node', 'feat'))
- gain_copy: bfloat16 [5, 512], P(None, ('node', 'feat'))
- bias_new: float32 [5, 512], P(None, ('node', 'feat'))
- bias_first: float32 [5, 512], P(None, ('node', 'feat'))
- bias_second: float32 [5, 512], P(None, ('node', 'feat'))
- bias_copy: bfloat16 [5, 512], P(None, ('node', 'feat'))
- loss_sum: float32 [], replicated
- weight_total: float32 [], replicated
- grad_norm: float32 [], replicated
The draws below stay inside these ranges and needn't reach their ends.
Inputs may be any that keep to these rules, and one draw needn't show every extreme that they name: `row_count`: each device's count of live grid rows in a micro-batch; some device has all. `edge_count`: live slots of an adjacency block; some block has all. `area`: positive; padded rows are those beyond row_count.
All inputs are finite; a program needn't handle non-finite values.
Results may differ from the reference program's by a relative error of at most 0.002.
Values may be sent and summed in bfloat16 or wider, within the bound.
A program may use at most 256 MiB of HBM per device.

```python
import math
import jax
import jax.numpy as jnp
from jax import lax

D = 512
HEADS = 8
HEAD_WIDTH = 64
C_IN = 227
C_OUT = 83
LAYERS = 2
NMB = 3
STEP = 5
BLOCK = 128
K_E = 16
K_G = 8
K_M = 3
M_DEV = 256
G_DEV = 128
M = 4096
G = 4096
NMAT = 12
NGAIN = 5
NPAR = 3309568
N_NODE = 16
N_FEAT = 2


def draw_area(key, part):
    key = jax.random.fold_in(key, 11)
    ramp = jnp.arange(G, dtype=jnp.float32) / (G - 1)
    base = jnp.exp(jax.random.uniform(key, (G,), jnp.float32, 0.0, math.log(3.0)))
    return base * (1.0 + 2.0 * ramp)


def draw_row_count(key, part):
    key = jax.random.fold_in(key, 12)
    counts = jax.random.randint(key, (NMB, N_NODE * N_FEAT), G_DEV // 2, G_DEV + 1)
    return counts.at[0, 0].set(G_DEV)


def draw_edge_count(key, part):
    key = jax.random.fold_in(key, 13)
    counts = jax.random.randint(key, (M // BLOCK,), K_E // 4, K_E + 1)
    return counts.at[0].set(K_E)


def touch_ends(values, stream_key, low, top_value):
    longest = values.shape.index(max(values.shape))
    spots = []
    for shift in (0, 1):
        where = [jax.random.randint(jax.random.fold_in(stream_key, axis), (), 0, length) for axis, length in enumerate(values.shape)]
        where[longest] = (where[longest] + shift) % values.shape[longest]
        spots.append(tuple(where))
    return values.at[spots[0]].set(low).at[spots[1]].set(top_value)


def steps_of(key, shape, pieces, least, largest):
    level = 1.0
    for position, shards_of in pieces:
        heights = jax.random.uniform(jax.random.fold_in(jax.random.fold_in(key, 6), position), (shards_of,), jnp.float32, least / len(pieces), largest / len(pieces))
        level = level * jnp.repeat(jnp.exp(heights), shape[position] // shards_of).reshape((-1,) + (1,) * (len(shape) - 1 - position))
    return level


def bell_draw(key, extent, scale, reach, pieces=(), kind=jnp.bfloat16):
    array = jax.random.normal(key, extent, jnp.float32) * scale
    if len(pieces) > 0:
        array = steps_of(key, extent, pieces, -0.22, 0.18) * array
    return jnp.clip(array, min=-reach, max=reach).astype(kind)


def setup_inputs(seed: int = 0) -> dict:
    streams_of = jax.random.split(jax.random.key(seed), 24)
    grid_in = bell_draw(streams_of[0], (NMB, G, C_IN), 1.0, 6.0, ((1, 32),))
    targets = bell_draw(streams_of[1], (NMB, G, C_OUT), 1.0, 6.0, ((1, 32),))
    area = draw_area(jax.random.fold_in(streams_of[23], 71), 0)
    row_count = draw_row_count(jax.random.fold_in(streams_of[23], 71), 0)
    g2m = touch_ends(jax.random.randint(streams_of[4], (M, K_G), 0, 2 * G_DEV), jax.random.fold_in(streams_of[4], 1), 0, (2 * G_DEV) - 1).astype(jnp.int32)
    m2g = touch_ends(jax.random.randint(streams_of[5], (G, K_M), 0, M_DEV), jax.random.fold_in(streams_of[5], 1), 0, M_DEV - 1).astype(jnp.int32)
    senders = touch_ends(jax.random.randint(streams_of[6], (M, K_E), 0, 2 * M_DEV), jax.random.fold_in(streams_of[6], 1), 0, (2 * M_DEV) - 1).astype(jnp.int32)
    edge_count = draw_edge_count(jax.random.fold_in(streams_of[23], 71), 0)
    mat_w = bell_draw(streams_of[8], (NMAT, D, D), D ** -0.5, 0.25, ((1, 32),), jnp.float32)
    mat_m = bell_draw(streams_of[9], (NMAT, D, D), ((400 * NPAR) ** -0.5), 0.00015258789, ((1, 32),), jnp.float32)
    mat_v = jnp.clip(jnp.exp(math.log(3.0215423496571248e-09) - 1.3862944 * jax.random.uniform(streams_of[10], (NMAT, D, D), jnp.float32) ** steps_of(streams_of[10], (NMAT, D, D), ((1, 32),), -0.2, 0.2)), 7.553855874142812e-10, 3.0215423496571248e-09)
    in_w = bell_draw(streams_of[11], (C_IN, D), C_IN ** -0.5, 0.375, ((1, 32),), jnp.float32)
    in_m = bell_draw(streams_of[12], (C_IN, D), ((400 * NPAR) ** -0.5), 0.00015258789, ((1, 32),), jnp.float32)
    in_v = jnp.clip(jnp.exp(math.log(3.0215423496571248e-09) - 1.3862944 * jax.random.uniform(streams_of[13], (C_IN, D), jnp.float32) ** steps_of(streams_of[13], (C_IN, D), ((1, 32),), -0.2, 0.2)), 7.553855874142812e-10, 3.0215423496571248e-09)
    out_w = bell_draw(streams_of[14], (D, C_OUT), D ** -0.5, 0.25, ((0, 32),), jnp.float32)
    out_m = bell_draw(streams_of[15], (D, C_OUT), ((400 * NPAR) ** -0.5), 0.00015258789, ((0, 32),), jnp.float32)
    out_v = jnp.clip(jnp.exp(math.log(3.0215423496571248e-09) - 1.3862944 * jax.random.uniform(streams_of[16], (D, C_OUT), jnp.float32) ** steps_of(streams_of[16], (D, C_OUT), ((0, 32),), -0.2, 0.2)), 7.553855874142812e-10, 3.0215423496571248e-09)
    gain_w = jnp.clip(1.0 + 0.1 * jax.random.normal(streams_of[17], (NGAIN, D), jnp.float32), 0.5, 1.5)
    gain_m = bell_draw(streams_of[18], (NGAIN, D), (4 * (400 * NPAR) ** -0.5), 0.00061035156, ((1, 32),), jnp.float32)
    gain_v = jnp.clip(jnp.exp(math.log(4.8344677594513996e-08) - 2.7725887 * jax.random.uniform(streams_of[19], (NGAIN, D), jnp.float32) ** steps_of(streams_of[19], (NGAIN, D), ((1, 32),), -0.2, 0.2)), 3.0215423496571248e-09, 4.8344677594513996e-08)
    bias_w = bell_draw(streams_of[20], (NGAIN, D), 0.3, 2.0, ((1, 32),), jnp.float32)
    bias_m = bell_draw(streams_of[21], (NGAIN, D), (4 * (400 * NPAR) ** -0.5), 0.00061035156, ((1, 32),), jnp.float32)
    bias_v = jnp.clip(jnp.exp(math.log(4.8344677594513996e-08) - 2.7725887 * jax.random.uniform(streams_of[22], (NGAIN, D), jnp.float32) ** steps_of(streams_of[22], (NGAIN, D), ((1, 32),), -0.2, 0.2)), 3.0215423496571248e-09, 4.8344677594513996e-08)
    return {"grid_in": grid_in, "targets": targets, "area": area, "row_count": row_count, "g2m": g2m, "m2g": m2g, "senders": senders, "edge_count": edge_count, "mat_w": mat_w, "mat_m": mat_m, "mat_v": mat_v, "in_w": in_w, "in_m": in_m, "in_v": in_v, "out_w": out_w, "out_m": out_m, "out_v": out_v, "gain_w": gain_w, "gain_m": gain_m, "gain_v": gain_v, "bias_w": bias_w, "bias_m": bias_m, "bias_v": bias_v}


NORM_EPS = 1e-05
CLIP = 0.05
RATE = 0.02
BETA_ONE = 0.5
BETA_TWO = 0.5
DECAY = 0.01
ADAM_EPS = 1e-08
MASKED = -1000000000.0
HIGH_PRECISION = lax.Precision.HIGHEST

@jax.custom_vjp
def reduced_precision(v):
    return lax.optimization_barrier(v.astype(jnp.bfloat16)).astype(jnp.float32)

@jax.custom_vjp
def reduced_backward(v):
    return v

def low_keep(v):
    return (reduced_precision(v), None)

def low_pass(kept, grad):
    return (grad,)

def back_keep(v):
    return (v, None)

def back_low(kept, grad):
    return (reduced_precision(grad),)
reduced_precision.defvjp(low_keep, low_pass)
reduced_backward.defvjp(back_keep, back_low)

def send_low(value):
    return reduced_backward(reduced_precision(value))

def product(left, right):
    return jnp.dot(left, right, precision=HIGH_PRECISION)

def layer_norm(state, gain):
    centre = state - lax.optimization_barrier(jnp.mean(state, axis=-1, keepdims=True))
    spread = lax.optimization_barrier(jnp.mean(centre * centre, axis=-1, keepdims=True))
    return centre * lax.rsqrt(spread + NORM_EPS) * gain

def mean_block(pair):
    table, index = pair
    return lax.optimization_barrier(jnp.mean(jnp.take(table, index, axis=0), axis=1))

def blocked_mean(table, index):
    picked = lax.map(jax.checkpoint(mean_block), (table, index))
    return picked.reshape(-1, table.shape[-1])

def attend_block(group):
    queries, keys_all, values_all, sender_ids, allowed = group
    row_total = queries.shape[0]
    keys_per_edge = jnp.take(keys_all, sender_ids, axis=0).reshape(row_total, K_E, HEADS, HEAD_WIDTH)
    values_per_edge = jnp.take(values_all, sender_ids, axis=0).reshape(row_total, K_E, HEADS, HEAD_WIDTH)
    query_per_head = queries.reshape(row_total, HEADS, HEAD_WIDTH)
    edge_scores = reduced_backward(jnp.einsum('lgz,lpgz->lgp', query_per_head, keys_per_edge, precision=HIGH_PRECISION) * HEAD_WIDTH ** (-0.5))
    edge_scores = jnp.where(allowed[:, None, :], edge_scores, MASKED)
    expo = jnp.exp(edge_scores - lax.optimization_barrier(jnp.max(edge_scores, axis=-1, keepdims=True)))
    attention_probabilities = expo / lax.optimization_barrier(jnp.sum(expo, axis=-1, keepdims=True))
    mixed_values = jnp.einsum('vzn,vnzb->vzb', reduced_precision(attention_probabilities), values_per_edge, precision=HIGH_PRECISION)
    return mixed_values.reshape(row_total, D)

def attention(queries, keys_loc, values_loc, senders, allowed):
    keys_three = keys_loc.reshape(N_NODE, M_DEV, D)
    values_three = values_loc.reshape(N_NODE, M_DEV, D)
    keys_all = jnp.concatenate([keys_three, jnp.roll(keys_three, 1, axis=0)], axis=1)
    values_all = jnp.concatenate([values_three, jnp.roll(values_three, 1, axis=0)], axis=1)
    mixed_values = lax.map(jax.checkpoint(attend_block), (queries.reshape(N_NODE, M_DEV, D), keys_all, values_all, senders.reshape(N_NODE, M_DEV, K_E), allowed.reshape(N_NODE, M_DEV, K_E)))
    return mixed_values.reshape(-1, D)

def forward(params, grid_rows, target, wrow, g2m, m2g, senders, allowed):
    mats, inputs, outputs, gains, biases = [reduced_precision(param) for param in params]
    pre_enc = reduced_backward(product(grid_rows, inputs) + biases[0])
    encoded = send_low(jax.nn.silu(pre_enc))
    state = send_low(blocked_mean(encoded.reshape(N_NODE, 2 * G_DEV, D), g2m.reshape(N_NODE, M_DEV, K_G)))
    for layer in range(LAYERS):
        base = 6 * layer
        normed = reduced_precision(layer_norm(state, gains[2 * layer]))
        queries = send_low(product(normed, mats[base]))
        keys_loc = send_low(product(normed, mats[base + 1]))
        values_loc = send_low(product(normed, mats[base + 2]))
        mixed_values = send_low(attention(queries, keys_loc, values_loc, senders, allowed))
        middle = state + reduced_backward(product(mixed_values, mats[base + 3]))
        normed_mlp = reduced_precision(layer_norm(middle, gains[2 * layer + 1]))
        pre_mlp = reduced_backward(product(normed_mlp, mats[base + 4]) + biases[1 + 2 * layer])
        hidden = reduced_precision(jax.nn.silu(pre_mlp))
        state = middle + reduced_backward(product(hidden, mats[base + 5])) + biases[2 + 2 * layer]
    last = send_low(state)
    decoded = send_low(blocked_mean(last.reshape(N_NODE, M_DEV, D), m2g.reshape(N_NODE, 2 * G_DEV, K_M)))
    predict = reduced_backward(product(reduced_precision(layer_norm(decoded, gains[2 * LAYERS])), outputs))
    error = predict - target
    return jnp.sum(wrow[:, None] * error * error)

def adam(weight, first, second, grad):
    first_new = BETA_ONE * first + (1.0 - BETA_ONE) * grad
    second_new = BETA_TWO * second + (1.0 - BETA_TWO) * grad * grad
    first_hat = first_new / (1.0 - BETA_ONE ** STEP)
    second_hat = second_new / (1.0 - BETA_TWO ** STEP)
    weight_new = weight - RATE * (first_hat / (jnp.sqrt(second_hat) + ADAM_EPS) + DECAY * weight)
    return (weight_new, first_new, second_new, weight_new.astype(jnp.bfloat16))

def reference(grid_in, targets, area, row_count, g2m, m2g, senders, edge_count, mat_w, mat_m, mat_v, in_w, in_m, in_v, out_w, out_m, out_v, gain_w, gain_m, gain_v, bias_w, bias_m, bias_v):
    live = (jnp.arange(G) % G_DEV)[None, :] < jnp.repeat(row_count, G_DEV, axis=1)
    weights_all = area[None, :] * live.astype(jnp.float32)
    weight_total = jnp.sum(weights_all) * C_OUT
    allowed = jnp.arange(K_E)[None, :] < jnp.repeat(edge_count, BLOCK)[:, None]
    params = (mat_w, in_w, out_w, gain_w, bias_w)
    totals = tuple((jnp.zeros(param.shape, jnp.float32) for param in params))
    loss_sum = jnp.float32(0.0)
    for batch in range(NMB):
        grid_rows = grid_in[batch].astype(jnp.float32)
        target = targets[batch].astype(jnp.float32)
        wrow = weights_all[batch]

        def objective(weights):
            part = forward(weights, grid_rows, target, wrow, g2m, m2g, senders, allowed)
            return (part / weight_total, part)
        value, backward, part = jax.vjp(objective, params, has_aux=True)
        grads = backward(jnp.float32(1.0))[0]
        totals = tuple((total + grad for total, grad in zip(totals, grads)))
        loss_sum = loss_sum + part
    grad_norm = jnp.sqrt(sum((jnp.sum(total * total) for total in totals)))
    factor = jnp.minimum(1.0, CLIP / (grad_norm + 1e-06))
    mat_new, mat_first, mat_second, mat_copy = adam(mat_w, mat_m, mat_v, factor * totals[0])
    in_new, in_first, in_second, in_copy = adam(in_w, in_m, in_v, factor * totals[1])
    out_new, out_first, out_second, out_copy = adam(out_w, out_m, out_v, factor * totals[2])
    gain_new, gain_first, gain_second, gain_copy = adam(gain_w, gain_m, gain_v, factor * totals[3])
    bias_new, bias_first, bias_second, bias_copy = adam(bias_w, bias_m, bias_v, factor * totals[4])
    return (mat_new, mat_first, mat_second, mat_copy, in_new, in_first, in_second, in_copy, out_new, out_first, out_second, out_copy, gain_new, gain_first, gain_second, gain_copy, bias_new, bias_first, bias_second, bias_copy, loss_sum, weight_total, grad_norm)
```

```python
import functools

import jax
import jax.numpy as jnp
from jax import lax
from jax.experimental import pallas as pl
from jax.experimental.pallas import tpu as pltpu
from jax.sharding import PartitionSpec as P

HEADS = 8
STEP = 5
NORM_EPS = 1e-05
CLIP = 0.05
RATE = 0.02
BETA_ONE = 0.5
BETA_TWO = 0.5
DECAY = 0.01
ADAM_EPS = 1e-08
DEAD = -1e30
MESH = pl.DeviceIdType.MESH
F32 = jnp.float32
BF16 = jnp.bfloat16


def nn(left, right):
    return jnp.dot(left, right, preferred_element_type=F32)


def nt(left, right):
    return lax.dot_general(left, right, (((1,), (1,)), ((), ())), preferred_element_type=F32)


def tn(left, right):
    return lax.dot_general(left, right, (((0,), (0,)), ((), ())), preferred_element_type=F32)


def norm_parts(state):
    centre = state - jnp.mean(state, axis=-1, keepdims=True)
    spread = jnp.mean(centre * centre, axis=-1, keepdims=True)
    scale = lax.rsqrt(spread + NORM_EPS)
    return centre * scale, scale


def norm_back(grad, hat, scale, gain):
    inner = grad * gain
    mean_inner = jnp.mean(inner, axis=-1, keepdims=True)
    mean_hat = jnp.mean(inner * hat, axis=-1, keepdims=True)
    return scale * (inner - mean_inner - hat * mean_hat)


def column_sum(value):
    return jnp.sum(value, axis=0, keepdims=True)


def sigmoid(value):
    return 1.0 / (1.0 + jnp.exp(-value))


def silu_slope(value):
    gate = sigmoid(value)
    return gate * (1.0 + value * (1.0 - gate))


class Sizes:
    def __init__(self, node, feat, batches, half, width, layers, heads, slots, c_in, c_out):
        self.node, self.feat = node, feat
        self.batches, self.half, self.width = batches, half, width
        self.rows = 2 * half
        self.layers, self.heads, self.slots = layers, heads, slots
        self.c_in, self.c_out = c_in, c_out
        self.shard = width // (node * feat)
        self.depth = node // 4
        self.mats = 6 * layers + 1
        self.cols = width // feat
        self.near = heads // feat
        self.fused = self.shard % 16 == 0 and node % 4 == 0
        groups = [(0, 4)]
        for first in range(4, self.mats, 3):
            groups.append((first, 3))
        self.groups = groups


def step_kernel(sz, *refs):
    refs = list(refs)

    def take(count):
        out = refs[:count]
        del refs[:count]
        return out

    grid_ref, target_ref, area_ref, count_ref, g2m_ref, m2g_ref, send_ref, edge_ref = take(8)
    if sz.fused:
        mat_ref, in_ref, out_ref, gain_ref, bias_ref = take(5)
        share, scalars = take(2)
        full, total = take(2)
    else:
        full, weight_ref = take(2)
        total, scalars = take(2)
    (
        rows_in,
        aim,
        pre_enc,
        state,
        middle,
        pre_mlp,
        mixed,
        query,
        pair,
        prob,
        edge_bias,
        g_row,
        g_col,
        m_row,
        m_col,
        affine,
        affine_grad,
        final,
        grad_pred,
        low,
        pre_low,
        mid_low,
        n_one,
        n_two,
        hidden,
        d_own,
        d_far,
        pair_out,
        pair_in,
        loss_acc,
    ) = take(30)
    (s_rows, r_rows, s_aim, r_aim, s_kv, r_kv, s_mix, r_mix, s_pair, r_pair, s_far, r_far) = take(12)
    if sz.fused:
        got_c, got_x, got_z, got_y, tile, tile_far, tile_z = take(7)
        (gz_s, gz_r, g2_s, g2_r, g3_s, g3_r, g4_s, g4_r) = take(8)
        (rc_s, rc_r, rx_s, rx_r, rz_s, rz_r, ry_s, ry_r) = take(8)
        (t_s, t_r, tz_s, tz_r) = take(4)

    nb, rows, half, width, cols = sz.batches, sz.rows, sz.half, sz.width, sz.cols
    node = lax.axis_index("node")
    j = lax.axis_index("feat")
    other = 1 - j
    after = lax.rem(node + 1, sz.node)
    before = lax.rem(node + sz.node - 1, sz.node)
    partner = (node, other)
    mine = pl.ds(pl.multiple_of(j * cols, cols), cols)
    theirs = pl.ds(pl.multiple_of(other * cols, cols), cols)
    waits = []

    def remote(src, dst, s_sem, r_sem, device):
        return pltpu.make_async_remote_copy(
            src_ref=src, dst_ref=dst, send_sem=s_sem, recv_sem=r_sem, device_id=device, device_id_type=MESH
        )

    barrier = pltpu.get_barrier_semaphore()
    greet = [(after, j), (before, j), partner]
    if sz.fused:
        depth = sz.depth
        c = lax.rem(node, 2)
        x = lax.rem(node // 2, 2)
        z = node // 4

        def place(zz, xx, cc):
            return zz * 4 + xx * 2 + cc

        core_dev = (place(z, x, 1 - c), j)
        x_dev = (place(z, 1 - x, c), j)
        z_devs = [(place(lax.rem(z + step, depth), x, c), j) for step in range(1, depth)]
        greet = greet + [core_dev, x_dev] + z_devs
    for device in greet:
        pl.semaphore_signal(barrier, inc=1, device_id=device, device_id_type=MESH)
    pl.semaphore_wait(barrier, len(greet))

    lanes_c = lax.broadcasted_iota(jnp.int32, (1, cols), 1) // (width // sz.heads)
    mask_low = [(lanes_c == head).astype(F32).astype(BF16) for head in range(sz.near)]
    mask_full = [(lanes_c == head).astype(F32) for head in range(sz.near)]

    def w_full(index):
        return full[index].reshape(width, width)

    def w_cols(index, which):
        if sz.fused:
            return full[index, :, :, :, :, :, which].reshape(width, cols)
        return full[index, :, :, which].reshape(width, cols)

    def w_rows(index, which):
        if sz.fused:
            count = sz.depth // 2
            return full[index, pl.ds(which * count, count)].reshape(width // 2, width)
        return full[index, which]

    def put_total(index, value):
        total[index] = value.reshape(total.shape[1:])

    if sz.fused:
        n_groups = len(sz.groups)
        packed = jnp.concatenate(
            [
                in_ref[...],
                jnp.zeros((sz.shard, 256 - sz.c_in), F32),
                jnp.zeros((sz.shard, 128), F32),
                out_ref[...],
                jnp.zeros((sz.shard, 128 - sz.c_out), F32),
            ],
            axis=1,
        )
        small = jnp.concatenate(
            [
                gain_ref[...],
                jnp.zeros((3, sz.shard), F32),
                bias_ref[...],
                jnp.zeros((3, sz.shard), F32),
            ],
            axis=0,
        )
        small = jnp.concatenate([small, jnp.zeros((16, 128 - sz.shard), F32)], axis=1)
        small = jnp.concatenate([small, jnp.zeros((112, 128), F32)], axis=0)
        small = jnp.transpose(small)[0 : sz.shard, :]
        full[0, z, x, c, j] = jnp.concatenate([packed[:, 0:256], small, packed[:, 384:512]], axis=1).astype(BF16)
        for index in range(sz.mats - 1):
            full[1 + index, z, x, c, j] = mat_ref[index].astype(BF16)
        for g, (first, count) in enumerate(sz.groups):
            span = pl.ds(first, count)
            own = full.at[span, z, x, c, j]
            for step in range(1, depth):
                copy = remote(own, own, gz_s.at[g, step - 1], gz_r.at[g, step - 1], z_devs[step - 1])
                copy.start()
                waits.append(copy)

    for b in range(nb):
        block = jnp.concatenate(
            [grid_ref[b].astype(F32), jnp.zeros((256 - sz.c_in, half), F32)], axis=0
        )
        rows_in[b, j] = jnp.transpose(block).astype(BF16)
    cell = lax.broadcasted_iota(jnp.int32, (1, half), 1)
    for b in range(nb):
        weight = jnp.where(cell < count_ref[b : b + 1, 0:1], area_ref[...], 0.0)
        block = jnp.concatenate(
            [
                target_ref[b].astype(F32),
                jnp.zeros((127 - sz.c_out, half), F32),
                weight,
            ],
            axis=0,
        )
        aim[b, j] = jnp.transpose(block)
    copy_rows = remote(rows_in.at[:, j], rows_in.at[:, j], s_rows, r_rows, partner)
    copy_aim = remote(aim.at[:, j], aim.at[:, j], s_aim, r_aim, partner)
    copy_rows.start()
    copy_aim.start()
    waits += [copy_rows, copy_aim]

    if sz.fused:
        weight_sum = jnp.zeros((1, 1), F32)
        for b in range(nb):
            weight = jnp.where(cell < count_ref[b : b + 1, 0:1], area_ref[...], 0.0)
            weight_sum = weight_sum + jnp.sum(weight, axis=1, keepdims=True)
        tile[0, 0] = jnp.broadcast_to(weight_sum * float(sz.c_out), (8, 128))

        def tile_reduce(slot):
            for level, device in enumerate((core_dev, x_dev, partner)):
                copy = remote(
                    tile.at[slot, level], tile_far.at[slot, level], t_s.at[slot, level], t_r.at[slot, level], device
                )
                copy.start()
                copy.wait()
                tile[slot, level + 1] = tile[slot, level] + tile_far[slot, level]
            tile_z[slot, z] = tile[slot, 3]
            copies = []
            for step in range(1, depth):
                copy = remote(
                    tile.at[slot, 3], tile_z.at[slot, z], tz_s.at[slot, step - 1], tz_r.at[slot, step - 1], z_devs[step - 1]
                )
                copy.start()
                copies.append(copy)
            for step in range(1, depth):
                copies[step - 1].wait_send()
                source = lax.rem(z + depth - step, depth)
                remote(
                    tile.at[slot, 3], tile_z.at[slot, source], tz_s.at[slot, step - 1], tz_r.at[slot, step - 1], z_devs[step - 1]
                ).wait_recv()
            result = tile_z[slot, 0]
            for index in range(1, depth):
                result = result + tile_z[slot, index]
            return result

    def counts(ref, slots, height, live=None):
        wide = lax.broadcasted_iota(jnp.int32, (height, rows), 0)
        acc = jnp.zeros((height, rows), F32)
        for slot in range(slots):
            hit = wide == ref[slot : slot + 1, :]
            if live is not None:
                hit = jnp.logical_and(hit, live > slot)
            acc = acc + jnp.where(hit, 1.0, 0.0)
        return acc

    receiver = lax.broadcasted_iota(jnp.int32, (1, rows), 1)
    live = jnp.where(receiver < rows // 2, edge_ref[0:1, 0:1], edge_ref[0:1, 1:2])
    for part in range(2):
        wide = lax.broadcasted_iota(jnp.int32, (rows, rows), 0) + part * rows
        acc = jnp.zeros((rows, rows), F32)
        for slot in range(sz.slots):
            hit = jnp.logical_and(wide == send_ref[slot : slot + 1, :], live > slot)
            acc = acc + jnp.where(hit, 1.0, 0.0)
        acc = jnp.transpose(acc)
        edge_bias[:, part * rows : (part + 1) * rows] = jnp.where(acc > 0.5, jnp.log(jnp.maximum(acc, 1.0)), DEAD)
    k_g = g2m_ref.shape[0]
    k_m = m2g_ref.shape[0]
    table = counts(g2m_ref, k_g, rows)
    g_col[...] = table.astype(BF16)
    g_row[...] = jnp.transpose(table).astype(BF16)
    table = counts(m2g_ref, k_m, rows)
    m_col[...] = table.astype(BF16)
    m_row[...] = jnp.transpose(table).astype(BF16)
    affine_grad[...] = jnp.zeros_like(affine_grad)
    loss_acc[...] = jnp.zeros_like(loss_acc)

    if sz.fused:
        side_a = pl.ds(0, width // 2)
        side_b = pl.ds(width // 2, width // 2)

        def gather_two(g):
            first, count = sz.groups[g]
            span = pl.ds(first, count)
            for step in range(1, depth):
                there = full.at[span, lax.rem(z + depth - step, depth), x, c, j]
                remote(there, there, gz_s.at[g, step - 1], gz_r.at[g, step - 1], z_devs[step - 1]).wait_recv()
            part = full.at[span, :, x, c, j, :, side_a]
            copy = remote(part, part, g2_s.at[g, 0], g2_r.at[g, 0], x_dev)
            copy.start()
            waits.append(copy)
            part = full.at[span, :, x, c, j, :, side_b]
            copy = remote(part, part, g2_s.at[g, 1], g2_r.at[g, 1], partner)
            copy.start()
            waits.append(copy)

        def gather_three(g):
            first, count = sz.groups[g]
            span = pl.ds(first, count)
            part = full.at[span, :, 1 - x, c, j, :, side_a]
            remote(part, part, g2_s.at[g, 0], g2_r.at[g, 0], x_dev).wait_recv()
            part = full.at[span, :, :, c, j, :, side_a]
            copy = remote(part, part, g3_s.at[g, 0], g3_r.at[g, 0], partner)
            copy.start()
            waits.append(copy)
            part = full.at[span, :, x, c, other, :, side_b]
            remote(part, part, g2_s.at[g, 1], g2_r.at[g, 1], partner).wait_recv()
            part = full.at[span, :, x, c, :, :, side_b]
            copy = remote(part, part, g3_s.at[g, 1], g3_r.at[g, 1], x_dev)
            copy.start()
            waits.append(copy)

        def gather_four(g):
            first, count = sz.groups[g]
            span = pl.ds(first, count)
            part = full.at[span, :, :, c, other, :, side_a]
            remote(part, part, g3_s.at[g, 0], g3_r.at[g, 0], partner).wait_recv()
            part = full.at[span, :, 1 - x, c, :, :, side_b]
            remote(part, part, g3_s.at[g, 1], g3_r.at[g, 1], x_dev).wait_recv()
            part = full.at[span, :, :, c]
            copy = remote(part, part, g4_s.at[g], g4_r.at[g], core_dev)
            copy.start()
            waits.append(copy)

        def gather_done(g):
            first, count = sz.groups[g]
            part = full.at[pl.ds(first, count), :, :, 1 - c]
            remote(part, part, g4_s.at[g], g4_r.at[g], core_dev).wait_recv()

        gather_two(0)
        weight_total = tile_reduce(0)
        gather_three(0)
        gather_two(1)
        gather_four(0)
        gather_three(1)
        gather_two(2)
        gather_done(0)
    else:
        weight_total = jnp.broadcast_to(weight_ref[...], (8, 128))
        n_groups = 0

        def gather_two(g):
            pass

        gather_three = gather_four = gather_done = gather_two
    scalars[1] = weight_total
    total_one = scalars[1, 0:1, 0:1]

    remote(rows_in.at[:, other], rows_in.at[:, other], s_rows, r_rows, partner).wait_recv()
    remote(aim.at[:, other], aim.at[:, other], s_aim, r_aim, partner).wait_recv()

    in_cols = pl.ds(0, 256)
    small_cols = pl.ds(256, 128)
    out_cols = pl.ds(384, 128)

    def aux(which, size):
        if sz.fused:
            return full[0, :, :, :, :, :, which].reshape(width, size)
        return full[0, :, :, which].reshape(width, size)

    affine[...] = jnp.transpose(aux(small_cols, 128).astype(F32))[0:16, :]

    def gain_row(index):
        return affine[pl.ds(index, 1), :]

    def bias_row(index):
        return affine[pl.ds(8 + index, 1), :]

    def add_affine(index, value):
        affine_grad[pl.ds(index, 1), :] = affine_grad[pl.ds(index, 1), :] + value

    def each(body):
        def wrapped(b, carry):
            body(b)
            return carry

        lax.fori_loop(0, nb, wrapped, 0)

    def encode(b):
        pre = nt(rows_in[b].reshape(rows, 256), aux(in_cols, 256)) + bias_row(0)
        pre_enc[b] = pre
        enc = (pre * sigmoid(pre)).astype(BF16)
        start = nn(g_row[...], enc) * (1.0 / k_g)
        state[0, b] = start.astype(BF16).astype(F32)

    each(encode)

    def kv_copy(layer, b):
        return remote(
            pair.at[layer, b, :, pl.ds(0, rows)],
            pair.at[layer, b, :, pl.ds(rows, rows)],
            s_kv.at[layer, b],
            r_kv.at[layer, b],
            (after, j),
        )

    def mix_copy(layer, b):
        return remote(
            mixed.at[layer, b, j], mixed.at[layer, b, j], s_mix.at[layer, b], r_mix.at[layer, b], partner
        )

    def mix_wait(layer, b):
        there = mixed.at[layer, b, other]
        remote(there, there, s_mix.at[layer, b], r_mix.at[layer, b], partner).wait_recv()

    scale = float(width // sz.heads) ** -0.5

    def forward_layer(layer):
        base = 1 + 6 * layer

        def project(b):
            hat, _ = norm_parts(state[layer, b])
            normed = (hat * gain_row(2 * layer)).astype(BF16)
            query[layer, b] = nn(normed, w_cols(base, mine)).astype(BF16)
            pair[layer, b, 0, 0:rows] = nn(normed, w_cols(base + 1, mine)).astype(BF16)
            pair[layer, b, 1, 0:rows] = nn(normed, w_cols(base + 2, mine)).astype(BF16)
            kv_copy(layer, b).start()

        def attend(b):
            kv_copy(layer, b).wait_recv()
            keys, values, queries = pair[layer, b, 0], pair[layer, b, 1], query[layer, b]
            out = jnp.zeros((rows, cols), F32)
            for head in range(sz.near):
                score = nt(queries * mask_low[head], keys) * scale + edge_bias[...]
                expo = jnp.exp(score - jnp.max(score, axis=-1, keepdims=True))
                weight = (expo * (1.0 / jnp.sum(expo, axis=-1, keepdims=True))).astype(BF16)
                prob[layer, b, head] = weight
                out = out + nn(weight, values) * mask_full[head]
            mixed[layer, b, j] = out.astype(BF16)
            mix_copy(layer, b).start()

        def mlp(b):
            mix_wait(layer, b)
            mid = (
                state[layer, b]
                + nn(mixed[layer, b, 0], w_rows(base + 3, 0))
                + nn(mixed[layer, b, 1], w_rows(base + 3, 1))
            )
            middle[layer, b] = mid
            hat, _ = norm_parts(mid)
            normed = (hat * gain_row(2 * layer + 1)).astype(BF16)
            pre = nn(normed, w_full(base + 4)) + bias_row(1 + 2 * layer)
            pre_mlp[layer, b] = pre
            act = (pre * sigmoid(pre)).astype(BF16)
            state[layer + 1, b] = mid + nn(act, w_full(base + 5)) + bias_row(2 + 2 * layer)

        each(project)
        if layer == 0:
            gather_four(1)
            gather_three(2)
            gather_two(3)
        each(attend)
        if layer == 0:
            gather_done(1)
            gather_four(2)
            gather_three(3)
        each(mlp)
        if layer == 0:
            gather_done(2)
            gather_four(3)
            gather_done(3)

    for layer in range(sz.layers):
        forward_layer(layer)

    last = sz.layers
    lane_out = lax.broadcasted_iota(jnp.int32, (1, 128), 1)
    row_index = lax.broadcasted_iota(jnp.int32, (rows, 1), 0)
    own_row = jnp.logical_and(row_index >= j * half, row_index < (j + 1) * half).astype(F32)
    real_lane = (lane_out < sz.c_out).astype(F32)

    def decode(b):
        gain = gain_row(2 * sz.layers)
        dec = (nn(m_row[...], state[last, b].astype(BF16)) * (1.0 / k_m)).astype(BF16).astype(F32)
        hat, inv = norm_parts(dec)
        normed = (hat * gain).astype(BF16)
        final[b] = normed
        weights = aux(out_cols, 128)
        goal = aim[b].reshape(rows, 128)
        error = (nn(normed, weights) - goal) * real_lane
        weight = goal[:, 127:128]
        loss_acc[...] = loss_acc[...] + jnp.sum(
            jnp.sum((weight * own_row) * error * error, axis=1, keepdims=True), axis=0, keepdims=True
        )
        pred_low = (2.0 * weight * error / total_one).astype(BF16)
        grad_pred[b] = pred_low
        back = nt(pred_low, weights)
        add_affine(2 * sz.layers, column_sum(back * hat))
        dec_low = norm_back(back, hat, inv, gain).astype(BF16)
        state[last, b] = (nn(m_col[...], dec_low) * (1.0 / k_m)).astype(BF16).astype(F32)

    each(decode)

    if sz.fused:

        def reduce_core(g):
            first, count = sz.groups[g]
            span = pl.ds(first, count)
            copy = remote(total.at[span, :, :, 1 - c], got_c.at[span], rc_s.at[g], rc_r.at[g], core_dev)
            copy.start()
            waits.append(copy)

        def reduce_x(g):
            first, count = sz.groups[g]
            span = pl.ds(first, count)
            remote(got_c.at[span], got_c.at[span], rc_s.at[g], rc_r.at[g], core_dev).wait_recv()
            for index in range(first, first + count):
                total[index, :, :, c] = total[index, :, :, c] + got_c[index]
            copy = remote(total.at[span, :, 1 - x, c], got_x.at[span], rx_s.at[g], rx_r.at[g], x_dev)
            copy.start()
            waits.append(copy)

        def reduce_z(g):
            first, count = sz.groups[g]
            span = pl.ds(first, count)
            remote(got_x.at[span], got_x.at[span], rx_s.at[g], rx_r.at[g], x_dev).wait_recv()
            for index in range(first, first + count):
                total[index, :, x, c] = total[index, :, x, c] + got_x[index]
            for step in range(1, depth):
                to = lax.rem(z + step, depth)
                copy = remote(
                    total.at[span, to, x, c],
                    got_z.at[step - 1, span],
                    rz_s.at[g, step - 1],
                    rz_r.at[g, step - 1],
                    z_devs[step - 1],
                )
                copy.start()
                waits.append(copy)

        def reduce_y(g):
            first, count = sz.groups[g]
            span = pl.ds(first, count)
            for step in range(1, depth):
                there = got_z.at[step - 1, span]
                remote(there, there, rz_s.at[g, step - 1], rz_r.at[g, step - 1], z_devs[step - 1]).wait_recv()
            for index in range(first, first + count):
                acc = total[index, z, x, c]
                for step in range(1, depth):
                    acc = acc + got_z[step - 1, index]
                total[index, z, x, c] = acc
            send = total.at[span, z, x, c, pl.ds(pl.multiple_of(other * sz.shard, sz.shard), sz.shard)]
            copy = remote(send, got_y.at[span], ry_s.at[g], ry_r.at[g], partner)
            copy.start()
            waits.append(copy)

        def reduce_done(g):
            first, count = sz.groups[g]
            span = pl.ds(first, count)
            remote(got_y.at[span], got_y.at[span], ry_s.at[g], ry_r.at[g], partner).wait_recv()
            keep = pl.ds(pl.multiple_of(j * sz.shard, sz.shard), sz.shard)
            for index in range(first, first + count):
                share[index, :, mine] = total[index, z, x, c, keep]
                share[index, :, theirs] = got_y[index]

    else:

        def reduce_core(g):
            pass

        reduce_x = reduce_z = reduce_y = reduce_done = reduce_core

    def pair_copy(layer, b):
        return remote(
            pair_out.at[b], pair_in.at[layer, b], s_pair.at[layer, b], r_pair.at[layer, b], (before, j)
        )

    def far_copy(layer, b):
        return remote(d_own.at[b], d_far.at[layer, b], s_far.at[layer, b], r_far.at[layer, b], partner)

    def backward_layer(layer):
        base = 1 + 6 * layer

        def mlp_and_attention(b):
            grad = state[last, b]
            grad_low = grad.astype(BF16)
            low[b] = grad_low
            add_affine(8 + 2 + 2 * layer, column_sum(grad))
            pre = pre_mlp[layer, b]
            hidden[b] = (pre * sigmoid(pre)).astype(BF16)
            back = (nt(grad_low, w_full(base + 5)) * silu_slope(pre)).astype(BF16)
            pre_low[b] = back
            add_affine(8 + 1 + 2 * layer, column_sum(back.astype(F32)))
            back = nt(back, w_full(base + 4))
            gain = gain_row(2 * layer + 1)
            hat, inv = norm_parts(middle[layer, b])
            n_two[b] = (hat * gain).astype(BF16)
            add_affine(2 * layer + 1, column_sum(back * hat))
            grad = grad + norm_back(back, hat, inv, gain)
            state[last, b] = grad
            grad_low = grad.astype(BF16)
            mid_low[b] = grad_low
            grad_out = nt(grad_low, w_rows(base + 3, j)).astype(BF16)
            keys, values, queries = pair[layer, b, 0], pair[layer, b, 1], query[layer, b]
            d_query = jnp.zeros((rows, cols), F32)
            d_keys = jnp.zeros((2 * rows, cols), F32)
            d_values = jnp.zeros((2 * rows, cols), F32)
            for head in range(sz.near):
                weight_low = prob[layer, b, head]
                out_head = grad_out * mask_low[head]
                weight = weight_low.astype(F32)
                part = weight * nt(out_head, values)
                score = (part - weight * jnp.sum(part, axis=-1, keepdims=True)).astype(BF16)
                d_query = d_query + nn(score, keys) * mask_full[head]
                d_keys = d_keys + tn(score, queries * mask_low[head])
                d_values = d_values + tn(weight_low, out_head)
            d_own[b, :, 0:cols] = (d_query * scale).astype(BF16)
            d_keys = d_keys * scale
            pair_out[b, 0] = d_keys[rows:].astype(BF16)
            pair_out[b, 1] = d_values[rows:].astype(BF16)
            pair_copy(layer, b).start()
            pre_mlp[layer, b, :, 0:cols] = d_keys[0:rows]
            pre_mlp[layer, b, :, cols : 2 * cols] = d_values[0:rows]

        each(mlp_and_attention)
        many = nb * rows
        put_total(base + 5, tn(hidden[...].reshape(many, width), low[:, :, mine].reshape(many, cols)))
        put_total(base + 4, tn(n_two[...].reshape(many, width), pre_low[:, :, mine].reshape(many, cols)))
        grad_mid = mid_low[:, :, mine].reshape(many, cols)
        put_total(
            base + 3,
            jnp.concatenate(
                [
                    tn(mixed[layer, :, 0].reshape(many, cols), grad_mid),
                    tn(mixed[layer, :, 1].reshape(many, cols), grad_mid),
                ],
                axis=0,
            ),
        )
        reduce_core(2 * layer + 1)

        def finish_pair(b):
            pair_copy(layer, b).wait()
            d_own[b, :, cols : 2 * cols] = (pre_mlp[layer, b, :, 0:cols] + pair_in[layer, b, 0].astype(F32)).astype(BF16)
            d_own[b, :, 2 * cols : 3 * cols] = (
                pre_mlp[layer, b, :, cols : 2 * cols] + pair_in[layer, b, 1].astype(F32)
            ).astype(BF16)
            far_copy(layer, b).start()
            hat, _ = norm_parts(state[layer, b])
            n_one[b] = (hat * gain_row(2 * layer)).astype(BF16)

        each(finish_pair)
        reduce_x(2 * layer + 1)
        if layer + 1 < sz.layers:
            reduce_y(2 * layer + 3)
            reduce_z(2 * layer + 2)
        outer = tn(n_one[...].reshape(many, width), d_own[...].reshape(many, 3 * cols))
        for which in range(3):
            put_total(base + which, outer[:, which * cols : (which + 1) * cols])
        if layer > 0:
            reduce_core(2 * layer)

        def join(b):
            far_copy(layer, b).wait()
            back = jnp.zeros((rows, width), F32)
            for which in range(3):
                part = pl.ds(which * cols, cols)
                back = back + nt(d_own[b, :, part], w_cols(base + which, mine))
                back = back + nt(d_far[layer, b, :, part], w_cols(base + which, theirs))
            gain = gain_row(2 * layer)
            hat, inv = norm_parts(state[layer, b])
            add_affine(2 * layer, column_sum(back * hat))
            state[last, b] = state[last, b] + norm_back(back, hat, inv, gain)

        each(join)
        reduce_z(2 * layer + 1)
        if layer > 0:
            reduce_x(2 * layer)

    for layer in reversed(range(sz.layers)):
        backward_layer(layer)

    def encode_back(b):
        back = nn(g_col[...], state[last, b].astype(BF16)) * (1.0 / k_g)
        back = (back.astype(BF16).astype(F32) * silu_slope(pre_enc[b])).astype(BF16)
        pre_low[b] = back
        add_affine(8, column_sum(back.astype(F32)))

    each(encode_back)
    many = nb * rows
    wide = jnp.concatenate([affine_grad[...], jnp.zeros((112, width), F32)], axis=0)

    @pl.when(j == 0)
    def _():
        put_total(0, tn(pre_low[...].reshape(many, width), rows_in[...].reshape(many, 256)))

    @pl.when(j == 1)
    def _():
        put_total(
            0,
            jnp.concatenate(
                [
                    jnp.transpose(wide),
                    tn(final[...].reshape(many, width), grad_pred[...].reshape(many, 128)),
                ],
                axis=1,
            ),
        )

    if sz.fused:
        reduce_core(0)
        if sz.layers > 1:
            reduce_y(2)
        reduce_x(0)
        reduce_y(1)
        reduce_z(0)
        for g in range(1, n_groups):
            reduce_done(g)
        reduce_y(0)
        reduce_done(0)
        squares = jnp.zeros((1, 1), F32)
        for index in range(sz.mats):
            value = share[index]
            squares = squares + jnp.sum(
                jnp.sum(value * value, axis=1, keepdims=True), axis=0, keepdims=True
            )
        sub = lax.broadcasted_iota(jnp.int32, (8, 128), 0)
        tile[1, 0] = jnp.where(sub == 0, squares, loss_acc[0:1, 0:1])
        result = tile_reduce(1)
        scalars[0] = jnp.broadcast_to(result[1:2, :], (8, 128))
        scalars[2] = jnp.broadcast_to(jnp.sqrt(result[0:1, :]), (8, 128))
    else:
        scalars[0] = loss_acc[...]
        scalars[2] = loss_acc[...]

    for copy in waits:
        copy.wait_send()
    for layer in range(sz.layers):
        for b in range(nb):
            kv_copy(layer, b).wait_send()
            mix_copy(layer, b).wait_send()


def dma(*shape):
    return pltpu.SemaphoreType.DMA(shape)


def train_kernel(sz, operands):
    nb, rows, half, width, cols = sz.batches, sz.rows, sz.half, sz.width, sz.cols
    layers = sz.layers
    scratch = []
    if sz.fused:
        out_shape = (
            jax.ShapeDtypeStruct((sz.mats, sz.shard, width), F32),
            jax.ShapeDtypeStruct((3, 8, 128), F32),
        )
        scratch += [
            pltpu.VMEM((sz.mats, sz.depth, 2, 2, 2, sz.shard, width), BF16),
            pltpu.VMEM((sz.mats, sz.depth, 2, 2, 2 * sz.shard, cols), F32),
        ]
    else:
        out_shape = (
            jax.ShapeDtypeStruct((sz.mats, width, cols), F32),
            jax.ShapeDtypeStruct((3, 8, 128), F32),
        )
    scratch += [
        pltpu.VMEM((nb, 2, half, 256), BF16),
        pltpu.VMEM((nb, 2, half, 128), F32),
        pltpu.VMEM((nb, rows, width), F32),
        pltpu.VMEM((layers + 1, nb, rows, width), F32),
        pltpu.VMEM((layers, nb, rows, width), F32),
        pltpu.VMEM((layers, nb, rows, width), F32),
        pltpu.VMEM((layers, nb, 2, rows, cols), BF16),
        pltpu.VMEM((layers, nb, rows, cols), BF16),
        pltpu.VMEM((layers, nb, 2, 2 * rows, cols), BF16),
        pltpu.VMEM((layers, nb, sz.near, rows, 2 * rows), BF16),
        pltpu.VMEM((rows, 2 * rows), F32),
        pltpu.VMEM((rows, rows), BF16),
        pltpu.VMEM((rows, rows), BF16),
        pltpu.VMEM((rows, rows), BF16),
        pltpu.VMEM((rows, rows), BF16),
        pltpu.VMEM((16, width), F32),
        pltpu.VMEM((16, width), F32),
        pltpu.VMEM((nb, rows, width), BF16),
        pltpu.VMEM((nb, rows, 128), BF16),
        pltpu.VMEM((nb, rows, width), BF16),
        pltpu.VMEM((nb, rows, width), BF16),
        pltpu.VMEM((nb, rows, width), BF16),
        pltpu.VMEM((nb, rows, width), BF16),
        pltpu.VMEM((nb, rows, width), BF16),
        pltpu.VMEM((nb, rows, width), BF16),
        pltpu.VMEM((nb, rows, 3 * cols), BF16),
        pltpu.VMEM((layers, nb, rows, 3 * cols), BF16),
        pltpu.VMEM((nb, 2, rows, cols), BF16),
        pltpu.VMEM((layers, nb, 2, rows, cols), BF16),
        pltpu.VMEM((8, 128), F32),
    ]
    one = pltpu.SemaphoreType.DMA
    scratch += [one, one, one, one] + [dma(layers, nb)] * 8
    if sz.fused:
        depth, groups = sz.depth, len(sz.groups)
        scratch += [
            pltpu.VMEM((sz.mats, depth, 2, 2 * sz.shard, cols), F32),
            pltpu.VMEM((sz.mats, depth, 2 * sz.shard, cols), F32),
            pltpu.VMEM((depth - 1, sz.mats, 2 * sz.shard, cols), F32),
            pltpu.VMEM((sz.mats, sz.shard, cols), F32),
            pltpu.VMEM((2, 4, 8, 128), F32),
            pltpu.VMEM((2, 3, 8, 128), F32),
            pltpu.VMEM((2, depth, 8, 128), F32),
        ]
        far = [dma(groups, depth - 1)] * 2
        two = [dma(groups, 2)] * 4
        scratch += far + two + [dma(groups)] * 2
        scratch += [dma(groups)] * 4 + far + [dma(groups)] * 2
        scratch += [dma(2, 3)] * 2 + [dma(2, depth - 1)] * 2
    return pl.pallas_call(
        functools.partial(step_kernel, sz),
        out_shape=out_shape,
        in_specs=[pl.BlockSpec(memory_space=pltpu.VMEM)] * len(operands),
        out_specs=(pl.BlockSpec(memory_space=pltpu.VMEM),) * 2,
        scratch_shapes=scratch,
        compiler_params=pltpu.CompilerParams(
            collective_id=0, has_side_effects=True, vmem_limit_bytes=60 * 1024 * 1024
        ),
    )(*operands)


def adam(weight, first, second, grad):
    first_new = BETA_ONE * first + (1.0 - BETA_ONE) * grad
    second_new = BETA_TWO * second + (1.0 - BETA_TWO) * grad * grad
    first_hat = first_new / (1.0 - BETA_ONE**STEP)
    second_hat = second_new / (1.0 - BETA_TWO**STEP)
    weight_new = weight - RATE * (first_hat / (jnp.sqrt(second_hat) + ADAM_EPS) + DECAY * weight)
    return (weight_new, first_new, second_new, weight_new.astype(BF16))


def adam_kernel(sz, share, scalars, *refs):
    masters = refs[:15]
    outs = refs[15:35]
    mat, inp, out, gain, bias = [masters[3 * k : 3 * k + 3] for k in range(5)]
    factor = jnp.minimum(1.0, CLIP / (scalars[2, 0:1, 0:1] + 1e-06))

    def put(k, values):
        for ref, value in zip(outs[4 * k : 4 * k + 4], values):
            ref[...] = value

    for index in range(sz.mats - 1):
        values = adam(mat[0][index], mat[1][index], mat[2][index], factor * share[1 + index])
        for ref, value in zip(outs[0:4], values):
            ref[index] = value
    last = share[0]
    put(1, adam(inp[0][...], inp[1][...], inp[2][...], factor * last[:, 0 : sz.c_in]))
    put(2, adam(out[0][...], out[1][...], out[2][...], factor * last[:, 384 : 384 + sz.c_out]))
    small = jnp.concatenate([last[:, 256:384], jnp.zeros((128 - sz.shard, 128), F32)], axis=0)
    small = jnp.transpose(small)[:, 0 : sz.shard]
    count = gain[0].shape[0]
    put(3, adam(gain[0][...], gain[1][...], gain[2][...], factor * small[0:count]))
    put(4, adam(bias[0][...], bias[1][...], bias[2][...], factor * small[8 : 8 + count]))


def update(sz, share, scalars, groups):
    operands = [share, scalars]
    out_shape = []
    for triple in groups:
        operands += list(triple)
        shape = triple[0].shape
        out_shape += [jax.ShapeDtypeStruct(shape, F32)] * 3 + [jax.ShapeDtypeStruct(shape, BF16)]
    return pl.pallas_call(
        functools.partial(adam_kernel, sz),
        out_shape=tuple(out_shape),
        in_specs=[pl.BlockSpec(memory_space=pltpu.VMEM)] * len(operands),
        out_specs=(pl.BlockSpec(memory_space=pltpu.VMEM),) * len(out_shape),
    )(*operands)


def per_device(
    grid_in, targets, area, row_count, g2m, m2g, senders, edge_count,
    mat_w, mat_m, mat_v, in_w, in_m, in_v, out_w, out_m, out_v,
    gain_w, gain_m, gain_v, bias_w, bias_m, bias_v,
):
    axes = ("node", "feat")
    sz = Sizes(
        lax.axis_size("node"),
        lax.axis_size("feat"),
        grid_in.shape[0],
        grid_in.shape[1],
        mat_w.shape[2],
        mat_w.shape[0] // 6,
        HEADS,
        senders.shape[1],
        grid_in.shape[2],
        targets.shape[2],
    )
    operands = [
        jnp.swapaxes(grid_in, 1, 2),
        jnp.swapaxes(targets, 1, 2),
        area.reshape(1, -1),
        row_count,
        g2m.T,
        m2g.T,
        senders.T,
        edge_count.reshape(1, -1),
    ]
    if sz.fused:
        operands += [mat_w, in_w.T, out_w, gain_w, bias_w]
        share, scalars = train_kernel(sz, operands)
        groups = (
            (mat_w, mat_m, mat_v),
            (in_w.T, in_m.T, in_v.T),
            (out_w, out_m, out_v),
            (gain_w, gain_m, gain_v),
            (bias_w, bias_m, bias_v),
        )
        outs = list(update(sz, share, scalars, groups))
        for index in range(4, 8):
            outs[index] = outs[index].T
        return tuple(outs) + (scalars[0, 0, 0], scalars[1, 0, 0], scalars[2, 0, 0])

    width, shard = sz.width, sz.shard

    def pad(value, size):
        return jnp.pad(value, ((0, 0), (0, size - value.shape[1])))

    def pack(square, inp, out, gain, bias):
        small = jnp.concatenate([pad(gain.T, 8), pad(bias.T, 120)], axis=1)
        first = jnp.concatenate([pad(inp.T, 256), small, pad(out, 128)], axis=1)
        return jnp.concatenate([first[None], square], axis=0)

    packed = pack(mat_w, in_w, out_w, gain_w, bias_w).astype(BF16)
    full = lax.all_gather(packed, axes, axis=1, tiled=True).reshape(sz.mats, 2, width // 2, width)
    live = (jnp.arange(sz.half)[None, :] < row_count).astype(F32)
    weight_total = lax.psum(jnp.sum(area[None, :] * live) * targets.shape[2], axes)
    operands += [full, weight_total.reshape(1, 1)]
    part, scalars = train_kernel(sz, operands)
    feat = lax.axis_index("feat")
    spread = lax.dynamic_update_slice(
        jnp.zeros((sz.mats, width, width), F32), part, (0, 0, feat * sz.cols)
    )
    share = lax.psum_scatter(spread, axes, scatter_dimension=1, tiled=True)
    square_sum, loss_sum = lax.psum((jnp.sum(share * share), scalars[0, 0, 0]), axes)
    grad_norm = jnp.sqrt(square_sum)
    share = jnp.minimum(1.0, CLIP / (grad_norm + 1e-06)) * share
    count = gain_w.shape[0]
    last = share[0]
    outs = adam(mat_w, mat_m, mat_v, share[1:])
    outs += adam(in_w, in_m, in_v, last[:, 0 : sz.c_in].T)
    outs += adam(out_w, out_m, out_v, last[:, 384 : 384 + sz.c_out])
    outs += adam(gain_w, gain_m, gain_v, last[:, 256 : 256 + count].T)
    outs += adam(bias_w, bias_m, bias_v, last[:, 264 : 264 + count].T)
    return outs + (loss_sum, weight_total, grad_norm)


def solution(mesh):
    both = ("node", "feat")
    rows_three = P(None, both, None)
    second = P(None, both)
    first = P(both, None)
    placed = (
        rows_three, rows_three, P(both), second,
        P("node", None), P("node", None), P("node", None), P("node"),
    )
    placed += (rows_three,) * 3 + (second,) * 3 + (first,) * 3 + (second,) * 6
    outs = (rows_three,) * 4 + (second,) * 4 + (first,) * 4 + (second,) * 8 + (P(), P(), P())
    return jax.shard_map(per_device, mesh=mesh, in_specs=placed, out_specs=outs, check_vma=False)
```

```python
import functools

import jax
import jax.numpy as jnp
from jax import lax
from jax.experimental import pallas as pl
from jax.experimental.pallas import tpu as pltpu
from jax.sharding import PartitionSpec as P

HEADS = 8
STEP = 5
NORM_EPS = 1e-05
CLIP = 0.05
RATE = 0.02
BETA_ONE = 0.5
BETA_TWO = 0.5
DECAY = 0.01
ADAM_EPS = 1e-08
DEAD = -1e30
MESH = pl.DeviceIdType.MESH
F32 = jnp.float32
BF16 = jnp.bfloat16


def nn(left, right):
    return jnp.dot(left, right, preferred_element_type=F32)


def nt(left, right):
    return lax.dot_general(left, right, (((1,), (1,)), ((), ())), preferred_element_type=F32)


def tn(left, right):
    return lax.dot_general(left, right, (((0,), (0,)), ((), ())), preferred_element_type=F32)


def norm_parts(state):
    centre = state - jnp.mean(state, axis=-1, keepdims=True)
    spread = jnp.mean(centre * centre, axis=-1, keepdims=True)
    scale = lax.rsqrt(spread + NORM_EPS)
    return centre * scale, scale


def norm_back(grad, hat, scale, gain):
    inner = grad * gain
    mean_inner = jnp.mean(inner, axis=-1, keepdims=True)
    mean_hat = jnp.mean(inner * hat, axis=-1, keepdims=True)
    return scale * (inner - mean_inner - hat * mean_hat)


def column_sum(value):
    return jnp.sum(value, axis=0, keepdims=True)


def sigmoid(value):
    return 1.0 / (1.0 + jnp.exp(-value))


def silu_slope(value):
    gate = sigmoid(value)
    return gate * (1.0 + value * (1.0 - gate))


class Sizes:
    def __init__(self, node, feat, batches, half, width, layers, heads, slots, c_in, c_out):
        self.node, self.feat = node, feat
        self.batches, self.half, self.width = batches, half, width
        self.rows = 2 * half
        self.layers, self.heads, self.slots = layers, heads, slots
        self.c_in, self.c_out = c_in, c_out
        self.shard = width // (node * feat)
        self.depth = node // 4
        self.mats = 6 * layers + 1
        self.cols = width // feat
        self.near = heads // feat
        self.fused = self.shard % 16 == 0 and node % 4 == 0
        self.groups = [(0, 1)] + [(first, 3) for first in range(1, self.mats, 3)]
        self.units = [(0, 1)]
        for layer in range(layers):
            self.units += [(1 + 6 * layer, 4), (5 + 6 * layer, 2)]


def step_kernel(sz, *refs):
    refs = list(refs)

    def take(count):
        out = refs[:count]
        del refs[:count]
        return out

    grid_ref, target_ref, area_ref, count_ref, g2m_ref, m2g_ref, send_ref, edge_ref = take(8)
    if sz.fused:
        mat_ref, in_ref, out_ref, gain_ref, bias_ref = take(5)
        share, scalars = take(2)
        full, total = take(2)
    else:
        full, weight_ref = take(2)
        total, scalars = take(2)
    (
        rows_own,
        rows_in,
        rows_prev,
        indices,
        start,
        start_prev,
        state,
        middle,
        pre_mlp,
        mixed,
        query,
        pair,
        prob,
        edge_bias,
        g_row,
        g_col,
        gp_row,
        gp_col,
        m_row,
        m_col,
        affine,
        affine_grad,
        final,
        grad_pred,
        low,
        pre_low,
        mid_low,
        n_own,
        n_prev,
        n_two,
        hidden,
        d_own,
        d_far,
        dn_out,
        dn_in,
        loss_acc,
    ) = take(36)
    (s_rows, r_rows, s_idx, r_idx, s_prev, r_prev) = take(6)
    (s_n, r_n, s_nf, r_nf, s_mix, r_mix, s_dn, r_dn, s_df, r_df, s_far, r_far) = take(12)
    (far_free,) = take(1)
    if sz.fused:
        (code_one, got_one, code_two, got_two, code_z, got_z, got_c) = take(7)
        (size_out, size_in, size_z, size_z_in, tile, tile_far, tile_all) = take(7)
        (gz_s, gz_r, g2_s, g2_r, g3_s, g3_r, g4_s, g4_r) = take(8)
        (rr_s, rr_r, rz_s, rz_r, rc_s, rc_r) = take(6)
        (t_s, t_r, tz_s, tz_r) = take(4)

    nb, rows, half, width, cols = sz.batches, sz.rows, sz.half, sz.width, sz.cols
    node = lax.axis_index("node")
    y = lax.axis_index("feat")
    waits = []
    if sz.fused:
        depth = sz.depth
        c = lax.rem(node, 2)
        x = lax.rem(node // 2, 2)
        z = node // 4
        j = c

        def device_of(zz, xx, cc, yy):
            return (zz * 4 + xx * 2 + cc, yy)

        def holder(block):
            return device_of(block // 4, lax.rem(block // 2, 2), c, lax.rem(block, 2))

        block = z * 4 + x * 2 + y
        after = holder(lax.rem(block + 1, sz.node))
        before = holder(lax.rem(block + sz.node - 1, sz.node))
        partner = device_of(z, x, 1 - c, y)
        x_dev = device_of(z, 1 - x, c, y)
        y_dev = device_of(z, x, c, 1 - y)
        z_devs = [device_of(lax.rem(z + step, depth), x, c, y) for step in range(1, depth)]

        def chip_at(dz, dx, dy):
            return device_of(lax.rem(z + dz, depth), lax.rem(x + dx, 2), c, lax.rem(y + dy, 2))

        offsets = [(k // 4, (k // 2) % 2, k % 2) for k in range(1, 4 * depth)]
        greet = [after, before, partner] + [chip_at(*offset) for offset in offsets]
    else:
        j = y
        after = (lax.rem(node + 1, sz.node), j)
        before = (lax.rem(node + sz.node - 1, sz.node), j)
        partner = (node, 1 - j)
        greet = [after, before, partner]
    other = 1 - j
    mine = pl.ds(pl.multiple_of(j * cols, cols), cols)
    theirs = pl.ds(pl.multiple_of(other * cols, cols), cols)

    def remote(src, dst, s_sem, r_sem, device):
        return pltpu.make_async_remote_copy(
            src_ref=src, dst_ref=dst, send_sem=s_sem, recv_sem=r_sem, device_id=device, device_id_type=MESH
        )

    def push(make):
        make().start()
        waits.append(make)

    barrier = pltpu.get_barrier_semaphore()
    for device in greet:
        pl.semaphore_signal(barrier, inc=1, device_id=device, device_id_type=MESH)
    pl.semaphore_wait(barrier, len(greet))

    lanes_c = lax.broadcasted_iota(jnp.int32, (1, cols), 1) // (width // sz.heads)
    mask_low = [(lanes_c == head).astype(F32).astype(BF16) for head in range(sz.near)]
    mask_full = [(lanes_c == head).astype(F32) for head in range(sz.near)]

    def w_full(index):
        return full[index].reshape(width, width)

    def w_cols(index, which):
        if sz.fused:
            return full[index, :, :, :, :, :, which].reshape(width, cols)
        return full[index, :, :, which].reshape(width, cols)

    def w_rows(index, which):
        if sz.fused:
            count = sz.depth // 2
            return full[index, pl.ds(which * count, count)].reshape(width // 2, width)
        return full[index, which]

    def w_block(index, rows_half, which):
        if sz.fused:
            count = sz.depth // 2
            return full[index, pl.ds(rows_half * count, count), :, :, :, :, which].reshape(width // 2, cols)
        return full[index, rows_half, :, which]

    def put_total(index, value):
        total[index] = value.reshape(total.shape[1:])

    cell = lax.broadcasted_iota(jnp.int32, (1, half), 1)
    for b in range(nb):
        block_in = jnp.concatenate([grid_ref[b].astype(F32), jnp.zeros((256 - sz.c_in, half), F32)], axis=0)
        rows_own[b, :, 0:256] = jnp.transpose(block_in).astype(BF16)
        weight = jnp.where(cell < count_ref[b : b + 1, 0:1], area_ref[...], 0.0)
        first = weight.astype(BF16).astype(F32)
        second = (weight - first).astype(BF16).astype(F32)
        third = weight - first - second
        block_in = jnp.concatenate(
            [target_ref[b].astype(F32), jnp.zeros((125 - sz.c_out, half), F32), first, second, third], axis=0
        )
        rows_own[b, :, 256:384] = jnp.transpose(block_in).astype(BF16)
    slot = c if sz.fused else 0
    k_g = g2m_ref.shape[0]
    k_m = m2g_ref.shape[0]
    receiver = lax.broadcasted_iota(jnp.int32, (1, rows), 1)
    indices[slot, 0:k_g] = g2m_ref[...]
    indices[slot, 8 : 8 + k_m] = m2g_ref[...]
    indices[slot, 15:16] = jnp.where(receiver < rows // 2, edge_ref[0:1, 0:1], edge_ref[0:1, 1:2])
    indices[slot, 16 : 16 + sz.slots] = send_ref[...]
    here = rows_in.at[:, y]
    there = rows_in.at[:, 1 - y]
    if sz.fused:
        push(lambda: remote(indices.at[c], indices.at[c], s_idx.at[0], r_idx.at[0], partner))
        to_partner = remote(rows_own, here, s_rows.at[0], r_rows.at[0], partner)
        to_chip = remote(rows_own, here, s_rows.at[1], r_rows.at[1], y_dev)
        forward = remote(there, there, s_rows.at[2], r_rows.at[1], partner)

        @pl.when(c == y)
        def _():
            to_partner.start()
            rows_in[:, y] = rows_own[...]

        @pl.when(c != y)
        def _():
            to_chip.start()

    else:
        push(lambda: remote(rows_own, here, s_rows.at[0], r_rows.at[0], partner))
        rows_in[:, y] = rows_own[...]

    if sz.fused:
        n_groups = len(sz.groups)
        packed = jnp.concatenate(
            [
                in_ref[...],
                jnp.zeros((sz.shard, 256 - sz.c_in), F32),
                jnp.zeros((sz.shard, 128), F32),
                out_ref[...],
                jnp.zeros((sz.shard, 128 - sz.c_out), F32),
            ],
            axis=1,
        )
        small = jnp.concatenate(
            [
                gain_ref[...],
                jnp.zeros((3, sz.shard), F32),
                bias_ref[...],
                jnp.zeros((3, sz.shard), F32),
            ],
            axis=0,
        )
        small = jnp.concatenate([small, jnp.zeros((16, 128 - sz.shard), F32)], axis=1)
        small = jnp.concatenate([small, jnp.zeros((112, 128), F32)], axis=0)
        small = jnp.transpose(small)[0 : sz.shard, :]
        full[0, z, x, c, y] = jnp.concatenate([packed[:, 0:256], small, packed[:, 384:512]], axis=1).astype(BF16)
        for index in range(sz.mats - 1):
            full[1 + index, z, x, c, y] = mat_ref[index].astype(BF16)

        def gather_one(g):
            first, count = sz.groups[g]
            for step in range(1, depth):

                def make(g=g, first=first, count=count, step=step):
                    own = full.at[pl.ds(first, count), z, x, c, y]
                    return remote(own, own, gz_s.at[g, step - 1], gz_r.at[g, step - 1], z_devs[step - 1])

                push(make)

        gather_one(0)
        gather_one(1)
        gather_one(2)

    if sz.fused:
        weight_sum = jnp.zeros((1, 1), F32)
        for b in range(nb):
            weight = jnp.where(cell < count_ref[b : b + 1, 0:1], area_ref[...], 0.0)
            weight_sum = weight_sum + jnp.sum(weight, axis=1, keepdims=True)
        tile[0, 0] = jnp.broadcast_to(weight_sum * float(sz.c_out), (8, 128))

        def tile_core(slot):
            return remote(tile.at[slot, 0], tile_far.at[slot], t_s.at[slot], t_r.at[slot], partner)

        def tile_chip(slot, k, place):
            return remote(
                tile.at[slot, 1], tile_all.at[slot, place], tz_s.at[slot, k], tz_r.at[slot, k], chip_at(*offsets[k])
            )

        def tile_start(slot):
            tile_core(slot).start()
            tile_core(slot).wait()
            tile[slot, 1] = tile[slot, 0] + tile_far[slot]
            spot = z * 4 + x * 2 + y
            tile_all[slot, spot] = tile[slot, 1]
            for k in range(len(offsets)):
                tile_chip(slot, k, spot).start()

        def tile_end(slot):
            for k, (dz, dx, dy) in enumerate(offsets):
                source = (
                    lax.rem(z + depth - dz, depth) * 4 + lax.rem(x + 2 - dx, 2) * 2 + lax.rem(y + 2 - dy, 2)
                )
                tile_chip(slot, k, source).wait()
            result = tile_all[slot, 0]
            for index in range(1, 4 * depth):
                result = result + tile_all[slot, index]
            return result

        tile_start(0)

    if sz.fused:
        remote(indices.at[1 - c], indices.at[1 - c], s_idx.at[0], r_idx.at[0], partner).wait_recv()
        slot = y
    push(lambda: remote(indices.at[slot], indices.at[2], s_idx.at[1], r_idx.at[1], after))

    def counts(place, first, slots, origin, live=None):
        wide = lax.broadcasted_iota(jnp.int32, (rows, rows), 0) + origin
        acc = jnp.zeros((rows, rows), F32)
        for k in range(slots):
            hit = wide == indices[place, first + k : first + k + 1, :]
            if live is not None:
                hit = jnp.logical_and(hit, live > k)
            acc = acc + jnp.where(hit, 1.0, 0.0)
        return acc

    live = indices[slot, 15:16, :]
    for part in range(2):
        acc = jnp.transpose(counts(slot, 16, sz.slots, part * rows, live))
        edge_bias[:, part * rows : (part + 1) * rows] = jnp.where(acc > 0.5, jnp.log(jnp.maximum(acc, 1.0)), DEAD)
    table = counts(slot, 0, k_g, 0)
    g_col[...] = table.astype(BF16)
    g_row[...] = jnp.transpose(table).astype(BF16)
    table = counts(slot, 8, k_m, 0)
    m_col[...] = table.astype(BF16)
    m_row[...] = jnp.transpose(table).astype(BF16)
    affine_grad[...] = jnp.zeros_like(affine_grad)
    loss_acc[...] = jnp.zeros_like(loss_acc)

    if sz.fused:

        @pl.when(c == y)
        def _():
            remote(there, there, s_rows.at[1], r_rows.at[1], y_dev).wait_recv()
            forward.start()
            to_partner.wait_send()
            forward.wait_send()

        @pl.when(c != y)
        def _():
            to_chip.wait_send()
            remote(here, here, s_rows.at[0], r_rows.at[0], partner).wait_recv()
            remote(there, there, s_rows.at[2], r_rows.at[1], partner).wait_recv()

    else:
        remote(there, there, s_rows.at[0], r_rows.at[0], partner).wait_recv()

    push(lambda: remote(rows_in.at[:, j, :, 0:256], rows_prev.at[:, j], s_prev.at[0], r_prev.at[0], after))

    if sz.fused:
        side_a = pl.ds(0, width // 2)
        side_b = pl.ds(width // 2, width // 2)

        def gather_part(g, stage, which):
            span = pl.ds(*sz.groups[g])
            if stage == 2:
                return full.at[span, :, x, c, y, :, which]
            if which is side_a:
                return full.at[span, :, :, c, y, :, which]
            return full.at[span, :, x, c, :, :, which]

        def gather_push(g, stage, side, sems, device):
            which = (side_a, side_b)[side]

            def make():
                part = gather_part(g, stage, which)
                return remote(part, part, sems[0].at[g, side], sems[1].at[g, side], device)

            push(make)

        def arrived(part, s_sem, r_sem, device):
            remote(part, part, s_sem, r_sem, device).wait_recv()

        def gather_two(g):
            span = pl.ds(*sz.groups[g])
            for step in range(1, depth):
                there = full.at[span, lax.rem(z + depth - step, depth), x, c, y]
                arrived(there, gz_s.at[g, step - 1], gz_r.at[g, step - 1], z_devs[step - 1])
            gather_push(g, 2, 0, (g2_s, g2_r), x_dev)
            gather_push(g, 2, 1, (g2_s, g2_r), y_dev)

        def gather_three(g):
            span = pl.ds(*sz.groups[g])
            arrived(full.at[span, :, 1 - x, c, y, :, side_a], g2_s.at[g, 0], g2_r.at[g, 0], x_dev)
            gather_push(g, 3, 0, (g3_s, g3_r), y_dev)
            arrived(full.at[span, :, x, c, 1 - y, :, side_b], g2_s.at[g, 1], g2_r.at[g, 1], y_dev)
            gather_push(g, 3, 1, (g3_s, g3_r), x_dev)

        def gather_four(g):
            span = pl.ds(*sz.groups[g])
            arrived(full.at[span, :, :, c, 1 - y, :, side_a], g3_s.at[g, 0], g3_r.at[g, 0], y_dev)
            arrived(full.at[span, :, 1 - x, c, :, :, side_b], g3_s.at[g, 1], g3_r.at[g, 1], x_dev)

            def make():
                part = full.at[span, :, :, c]
                return remote(part, part, g4_s.at[g], g4_r.at[g], partner)

            push(make)

        def gather_done(g):
            span = pl.ds(*sz.groups[g])
            arrived(full.at[span, :, :, 1 - c], g4_s.at[g], g4_r.at[g], partner)

    def gathered(stage, g):
        if sz.fused and g < len(sz.groups):
            (None, gather_one, gather_two, gather_three, gather_four, gather_done)[stage](g)

    gathered(2, 0)
    gathered(1, 3)
    gathered(2, 1)
    gathered(1, 4)
    gathered(3, 0)
    for g in range(5, len(sz.groups)):
        gathered(1, g)

    in_cols = pl.ds(0, 256)
    small_cols = pl.ds(256, 128)
    out_cols = pl.ds(384, 128)

    def aux(which, size):
        if sz.fused:
            return full[0, :, :, :, :, :, which].reshape(width, size)
        return full[0, :, :, which].reshape(width, size)

    remote(indices.at[slot], indices.at[2], s_idx.at[1], r_idx.at[1], after).wait_recv()
    table = counts(2, 0, k_g, 0)
    gp_col[...] = table.astype(BF16)
    gp_row[...] = jnp.transpose(table).astype(BF16)
    remote(rows_prev.at[:, j], rows_prev.at[:, j], s_prev.at[0], r_prev.at[0], after).wait_recv()
    push(lambda: remote(rows_prev.at[:, j], rows_prev.at[:, j], s_prev.at[1], r_prev.at[1], partner))
    gathered(3, 1)
    gathered(2, 2)
    gathered(4, 0)
    gathered(4, 1)
    gathered(5, 0)
    remote(rows_prev.at[:, other], rows_prev.at[:, other], s_prev.at[1], r_prev.at[1], partner).wait_recv()

    affine[...] = jnp.transpose(aux(small_cols, 128).astype(F32))[0:16, :]

    def gain_row(index):
        return affine[pl.ds(index, 1), :]

    def bias_row(index):
        return affine[pl.ds(8 + index, 1), :]

    def add_affine(index, value):
        affine_grad[pl.ds(index, 1), :] = affine_grad[pl.ds(index, 1), :] + value

    def staggered(*bodies, hooks=()):
        def wrapped(t, carry):
            for step, hook in enumerate(hooks):
                if hook is not None:
                    pl.when(t == step)(hook)
            for late in reversed(range(len(bodies))):

                @pl.when(jnp.logical_and(t >= late, t < nb + late))
                def _(late=late):
                    bodies[late](t - late)

            return carry

        lax.fori_loop(0, nb + len(bodies) - 1, wrapped, 0)

    def each(body, hooks=()):
        def wrapped(b, carry):
            for step, hook in enumerate(hooks):
                if hook is not None:
                    pl.when(b == step)(hook)
            body(b)
            return carry

        lax.fori_loop(0, nb, wrapped, 0)

    def pre_encode(ref, b):
        return nt(ref[b, :, :, 0:256].reshape(rows, 256), aux(in_cols, 256)) + bias_row(0)

    def encode(b):
        gain = gain_row(0)
        for ref, table, keep, normed in (
            (rows_in, g_row, start, n_own),
            (rows_prev, gp_row, start_prev, n_prev),
        ):
            pre = pre_encode(ref, b)
            enc = (pre * sigmoid(pre)).astype(BF16)
            first = (nn(table[...], enc) * (1.0 / k_g)).astype(BF16)
            keep[b] = first
            hat, _ = norm_parts(first.astype(F32))
            normed[0, b] = (hat * gain).astype(BF16)

    def n_copy(layer, b):
        return remote(
            n_own.at[layer, b, :, mine], n_prev.at[layer, b, :, mine], s_n.at[layer, b], r_n.at[layer, b], after
        )

    def n_forward(layer, b, which):
        there = n_prev.at[layer, b, :, which]
        return remote(there, there, s_nf.at[layer, b], r_nf.at[layer, b], partner)

    def mix_copy(layer, b):
        return remote(
            mixed.at[layer, b, j], mixed.at[layer, b, j], s_mix.at[layer, b], r_mix.at[layer, b], partner
        )

    def mix_wait(layer, b):
        there = mixed.at[layer, b, other]
        remote(there, there, s_mix.at[layer, b], r_mix.at[layer, b], partner).wait_recv()

    scale = float(width // sz.heads) ** -0.5

    def spot(layer, b):
        return layer * nb + (b if layer < sz.layers - 1 else 0)

    def entry(layer, b):
        if layer == 0:
            return start[b].astype(F32)
        return state[layer - 1, b]

    def project(layer, b):
        base = 1 + 6 * layer
        if layer > 0:
            hat, _ = norm_parts(state[layer - 1, b])
            n_own[layer, b] = (hat * gain_row(2 * layer)).astype(BF16)
            n_copy(layer, b).start()
        normed = n_own[layer, b]
        query[layer, b] = nn(normed, w_cols(base, mine)).astype(BF16)
        pair[layer, b, 0, 0:rows] = nn(normed, w_cols(base + 1, mine)).astype(BF16)
        pair[layer, b, 1, 0:rows] = nn(normed, w_cols(base + 2, mine)).astype(BF16)

    def take_prev(layer, b):
        if layer > 0:
            n_copy(layer, b).wait_recv()
            n_forward(layer, b, mine).start()

    def attend(layer, b):
        base = 1 + 6 * layer
        if layer > 0:
            n_forward(layer, b, theirs).wait_recv()
        normed = n_prev[layer, b]
        pair[layer, b, 0, rows : 2 * rows] = nn(normed, w_cols(base + 1, mine)).astype(BF16)
        pair[layer, b, 1, rows : 2 * rows] = nn(normed, w_cols(base + 2, mine)).astype(BF16)
        keys, values, queries = pair[layer, b, 0], pair[layer, b, 1], query[layer, b]
        out = jnp.zeros((rows, cols), F32)
        for head in range(sz.near):
            score = nt(queries * mask_low[head], keys) * scale + edge_bias[...]
            expo = jnp.exp(score - jnp.max(score, axis=-1, keepdims=True))
            weight = (expo * (1.0 / jnp.sum(expo, axis=-1, keepdims=True))).astype(BF16)
            prob[layer, b, head] = weight
            out = out + nn(weight, values) * mask_full[head]
        mixed[layer, b, j] = out.astype(BF16)
        mix_copy(layer, b).start()

    def mlp(layer, b):
        base = 1 + 6 * layer
        mix_wait(layer, b)
        mid = (
            entry(layer, b)
            + nn(mixed[layer, b, 0], w_rows(base + 3, 0))
            + nn(mixed[layer, b, 1], w_rows(base + 3, 1))
        )
        middle[spot(layer, b)] = mid
        hat, _ = norm_parts(mid)
        normed = (hat * gain_row(2 * layer + 1)).astype(BF16)
        pre = nn(normed, w_full(base + 4)) + bias_row(1 + 2 * layer)
        pre_mlp[spot(layer, b)] = pre
        act = (pre * sigmoid(pre)).astype(BF16)
        state[layer, b] = mid + nn(act, w_full(base + 5)) + bias_row(2 + 2 * layer)

    last = sz.layers - 1
    lane_out = lax.broadcasted_iota(jnp.int32, (1, 128), 1)
    row_index = lax.broadcasted_iota(jnp.int32, (rows, 1), 0)
    own_row = jnp.logical_and(row_index >= j * half, row_index < (j + 1) * half).astype(F32)
    real_lane = (lane_out < sz.c_out).astype(F32)

    def decode(b):
        gain = gain_row(2 * sz.layers)
        dec = (nn(m_row[...], state[last, b].astype(BF16)) * (1.0 / k_m)).astype(BF16).astype(F32)
        hat, inv = norm_parts(dec)
        normed = (hat * gain).astype(BF16)
        final[b] = normed
        weights = aux(out_cols, 128)
        goal = rows_in[b, :, :, 256:384].reshape(rows, 128).astype(F32)
        error = (nn(normed, weights) - goal) * real_lane
        weight = goal[:, 125:126] + goal[:, 126:127] + goal[:, 127:128]
        loss_acc[...] = loss_acc[...] + jnp.sum(
            jnp.sum((weight * own_row) * error * error, axis=1, keepdims=True), axis=0, keepdims=True
        )
        pred_low = (2.0 * weight * error / scalars[1, 0:1, 0:1]).astype(BF16)
        grad_pred[b] = pred_low
        back = nt(pred_low, weights)
        add_affine(2 * sz.layers, column_sum(back * hat))
        dec_low = norm_back(back, hat, inv, gain).astype(BF16)
        state[last, b] = (nn(m_col[...], dec_low) * (1.0 / k_m)).astype(BF16).astype(F32)

    if sz.fused:
        lane_a = pl.ds(0, cols // 2)
        lane_b = pl.ds(cols // 2, cols // 2)
        lanes = (lane_a, lane_b)
        top = 32767.0

        def encoded(value, code_ref, scale_ref):
            size = jnp.max(jnp.abs(value), axis=tuple(range(value.ndim - 1)), keepdims=True)
            size = size.reshape(1, size.shape[-1])
            inverse = jnp.where(size > 1e-30, top / jnp.maximum(size, 1e-30), 0.0)
            code_ref[...] = jnp.round(value * inverse).astype(jnp.int32).astype(jnp.int16)
            scale_ref[...] = jnp.broadcast_to(size * (1.0 / top), scale_ref.shape)

        def decoded(code, scale_row):
            return code.astype(jnp.int32).astype(F32) * scale_row

        def over(unit, body):
            first, count = sz.units[unit]

            def wrapped(m, carry):
                body(m)
                return carry

            lax.fori_loop(first, first + count, wrapped, 0)

        def send_codes(unit, stage, side, device):
            span = pl.ds(*sz.units[unit])
            codes_out, codes_in = ((code_one, got_one), (code_two, got_two))[stage]

            def make_codes():
                k = 2 * stage
                return remote(
                    codes_out.at[side, span], codes_in.at[side, span], rr_s.at[unit, k, side], rr_r.at[unit, k, side], device
                )

            def make_scales():
                k = 2 * stage + 1
                return remote(
                    size_out.at[stage, side, span],
                    size_in.at[stage, side, span],
                    rr_s.at[unit, k, side],
                    rr_r.at[unit, k, side],
                    device,
                )

            return make_codes, make_scales

        def reduce_one(unit):
            def body(m):
                encoded(total[m, :, 1 - x, :, :, :, lane_a], code_one.at[0, m], size_out.at[0, 0, m])
                encoded(total[m, :, :, :, 1 - y, :, lane_b], code_one.at[1, m], size_out.at[0, 1, m])

            over(unit, body)
            for side, device in ((0, x_dev), (1, y_dev)):
                for make in send_codes(unit, 0, side, device):
                    push(make)

        def reduce_two(unit):
            for side, device in ((0, x_dev), (1, y_dev)):
                for make in send_codes(unit, 0, side, device):
                    make().wait_recv()

            def body(m):
                row_a = size_in[0, 0, m, 0:1, :]
                row_b = size_in[0, 1, m, 0:1, :]
                total[m, :, x, :, :, :, lane_a] = total[m, :, x, :, :, :, lane_a] + decoded(got_one[0, m], row_a)
                total[m, :, :, :, y, :, lane_b] = total[m, :, :, :, y, :, lane_b] + decoded(got_one[1, m], row_b)
                encoded(total[m, :, x, :, 1 - y, :, lane_a], code_two.at[0, m], size_out.at[1, 0, m])
                encoded(total[m, :, 1 - x, :, y, :, lane_b], code_two.at[1, m], size_out.at[1, 1, m])

            over(unit, body)
            for side, device in ((0, y_dev), (1, x_dev)):
                for make in send_codes(unit, 1, side, device):
                    push(make)

        def send_z(unit, step):
            span = pl.ds(*sz.units[unit])

            def make_codes():
                return remote(
                    code_z.at[span, lax.rem(z + step, depth)],
                    got_z.at[step - 1, span],
                    rz_s.at[unit, 0, step - 1],
                    rz_r.at[unit, 0, step - 1],
                    z_devs[step - 1],
                )

            def make_scales():
                return remote(
                    size_z.at[span],
                    size_z_in.at[step - 1, span],
                    rz_s.at[unit, 1, step - 1],
                    rz_r.at[unit, 1, step - 1],
                    z_devs[step - 1],
                )

            return make_codes, make_scales

        def reduce_three(unit):
            for side, device in ((0, y_dev), (1, x_dev)):
                for make in send_codes(unit, 1, side, device):
                    make().wait_recv()

            def body(m):
                for side in range(2):
                    row = size_in[1, side, m, 0:1, :]
                    total[m, :, x, :, y, :, lanes[side]] = total[m, :, x, :, y, :, lanes[side]] + decoded(
                        got_two[side, m], row
                    )
                encoded(total[m, :, x, :, y], code_z.at[m], size_z.at[m])

            over(unit, body)
            for step in range(1, depth):
                for make in send_z(unit, step):
                    push(make)

        def core_copy(unit):
            span = pl.ds(*sz.units[unit])
            return remote(total.at[span, z, x, 1 - c, y], got_c.at[span], rc_s.at[unit], rc_r.at[unit], partner)

        def reduce_four(unit):
            for step in range(1, depth):
                for make in send_z(unit, step):
                    make().wait_recv()

            def body(m):
                acc = total[m, z, x, :, y]
                for step in range(1, depth):
                    acc = acc + decoded(got_z[step - 1, m], size_z_in[step - 1, m, 0:1, :])
                total[m, z, x, :, y] = acc

            over(unit, body)
            push(lambda: core_copy(unit))

        def reduce_done(unit):
            core_copy(unit).wait_recv()

            def body(m):
                share[m, :, mine] = total[m, z, x, c, y]
                share[m, :, theirs] = got_c[m]

            over(unit, body)

        stages = (None, reduce_one, reduce_two, reduce_three, reduce_four, reduce_done)

    def summed(stage, unit):
        if sz.fused:
            stages[stage](unit)

    def far_copy(layer, b):
        return remote(d_own.at[b], d_far.at[b], s_far.at[layer, b], r_far.at[layer, b], partner)

    def dn_copy(layer, b):
        return remote(
            dn_out.at[layer - 1, b],
            dn_in.at[layer - 1, b, :, mine],
            s_dn.at[layer, b],
            r_dn.at[layer, b],
            before,
        )

    def dn_forward(layer, b, which):
        there = dn_in.at[layer - 1, b, :, which]
        return remote(there, there, s_df.at[layer, b], r_df.at[layer, b], partner)

    def mlp_back(layer, b):
        base = 1 + 6 * layer
        grad = state[last, b]
        grad_low = grad.astype(BF16)
        low[b] = grad_low
        add_affine(8 + 2 + 2 * layer, column_sum(grad))
        pre = pre_mlp[spot(layer, b)]
        gate = sigmoid(pre)
        hidden[b] = (pre * gate).astype(BF16)
        back = (nt(grad_low, w_full(base + 5)) * (gate * (1.0 + pre * (1.0 - gate)))).astype(BF16)
        pre_low[b] = back
        add_affine(8 + 1 + 2 * layer, column_sum(back.astype(F32)))
        back = nt(back, w_full(base + 4))
        gain = gain_row(2 * layer + 1)
        hat, inv = norm_parts(middle[spot(layer, b)])
        n_two[b] = (hat * gain).astype(BF16)
        add_affine(2 * layer + 1, column_sum(back * hat))
        grad = grad + norm_back(back, hat, inv, gain)
        state[last, b] = grad
        mid_low[b] = grad.astype(BF16)

    def attend_back(layer, b):
        base = 1 + 6 * layer
        grad_out = nt(mid_low[b], w_rows(base + 3, j)).astype(BF16)
        keys, values, queries = pair[layer, b, 0], pair[layer, b, 1], query[layer, b]
        d_query = jnp.zeros((rows, cols), F32)
        d_keys = jnp.zeros((2 * rows, cols), F32)
        d_values = jnp.zeros((2 * rows, cols), F32)
        for head in range(sz.near):
            weight_low = prob[layer, b, head]
            out_head = grad_out * mask_low[head]
            weight = weight_low.astype(F32)
            part = weight * nt(out_head, values)
            score = (part - weight * jnp.sum(part, axis=-1, keepdims=True)).astype(BF16)
            d_query = d_query + nn(score, keys) * mask_full[head]
            d_keys = d_keys + tn(score, queries * mask_low[head])
            d_values = d_values + tn(weight_low, out_head)
        d_keys = (d_keys * scale).astype(BF16)
        d_values = d_values.astype(BF16)
        d_own[b, :, 0:cols] = (d_query * scale).astype(BF16)
        d_own[b, :, cols : 2 * cols] = d_keys[0:rows]
        d_own[b, :, 2 * cols : 3 * cols] = d_values[0:rows]
        d_own[b, :, 3 * cols : 4 * cols] = d_keys[rows:]
        d_own[b, :, 4 * cols : 5 * cols] = d_values[rows:]
        if layer < last:
            pl.semaphore_wait(far_free, 1)
        far_copy(layer, b).start()

    def send_prev(layer, b):
        base = 1 + 6 * layer
        far_copy(layer, b).wait()
        back = jnp.zeros((rows, cols), F32)
        for which in (1, 2):
            part = pl.ds((which + 2) * cols, cols)
            back = back + nt(d_own[b, :, part], w_block(base + which, j, mine))
            back = back + nt(d_far[b, :, part], w_block(base + which, j, theirs))
        dn_out[layer - 1, b] = back.astype(BF16)
        dn_copy(layer, b).start()

    def take_next(layer, b):
        dn_copy(layer, b).wait_recv()
        dn_forward(layer, b, mine).start()

    def join(layer, b):
        base = 1 + 6 * layer
        if layer > 0:
            dn_forward(layer, b, theirs).wait_recv()
            back = dn_in[layer - 1, b].astype(F32)
        else:
            far_copy(layer, b).wait()
            back = jnp.zeros((rows, width), F32)
        for which in range(3):
            part = pl.ds(which * cols, cols)
            back = back + nt(d_own[b, :, part], w_cols(base + which, mine))
            back = back + nt(d_far[b, :, part], w_cols(base + which, theirs))
        if layer > 0:
            pl.semaphore_signal(far_free, inc=1, device_id=partner, device_id_type=MESH)
        gain = gain_row(2 * layer)
        hat, inv = norm_parts(entry(layer, b))
        add_affine(2 * layer, column_sum(back * hat))
        state[last, b] = state[last, b] + norm_back(back, hat, inv, gain)

    many = nb * rows

    def outer_mlp(layer):
        base = 1 + 6 * layer
        put_total(base + 5, tn(hidden[...].reshape(many, width), low[:, :, mine].reshape(many, cols)))
        put_total(base + 4, tn(n_two[...].reshape(many, width), pre_low[:, :, mine].reshape(many, cols)))

    def outer_mixed(layer):
        base = 1 + 6 * layer
        grad_mid = mid_low[:, :, mine].reshape(many, cols)
        put_total(
            base + 3,
            jnp.concatenate(
                [
                    tn(mixed[layer, :, 0].reshape(many, cols), grad_mid),
                    tn(mixed[layer, :, 1].reshape(many, cols), grad_mid),
                ],
                axis=0,
            ),
        )

    def outer_pair(layer):
        base = 1 + 6 * layer
        near = tn(n_own[layer].reshape(many, width), d_own[:, :, 0 : 3 * cols].reshape(many, 3 * cols))
        put_total(base, near[:, 0:cols])
        away = tn(n_prev[layer].reshape(many, width), d_own[:, :, 3 * cols : 5 * cols].reshape(many, 2 * cols))
        put_total(base + 1, near[:, cols : 2 * cols] + away[:, 0:cols])
        put_total(base + 2, near[:, 2 * cols : 3 * cols] + away[:, cols : 2 * cols])

    def encode_back(b):
        back = nn(g_col[...], state[last, b].astype(BF16)) * (1.0 / k_g)
        back = (back.astype(BF16).astype(F32) * silu_slope(pre_encode(rows_in, b))).astype(BF16)
        low[b] = back
        add_affine(8, column_sum(back.astype(F32)))
        back = jnp.zeros((rows, width), F32)
        for which in (1, 2):
            part = pl.ds((which + 2) * cols, cols)
            back = back + nt(d_own[b, :, part], w_cols(1 + which, mine))
            back = back + nt(d_far[b, :, part], w_cols(1 + which, theirs))
        gain = gain_row(0)
        hat, inv = norm_parts(start_prev[b].astype(F32))
        add_affine(0, column_sum(back * hat))
        back = nn(gp_col[...], norm_back(back, hat, inv, gain).astype(BF16)) * (1.0 / k_g)
        back = (back.astype(BF16).astype(F32) * silu_slope(pre_encode(rows_prev, b))).astype(BF16)
        mid_low[b] = back
        add_affine(8, column_sum(back.astype(F32)))

    each(encode)
    gathered(3, 2)
    gathered(2, 3)
    gathered(5, 1)

    def first_project(b):
        project(0, b)

    each(first_project)
    gathered(4, 2)
    gathered(3, 3)
    gathered(2, 4)
    for layer in range(last):

        def attend_this(b, layer=layer):
            take_prev(layer, b)
            attend(layer, b)

        def mlp_this(b, layer=layer):
            mlp(layer, b)

        def project_next(b, layer=layer):
            project(layer + 1, b)

        def ready(g=2 * layer):
            gathered(5, g + 2)
            gathered(4, g + 3)
            gathered(3, g + 4)

        def ready_next(g=2 * layer):
            gathered(5, g + 3)
            gathered(4, g + 4)

        staggered(attend_this, mlp_this, project_next, hooks=(None, ready, ready_next))
        gathered(2, 2 * layer + 5)
        gathered(3, 2 * layer + 5)
        gathered(2, 2 * layer + 6)
        gathered(4, 2 * layer + 5)
        gathered(3, 2 * layer + 6)

    def ready_last():
        if last == 0:
            gathered(4, 2)
        gathered(5, 2 * last + 2)
        scalars[1] = tile_end(0) if sz.fused else jnp.broadcast_to(weight_ref[...], (8, 128))

    def attend_last(b):
        take_prev(last, b)
        attend(last, b)

    def turn(b):
        mlp(last, b)
        decode(b)
        mlp_back(last, b)
        attend_back(last, b)

    def send_last(b):
        if last > 0:
            send_prev(last, b)

    staggered(attend_last, turn, send_last, hooks=(None, ready_last))
    outer_mlp(last)
    summed(1, 2 * last + 2)
    outer_mixed(last)
    outer_pair(last)
    summed(1, 2 * last + 1)
    for layer in reversed(range(last)):

        def take_this(b, layer=layer):
            take_next(layer + 1, b)

        each(take_this)

        def back_this(b, layer=layer):
            join(layer + 1, b)
            mlp_back(layer, b)

        def pair_this(b, layer=layer):
            attend_back(layer, b)

        def send_this(b, layer=layer):
            if layer > 0:
                send_prev(layer, b)

        u = 2 * layer
        each(back_this, hooks=(None, lambda u=u: summed(2, u + 4), lambda u=u: summed(2, u + 3)))
        outer_mlp(layer)
        summed(1, u + 2)
        summed(3, u + 4)
        hooks = (None, lambda u=u: summed(2, u + 2), lambda u=u: summed(3, u + 3))
        if layer > 0:
            staggered(pair_this, send_this, hooks=hooks)
        else:
            each(pair_this, hooks=hooks)
        outer_mixed(layer)
        outer_pair(layer)
        summed(1, u + 1)
        summed(4, u + 4)
        if layer > 0:
            summed(4, u + 3)

    def last_back(b):
        join(0, b)
        encode_back(b)

    each(last_back, hooks=(None, lambda: summed(3, 2), lambda: summed(2, 1)))
    wide = jnp.concatenate([affine_grad[...], jnp.zeros((112, width), F32)], axis=0)

    @pl.when(j == 0)
    def _():
        put_total(
            0,
            tn(low[...].reshape(many, width), rows_in[:, :, :, 0:256].reshape(many, 256))
            + tn(mid_low[...].reshape(many, width), rows_prev[...].reshape(many, 256)),
        )

    @pl.when(j == 1)
    def _():
        put_total(
            0,
            jnp.concatenate(
                [
                    jnp.transpose(wide),
                    tn(final[...].reshape(many, width), grad_pred[...].reshape(many, 128)),
                ],
                axis=1,
            ),
        )

    if sz.fused:
        reduce_one(0)
        if sz.layers > 1:
            reduce_four(3)
        reduce_three(1)
        reduce_two(0)
        reduce_four(2)
        reduce_three(0)
        for unit in range(2, len(sz.units)):
            reduce_done(unit)
        reduce_four(1)
        reduce_four(0)
        reduce_done(1)
        reduce_done(0)
        squares = jnp.zeros((1, 1), F32)
        for index in range(sz.mats):
            value = share[index]
            squares = squares + jnp.sum(
                jnp.sum(value * value, axis=1, keepdims=True), axis=0, keepdims=True
            )
        sub = lax.broadcasted_iota(jnp.int32, (8, 128), 0)
        tile[1, 0] = jnp.where(sub == 0, squares, loss_acc[0:1, 0:1])
        tile_start(1)
        result = tile_end(1)
        scalars[0] = jnp.broadcast_to(result[1:2, :], (8, 128))
        scalars[2] = jnp.broadcast_to(jnp.sqrt(result[0:1, :]), (8, 128))
    else:
        scalars[0] = loss_acc[...]
        scalars[2] = loss_acc[...]

    for make in waits:
        make().wait_send()
    for layer in range(sz.layers):
        for b in range(nb):
            mix_copy(layer, b).wait_send()
            if layer > 0:
                n_copy(layer, b).wait_send()
                n_forward(layer, b, mine).wait_send()
                dn_copy(layer, b).wait_send()
                dn_forward(layer, b, mine).wait_send()


def dma(*shape):
    return pltpu.SemaphoreType.DMA(shape)


def train_kernel(sz, operands):
    nb, rows, half, width, cols = sz.batches, sz.rows, sz.half, sz.width, sz.cols
    layers = sz.layers
    scratch = []
    if sz.fused:
        out_shape = (
            jax.ShapeDtypeStruct((sz.mats, sz.shard, width), F32),
            jax.ShapeDtypeStruct((3, 8, 128), F32),
        )
        scratch += [
            pltpu.VMEM((sz.mats, sz.depth, 2, 2, 2, sz.shard, width), BF16),
            pltpu.VMEM((sz.mats, sz.depth, 2, 2, 2, sz.shard, cols), F32),
        ]
    else:
        out_shape = (
            jax.ShapeDtypeStruct((sz.mats, width, cols), F32),
            jax.ShapeDtypeStruct((3, 8, 128), F32),
        )
    scratch += [
        pltpu.VMEM((nb, half, 384), BF16),
        pltpu.VMEM((nb, 2, half, 384), BF16),
        pltpu.VMEM((nb, 2, half, 256), BF16),
        pltpu.VMEM((3, 32, rows), jnp.int32),
        pltpu.VMEM((nb, rows, width), BF16),
        pltpu.VMEM((nb, rows, width), BF16),
        pltpu.VMEM((layers, nb, rows, width), F32),
        pltpu.VMEM(((layers - 1) * nb + 1, rows, width), F32),
        pltpu.VMEM(((layers - 1) * nb + 1, rows, width), F32),
        pltpu.VMEM((layers, nb, 2, rows, cols), BF16),
        pltpu.VMEM((layers, nb, rows, cols), BF16),
        pltpu.VMEM((layers, nb, 2, 2 * rows, cols), BF16),
        pltpu.VMEM((layers, nb, sz.near, rows, 2 * rows), BF16),
        pltpu.VMEM((rows, 2 * rows), F32),
    ]
    scratch += [pltpu.VMEM((rows, rows), BF16)] * 6
    scratch += [pltpu.VMEM((16, width), F32)] * 2
    scratch += [
        pltpu.VMEM((nb, rows, width), BF16),
        pltpu.VMEM((nb, rows, 128), BF16),
        pltpu.VMEM((nb, rows, width), BF16),
        pltpu.VMEM((nb, rows, width), BF16),
        pltpu.VMEM((nb, rows, width), BF16),
        pltpu.VMEM((layers, nb, rows, width), BF16),
        pltpu.VMEM((layers, nb, rows, width), BF16),
        pltpu.VMEM((nb, rows, width), BF16),
        pltpu.VMEM((nb, rows, width), BF16),
        pltpu.VMEM((nb, rows, 5 * cols), BF16),
        pltpu.VMEM((nb, rows, 5 * cols), BF16),
        pltpu.VMEM((max(layers - 1, 1), nb, rows, cols), BF16),
        pltpu.VMEM((max(layers - 1, 1), nb, rows, width), BF16),
        pltpu.VMEM((8, 128), F32),
    ]
    scratch += [dma(3), dma(3), dma(2), dma(2), dma(2), dma(2)] + [dma(layers, nb)] * 12
    scratch += [pltpu.SemaphoreType.REGULAR]
    if sz.fused:
        depth, groups, units = sz.depth, len(sz.groups), len(sz.units)
        lane = cols // 2
        one_shape = (2, sz.mats, depth, 2, 2, sz.shard, lane)
        two_shape = (2, sz.mats, depth, 2, sz.shard, lane)
        scratch += [pltpu.VMEM(one_shape, jnp.int16)] * 2 + [pltpu.VMEM(two_shape, jnp.int16)] * 2
        scratch += [
            pltpu.VMEM((sz.mats, depth, 2, sz.shard, cols), jnp.int16),
            pltpu.VMEM((depth - 1, sz.mats, 2, sz.shard, cols), jnp.int16),
            pltpu.VMEM((sz.mats, sz.shard, cols), F32),
            pltpu.VMEM((2, 2, sz.mats, 8, lane), F32),
            pltpu.VMEM((2, 2, sz.mats, 8, lane), F32),
            pltpu.VMEM((sz.mats, 8, cols), F32),
            pltpu.VMEM((depth - 1, sz.mats, 8, cols), F32),
            pltpu.VMEM((2, 2, 8, 128), F32),
            pltpu.VMEM((2, 8, 128), F32),
            pltpu.VMEM((2, 4 * depth, 8, 128), F32),
        ]
        far = [dma(groups, depth - 1)] * 2
        scratch += far + [dma(groups, 2)] * 4 + [dma(groups)] * 2
        scratch += [dma(units, 4, 2)] * 2 + [dma(units, 2, depth - 1)] * 2 + [dma(units)] * 2
        scratch += [dma(2)] * 2 + [dma(2, 4 * depth - 1)] * 2
    return pl.pallas_call(
        functools.partial(step_kernel, sz),
        out_shape=out_shape,
        in_specs=[pl.BlockSpec(memory_space=pltpu.VMEM)] * len(operands),
        out_specs=(pl.BlockSpec(memory_space=pltpu.VMEM),) * 2,
        scratch_shapes=scratch,
        compiler_params=pltpu.CompilerParams(
            collective_id=0, has_side_effects=True, vmem_limit_bytes=60 * 1024 * 1024
        ),
    )(*operands)


def adam(weight, first, second, grad):
    first_new = BETA_ONE * first + (1.0 - BETA_ONE) * grad
    second_new = BETA_TWO * second + (1.0 - BETA_TWO) * grad * grad
    first_hat = first_new / (1.0 - BETA_ONE**STEP)
    second_hat = second_new / (1.0 - BETA_TWO**STEP)
    weight_new = weight - RATE * (first_hat / (jnp.sqrt(second_hat) + ADAM_EPS) + DECAY * weight)
    return (weight_new, first_new, second_new, weight_new.astype(BF16))


def adam_kernel(sz, share, scalars, *refs):
    masters = refs[:15]
    outs = refs[15:35]
    mat, inp, out, gain, bias = [masters[3 * k : 3 * k + 3] for k in range(5)]
    factor = jnp.minimum(1.0, CLIP / (scalars[2, 0:1, 0:1] + 1e-06))

    def put(k, values):
        for ref, value in zip(outs[4 * k : 4 * k + 4], values):
            ref[...] = value

    for index in range(sz.mats - 1):
        values = adam(mat[0][index], mat[1][index], mat[2][index], factor * share[1 + index])
        for ref, value in zip(outs[0:4], values):
            ref[index] = value
    last = share[0]
    put(1, adam(inp[0][...], inp[1][...], inp[2][...], factor * last[:, 0 : sz.c_in]))
    put(2, adam(out[0][...], out[1][...], out[2][...], factor * last[:, 384 : 384 + sz.c_out]))
    small = jnp.concatenate([last[:, 256:384], jnp.zeros((128 - sz.shard, 128), F32)], axis=0)
    small = jnp.transpose(small)[:, 0 : sz.shard]
    count = gain[0].shape[0]
    put(3, adam(gain[0][...], gain[1][...], gain[2][...], factor * small[0:count]))
    put(4, adam(bias[0][...], bias[1][...], bias[2][...], factor * small[8 : 8 + count]))


def update(sz, share, scalars, groups):
    operands = [share, scalars]
    out_shape = []
    for triple in groups:
        operands += list(triple)
        shape = triple[0].shape
        out_shape += [jax.ShapeDtypeStruct(shape, F32)] * 3 + [jax.ShapeDtypeStruct(shape, BF16)]
    return pl.pallas_call(
        functools.partial(adam_kernel, sz),
        out_shape=tuple(out_shape),
        in_specs=[pl.BlockSpec(memory_space=pltpu.VMEM)] * len(operands),
        out_specs=(pl.BlockSpec(memory_space=pltpu.VMEM),) * len(out_shape),
    )(*operands)


def per_device(
    grid_in, targets, area, row_count, g2m, m2g, senders, edge_count,
    mat_w, mat_m, mat_v, in_w, in_m, in_v, out_w, out_m, out_v,
    gain_w, gain_m, gain_v, bias_w, bias_m, bias_v,
):
    axes = ("node", "feat")
    sz = Sizes(
        lax.axis_size("node"),
        lax.axis_size("feat"),
        grid_in.shape[0],
        grid_in.shape[1],
        mat_w.shape[2],
        mat_w.shape[0] // 6,
        HEADS,
        senders.shape[1],
        grid_in.shape[2],
        targets.shape[2],
    )
    operands = [
        jnp.swapaxes(grid_in, 1, 2),
        jnp.swapaxes(targets, 1, 2),
        area.reshape(1, -1),
        row_count,
        g2m.T,
        m2g.T,
        senders.T,
        edge_count.reshape(1, -1),
    ]
    if sz.fused:
        operands += [mat_w, in_w.T, out_w, gain_w, bias_w]
        share, scalars = train_kernel(sz, operands)
        groups = (
            (mat_w, mat_m, mat_v),
            (in_w.T, in_m.T, in_v.T),
            (out_w, out_m, out_v),
            (gain_w, gain_m, gain_v),
            (bias_w, bias_m, bias_v),
        )
        outs = list(update(sz, share, scalars, groups))
        for index in range(4, 8):
            outs[index] = outs[index].T
        return tuple(outs) + (scalars[0, 0, 0], scalars[1, 0, 0], scalars[2, 0, 0])

    width, shard = sz.width, sz.shard

    def pad(value, size):
        return jnp.pad(value, ((0, 0), (0, size - value.shape[1])))

    def pack(square, inp, out, gain, bias):
        small = jnp.concatenate([pad(gain.T, 8), pad(bias.T, 120)], axis=1)
        first = jnp.concatenate([pad(inp.T, 256), small, pad(out, 128)], axis=1)
        return jnp.concatenate([first[None], square], axis=0)

    packed = pack(mat_w, in_w, out_w, gain_w, bias_w).astype(BF16)
    full = lax.all_gather(packed, axes, axis=1, tiled=True).reshape(sz.mats, 2, width // 2, width)
    live = (jnp.arange(sz.half)[None, :] < row_count).astype(F32)
    weight_total = lax.psum(jnp.sum(area[None, :] * live) * targets.shape[2], axes)
    operands += [full, weight_total.reshape(1, 1)]
    part, scalars = train_kernel(sz, operands)
    feat = lax.axis_index("feat")
    spread = lax.dynamic_update_slice(
        jnp.zeros((sz.mats, width, width), F32), part, (0, 0, feat * sz.cols)
    )
    share = lax.psum_scatter(spread, axes, scatter_dimension=1, tiled=True)
    square_sum, loss_sum = lax.psum((jnp.sum(share * share), scalars[0, 0, 0]), axes)
    grad_norm = jnp.sqrt(square_sum)
    share = jnp.minimum(1.0, CLIP / (grad_norm + 1e-06)) * share
    count = gain_w.shape[0]
    last = share[0]
    outs = adam(mat_w, mat_m, mat_v, share[1:])
    outs += adam(in_w, in_m, in_v, last[:, 0 : sz.c_in].T)
    outs += adam(out_w, out_m, out_v, last[:, 384 : 384 + sz.c_out])
    outs += adam(gain_w, gain_m, gain_v, last[:, 256 : 256 + count].T)
    outs += adam(bias_w, bias_m, bias_v, last[:, 264 : 264 + count].T)
    return outs + (loss_sum, weight_total, grad_norm)


def solution(mesh):
    both = ("node", "feat")
    rows_three = P(None, both, None)
    second = P(None, both)
    first = P(both, None)
    placed = (
        rows_three, rows_three, P(both), second,
        P("node", None), P("node", None), P("node", None), P("node"),
    )
    placed += (rows_three,) * 3 + (second,) * 3 + (first,) * 3 + (second,) * 6
    outs = (rows_three,) * 4 + (second,) * 4 + (first,) * 4 + (second,) * 8 + (P(), P(), P())
    return jax.shard_map(per_device, mesh=mesh, in_specs=placed, out_specs=outs, check_vma=False)
```

```python
import functools

import jax
import jax.numpy as jnp
from jax import lax
from jax.experimental import pallas as pl
from jax.experimental.pallas import tpu as pltpu
from jax.sharding import PartitionSpec as P

HEADS = 8
STEP = 5
NORM_EPS = 1e-05
CLIP = 0.05
RATE = 0.02
BETA_ONE = 0.5
BETA_TWO = 0.5
DECAY = 0.01
ADAM_EPS = 1e-08
DEAD = -1e30
MESH = pl.DeviceIdType.MESH
F32 = jnp.float32
BF16 = jnp.bfloat16


def nn(left, right):
    return jnp.dot(left, right, preferred_element_type=F32)


def nt(left, right):
    return lax.dot_general(left, right, (((1,), (1,)), ((), ())), preferred_element_type=F32)


def tn(left, right):
    return lax.dot_general(left, right, (((0,), (0,)), ((), ())), preferred_element_type=F32)


def norm_parts(state):
    centre = state - jnp.mean(state, axis=-1, keepdims=True)
    spread = jnp.mean(centre * centre, axis=-1, keepdims=True)
    scale = lax.rsqrt(spread + NORM_EPS)
    return centre * scale, scale


def norm_back(grad, hat, scale, gain):
    inner = grad * gain
    mean_inner = jnp.mean(inner, axis=-1, keepdims=True)
    mean_hat = jnp.mean(inner * hat, axis=-1, keepdims=True)
    return scale * (inner - mean_inner - hat * mean_hat)


def column_sum(value):
    return jnp.sum(value, axis=0, keepdims=True)


def sigmoid(value):
    return 0.5 * jnp.tanh(0.5 * value) + 0.5


def silu_slope(value):
    gate = sigmoid(value)
    return gate * (1.0 + value * (1.0 - gate))


class Sizes:
    def __init__(self, node, feat, batches, half, width, layers, heads, slots, c_in, c_out):
        self.node, self.feat = node, feat
        self.batches, self.half, self.width = batches, half, width
        self.rows = 2 * half
        self.layers, self.heads, self.slots = layers, heads, slots
        self.c_in, self.c_out = c_in, c_out
        self.shard = width // (node * feat)
        self.depth = node // 4
        self.mats = 6 * layers + 1
        self.cols = width // feat
        self.near = heads // feat
        self.fused = self.shard % 16 == 0 and node % 4 == 0
        self.groups = [(0, 1)] + [(first, 2) for first in range(1, self.mats, 2)]
        self.units = [(0, 1)]
        for layer in range(layers):
            self.units += [(1 + 6 * layer, 3), (4 + 6 * layer, 3)]


def step_kernel(sz, *refs):
    refs = list(refs)

    def take(count):
        out = refs[:count]
        del refs[:count]
        return out

    grid_ref, target_ref, area_ref, count_ref, g2m_ref, m2g_ref, send_ref, edge_ref = take(8)
    if sz.fused:
        mat_ref, in_ref, out_ref, gain_ref, bias_ref = take(5)
        share, scalars = take(2)
        full, total = take(2)
        held = take(13)
        (in_sems,) = take(1)
        incoming = [
            pltpu.make_async_copy(src, dst, in_sems.at[k])
            for k, (src, dst) in enumerate(
                zip(
                    (grid_ref, target_ref, area_ref, count_ref, g2m_ref, m2g_ref, send_ref, edge_ref)
                    + (mat_ref, in_ref, out_ref, gain_ref, bias_ref),
                    held,
                )
            )
        ]
        grid_ref, target_ref, area_ref, count_ref, g2m_ref, m2g_ref, send_ref, edge_ref = held[:8]
        mat_ref, in_ref, out_ref, gain_ref, bias_ref = held[8:]
    else:
        full, weight_ref = take(2)
        total, scalars = take(2)
    (
        rows_own,
        rows_in,
        rows_prev,
        indices,
        start,
        start_prev,
        state,
        middle,
        pre_mlp,
        mixed,
        query,
        pair,
        prob,
        edge_bias,
        g_row,
        g_col,
        gp_row,
        gp_col,
        m_row,
        m_col,
        affine,
        affine_grad,
        final,
        grad_pred,
        low,
        pre_low,
        mid_low,
        n_own,
        n_prev,
        n_two,
        hidden,
        d_own,
        d_far,
        dn_out,
        dn_in,
        loss_acc,
        square_acc,
    ) = take(37)
    (s_rows, r_rows, s_idx, r_idx, s_prev, r_prev) = take(6)
    (s_n, r_n, s_nf, r_nf, s_mix, r_mix, s_dn, r_dn, s_df, r_df, s_far, r_far) = take(12)
    (far_free,) = take(1)
    if sz.fused:
        (code_one, got_one, code_two, got_two, code_z, got_z, got_c) = take(7)
        (size_out, size_in, size_z, size_z_in, tile, tile_far, tile_all) = take(7)
        (gz_s, gz_r, g2_s, g2_r, g3_s, g3_r, g4_s, g4_r) = take(8)
        (rr_s, rr_r, rz_s, rz_r, rc_s, rc_r) = take(6)
        (t_s, t_r, tz_s, tz_r) = take(4)

    nb, rows, half, width, cols = sz.batches, sz.rows, sz.half, sz.width, sz.cols
    node = lax.axis_index("node")
    y = lax.axis_index("feat")
    waits = []
    if sz.fused:
        depth = sz.depth
        c = lax.rem(node, 2)
        x = lax.rem(node // 2, 2)
        z = node // 4
        j = c

        def device_of(zz, xx, cc, yy):
            return (zz * 4 + xx * 2 + cc, yy)

        def holder(block):
            return device_of(block // 4, lax.rem(block // 2, 2), c, lax.rem(block, 2))

        block = z * 4 + x * 2 + y
        after = holder(lax.rem(block + 1, sz.node))
        before = holder(lax.rem(block + sz.node - 1, sz.node))
        partner = device_of(z, x, 1 - c, y)
        x_dev = device_of(z, 1 - x, c, y)
        y_dev = device_of(z, x, c, 1 - y)
        z_devs = [device_of(lax.rem(z + step, depth), x, c, y) for step in range(1, depth)]

        def chip_at(dz, dx, dy):
            return device_of(lax.rem(z + dz, depth), lax.rem(x + dx, 2), c, lax.rem(y + dy, 2))

        offsets = [(k // 4, (k // 2) % 2, k % 2) for k in range(1, 4 * depth)]
        greet = [after, before, partner] + [chip_at(*offset) for offset in offsets]
    else:
        j = y
        after = (lax.rem(node + 1, sz.node), j)
        before = (lax.rem(node + sz.node - 1, sz.node), j)
        partner = (node, 1 - j)
        greet = [after, before, partner]
    other = 1 - j
    mine = pl.ds(pl.multiple_of(j * cols, cols), cols)
    theirs = pl.ds(pl.multiple_of(other * cols, cols), cols)

    def remote(src, dst, s_sem, r_sem, device):
        return pltpu.make_async_remote_copy(
            src_ref=src, dst_ref=dst, send_sem=s_sem, recv_sem=r_sem, device_id=device, device_id_type=MESH
        )

    def push(make):
        make().start()
        waits.append(make)

    barrier = pltpu.get_barrier_semaphore()
    for device in greet:
        pl.semaphore_signal(barrier, inc=1, device_id=device, device_id_type=MESH)
    if sz.fused:
        for copy in incoming:
            copy.start()
        for copy in incoming:
            copy.wait()

    lanes_c = lax.broadcasted_iota(jnp.int32, (1, cols), 1) // (width // sz.heads)
    mask_low = [(lanes_c == head).astype(F32).astype(BF16) for head in range(sz.near)]
    mask_full = [(lanes_c == head).astype(F32) for head in range(sz.near)]

    def w_full(index):
        return full[index].reshape(width, width)

    def w_cols(index, which):
        if sz.fused:
            return full[index, :, :, :, :, :, which].reshape(width, cols)
        return full[index, :, :, which].reshape(width, cols)

    def w_rows(index, which):
        if sz.fused:
            count = sz.depth // 2
            return full[index, pl.ds(which * count, count)].reshape(width // 2, width)
        return full[index, which]

    def w_block(index, rows_half, which):
        if sz.fused:
            count = sz.depth // 2
            return full[index, pl.ds(rows_half * count, count), :, :, :, :, which].reshape(width // 2, cols)
        return full[index, rows_half, :, which]

    def put_total(index, value):
        total[index] = value.reshape(total.shape[1:])

    cell = lax.broadcasted_iota(jnp.int32, (1, half), 1)
    for b in range(nb):
        block_in = jnp.concatenate([grid_ref[b].astype(F32), jnp.zeros((256 - sz.c_in, half), F32)], axis=0)
        rows_own[b, :, 0:256] = jnp.transpose(block_in).astype(BF16)
        weight = jnp.where(cell < count_ref[0:1, b : b + 1], area_ref[...], 0.0)
        first = weight.astype(BF16).astype(F32)
        second = (weight - first).astype(BF16).astype(F32)
        third = weight - first - second
        block_in = jnp.concatenate(
            [target_ref[b].astype(F32), jnp.zeros((125 - sz.c_out, half), F32), first, second, third], axis=0
        )
        rows_own[b, :, 256:384] = jnp.transpose(block_in).astype(BF16)
    slot = c if sz.fused else 0
    k_g = g2m_ref.shape[0]
    k_m = m2g_ref.shape[0]
    receiver = lax.broadcasted_iota(jnp.int32, (1, rows), 1)
    indices[slot, 0:k_g] = g2m_ref[...]
    indices[slot, 8 : 8 + k_m] = m2g_ref[...]
    indices[slot, 15:16] = jnp.where(receiver < rows // 2, edge_ref[0:1, 0:1], edge_ref[0:1, 1:2])
    indices[slot, 16 : 16 + sz.slots] = send_ref[...]
    if sz.fused:
        n_groups = len(sz.groups)
        packed = jnp.concatenate(
            [
                in_ref[...],
                jnp.zeros((sz.shard, 256 - sz.c_in), F32),
                jnp.zeros((sz.shard, 128), F32),
                out_ref[...],
                jnp.zeros((sz.shard, 128 - sz.c_out), F32),
            ],
            axis=1,
        )
        small = jnp.concatenate(
            [
                gain_ref[...],
                jnp.zeros((3, sz.shard), F32),
                bias_ref[...],
                jnp.zeros((3, sz.shard), F32),
            ],
            axis=0,
        )
        small = jnp.concatenate([small, jnp.zeros((16, 128 - sz.shard), F32)], axis=1)
        small = jnp.concatenate([small, jnp.zeros((112, 128), F32)], axis=0)
        small = jnp.transpose(small)[0 : sz.shard, :]
        full[0, z, x, c, y] = jnp.concatenate([packed[:, 0:256], small, packed[:, 384:512]], axis=1).astype(BF16)
        for index in range(sz.mats - 1):
            full[1 + index, z, x, c, y] = mat_ref[index].astype(BF16)

    pl.semaphore_wait(barrier, len(greet))

    here = rows_in.at[:, y]
    there = rows_in.at[:, 1 - y]
    if sz.fused:
        push(lambda: remote(indices.at[c], indices.at[c], s_idx.at[0], r_idx.at[0], partner))
        to_partner = remote(rows_own, here, s_rows.at[0], r_rows.at[0], partner)
        to_chip = remote(rows_own, here, s_rows.at[1], r_rows.at[1], y_dev)
        forward = remote(there, there, s_rows.at[2], r_rows.at[1], partner)

        @pl.when(c == y)
        def _():
            to_partner.start()
            rows_in[:, y] = rows_own[...]

        @pl.when(c != y)
        def _():
            to_chip.start()

    else:
        push(lambda: remote(rows_own, here, s_rows.at[0], r_rows.at[0], partner))
        rows_in[:, y] = rows_own[...]

    if sz.fused:

        def gather_one(g):
            first, count = sz.groups[g]
            for step in range(1, depth):

                def make(g=g, first=first, count=count, step=step):
                    own = full.at[pl.ds(first, count), z, x, c, y]
                    return remote(own, own, gz_s.at[g, step - 1], gz_r.at[g, step - 1], z_devs[step - 1])

                push(make)

        gather_one(0)
        gather_one(1)

    if sz.fused:
        weight_sum = jnp.zeros((1, 1), F32)
        for b in range(nb):
            weight = jnp.where(cell < count_ref[0:1, b : b + 1], area_ref[...], 0.0)
            weight_sum = weight_sum + jnp.sum(weight, axis=1, keepdims=True)
        tile[0, 0] = jnp.broadcast_to(weight_sum * float(sz.c_out), (8, 128))

        def tile_core(slot):
            return remote(tile.at[slot, 0], tile_far.at[slot], t_s.at[slot], t_r.at[slot], partner)

        def tile_chip(slot, k, place):
            return remote(
                tile.at[slot, 1], tile_all.at[slot, place], tz_s.at[slot, k], tz_r.at[slot, k], chip_at(*offsets[k])
            )

        def tile_start(slot):
            tile_core(slot).start()
            tile_core(slot).wait()
            tile[slot, 1] = tile[slot, 0] + tile_far[slot]
            spot = z * 4 + x * 2 + y
            tile_all[slot, spot] = tile[slot, 1]
            for k in range(len(offsets)):
                tile_chip(slot, k, spot).start()

        def tile_end(slot):
            for k, (dz, dx, dy) in enumerate(offsets):
                source = (
                    lax.rem(z + depth - dz, depth) * 4 + lax.rem(x + 2 - dx, 2) * 2 + lax.rem(y + 2 - dy, 2)
                )
                tile_chip(slot, k, source).wait()
            result = tile_all[slot, 0]
            for index in range(1, 4 * depth):
                result = result + tile_all[slot, index]
            return result

        tile_start(0)

    if sz.fused:
        remote(indices.at[1 - c], indices.at[1 - c], s_idx.at[0], r_idx.at[0], partner).wait_recv()
        slot = y
    push(lambda: remote(indices.at[slot], indices.at[2], s_idx.at[1], r_idx.at[1], after))

    affine_grad[...] = jnp.zeros_like(affine_grad)
    loss_acc[...] = jnp.zeros_like(loss_acc)
    square_acc[...] = jnp.zeros_like(square_acc)

    if sz.fused:
        side_a = pl.ds(0, width // 2)
        side_b = pl.ds(width // 2, width // 2)

        def gather_part(g, stage, which):
            span = pl.ds(*sz.groups[g])
            if stage == 2:
                return full.at[span, :, x, c, y, :, which]
            if which is side_a:
                return full.at[span, :, :, c, y, :, which]
            return full.at[span, :, x, c, :, :, which]

        def gather_push(g, stage, side, sems, device):
            which = (side_a, side_b)[side]

            def make():
                part = gather_part(g, stage, which)
                return remote(part, part, sems[0].at[g, side], sems[1].at[g, side], device)

            push(make)

        def arrived(part, s_sem, r_sem, device):
            remote(part, part, s_sem, r_sem, device).wait_recv()

        def gather_two(g):
            span = pl.ds(*sz.groups[g])
            for step in range(1, depth):
                there = full.at[span, lax.rem(z + depth - step, depth), x, c, y]
                arrived(there, gz_s.at[g, step - 1], gz_r.at[g, step - 1], z_devs[step - 1])
            gather_push(g, 2, 0, (g2_s, g2_r), x_dev)
            gather_push(g, 2, 1, (g2_s, g2_r), y_dev)

        def gather_three(g):
            span = pl.ds(*sz.groups[g])
            arrived(full.at[span, :, 1 - x, c, y, :, side_a], g2_s.at[g, 0], g2_r.at[g, 0], x_dev)
            gather_push(g, 3, 0, (g3_s, g3_r), y_dev)
            arrived(full.at[span, :, x, c, 1 - y, :, side_b], g2_s.at[g, 1], g2_r.at[g, 1], y_dev)
            gather_push(g, 3, 1, (g3_s, g3_r), x_dev)

        def gather_four(g):
            span = pl.ds(*sz.groups[g])
            arrived(full.at[span, :, :, c, 1 - y, :, side_a], g3_s.at[g, 0], g3_r.at[g, 0], y_dev)
            arrived(full.at[span, :, 1 - x, c, :, :, side_b], g3_s.at[g, 1], g3_r.at[g, 1], x_dev)

            def make():
                part = full.at[span, :, :, c]
                return remote(part, part, g4_s.at[g], g4_r.at[g], partner)

            push(make)

        def gather_done(g):
            span = pl.ds(*sz.groups[g])
            arrived(full.at[span, :, :, 1 - c], g4_s.at[g], g4_r.at[g], partner)

    def gather_step(step):
        if not sz.fused:
            return
        for stage, move in enumerate((gather_two, gather_three, gather_four, gather_done)):
            if 0 <= step - stage < len(sz.groups):
                move(step - stage)
        if 2 <= step + 2 < len(sz.groups):
            gather_one(step + 2)

    in_cols = pl.ds(0, 256)
    small_cols = pl.ds(256, 128)
    out_cols = pl.ds(384, 128)

    def aux(which, size):
        if sz.fused:
            return full[0, :, :, :, :, :, which].reshape(width, size)
        return full[0, :, :, which].reshape(width, size)

    gather_step(0)
    if sz.fused:

        @pl.when(c == y)
        def _():
            remote(there, there, s_rows.at[1], r_rows.at[1], y_dev).wait_recv()
            forward.start()
            to_partner.wait_send()
            forward.wait_send()

        @pl.when(c != y)
        def _():
            to_chip.wait_send()
            remote(here, here, s_rows.at[0], r_rows.at[0], partner).wait_recv()
            remote(there, there, s_rows.at[2], r_rows.at[1], partner).wait_recv()

    else:
        remote(there, there, s_rows.at[0], r_rows.at[0], partner).wait_recv()

    push(lambda: remote(rows_in.at[:, j, :, 0:256], rows_prev.at[:, j], s_prev.at[0], r_prev.at[0], after))

    gather_step(1)
    def counts(place, first, slots, origin, live=None):
        wide = lax.broadcasted_iota(jnp.int32, (rows, rows), 0) + origin
        acc = jnp.zeros((rows, rows), F32)
        for k in range(slots):
            hit = wide == indices[place, first + k : first + k + 1, :]
            if live is not None:
                hit = jnp.logical_and(hit, live > k)
            acc = acc + jnp.where(hit, 1.0, 0.0)
        return acc

    live = indices[slot, 15:16, :]
    for part in range(2):
        acc = jnp.transpose(counts(slot, 16, sz.slots, part * rows, live))
        edge_bias[:, part * rows : (part + 1) * rows] = jnp.where(acc > 0.5, jnp.log(jnp.maximum(acc, 1.0)), DEAD)
    table = counts(slot, 0, k_g, 0)
    g_col[...] = table.astype(BF16)
    g_row[...] = jnp.transpose(table).astype(BF16)
    table = counts(slot, 8, k_m, 0)
    m_col[...] = table.astype(BF16)
    m_row[...] = jnp.transpose(table).astype(BF16)
    gather_step(2)
    remote(rows_prev.at[:, j], rows_prev.at[:, j], s_prev.at[0], r_prev.at[0], after).wait_recv()
    push(lambda: remote(rows_prev.at[:, j], rows_prev.at[:, j], s_prev.at[1], r_prev.at[1], partner))
    remote(indices.at[slot], indices.at[2], s_idx.at[1], r_idx.at[1], after).wait_recv()
    table = counts(2, 0, k_g, 0)
    gp_col[...] = table.astype(BF16)
    gp_row[...] = jnp.transpose(table).astype(BF16)
    gather_step(3)
    remote(rows_prev.at[:, other], rows_prev.at[:, other], s_prev.at[1], r_prev.at[1], partner).wait_recv()

    affine[...] = jnp.transpose(aux(small_cols, 128).astype(F32))[0:16, :]

    def gain_row(index):
        return affine[pl.ds(index, 1), :]

    def bias_row(index):
        return affine[pl.ds(8 + index, 1), :]

    def add_affine(index, value):
        affine_grad[pl.ds(index, 1), :] = affine_grad[pl.ds(index, 1), :] + value

    def staggered(*bodies, hooks=()):
        def wrapped(t, carry):
            for step, hook in enumerate(hooks):
                if hook is not None:
                    pl.when(t == step)(hook)
            for late in reversed(range(len(bodies))):

                @pl.when(jnp.logical_and(t >= late, t < nb + late))
                def _(late=late):
                    bodies[late](t - late)

            return carry

        lax.fori_loop(0, nb + len(bodies) - 1, wrapped, 0)

    def each(body, hooks=()):
        def wrapped(b, carry):
            for step, hook in enumerate(hooks):
                if hook is not None:
                    pl.when(b == step)(hook)
            body(b)
            return carry

        lax.fori_loop(0, nb, wrapped, 0)

    def pre_encode(ref, b):
        return nt(ref[b, :, :, 0:256].reshape(rows, 256), aux(in_cols, 256)) + bias_row(0)

    def encode(b):
        gain = gain_row(0)
        for ref, table, keep, normed in (
            (rows_in, g_row, start, n_own),
            (rows_prev, gp_row, start_prev, n_prev),
        ):
            pre = pre_encode(ref, b)
            enc = (pre * sigmoid(pre)).astype(BF16)
            first = (nn(table[...], enc) * (1.0 / k_g)).astype(BF16)
            keep[b] = first
            hat, _ = norm_parts(first.astype(F32))
            normed[0, b] = (hat * gain).astype(BF16)

    def n_copy(layer, b):
        return remote(
            n_own.at[layer, b, :, mine], n_prev.at[layer, b, :, mine], s_n.at[layer, b], r_n.at[layer, b], after
        )

    def n_forward(layer, b, which):
        there = n_prev.at[layer, b, :, which]
        return remote(there, there, s_nf.at[layer, b], r_nf.at[layer, b], partner)

    def mix_copy(layer, b):
        return remote(
            mixed.at[layer, b, j], mixed.at[layer, b, j], s_mix.at[layer, b], r_mix.at[layer, b], partner
        )

    def mix_wait(layer, b):
        there = mixed.at[layer, b, other]
        remote(there, there, s_mix.at[layer, b], r_mix.at[layer, b], partner).wait_recv()

    scale = float(width // sz.heads) ** -0.5

    def spot(layer, b):
        return layer * nb + (b if layer < sz.layers - 1 else 0)

    def entry(layer, b):
        if layer == 0:
            return start[b].astype(F32)
        return state[layer - 1, b]

    def project(layer, b):
        base = 1 + 6 * layer
        if layer > 0:
            hat, _ = norm_parts(state[layer - 1, b])
            n_own[layer, b] = (hat * gain_row(2 * layer)).astype(BF16)
            n_copy(layer, b).start()
        normed = n_own[layer, b]
        query[layer, b] = nn(normed, w_cols(base, mine)).astype(BF16)
        pair[layer, b, 0, 0:rows] = nn(normed, w_cols(base + 1, mine)).astype(BF16)
        pair[layer, b, 1, 0:rows] = nn(normed, w_cols(base + 2, mine)).astype(BF16)

    def take_prev(layer, b):
        if layer > 0:
            n_copy(layer, b).wait_recv()
            n_forward(layer, b, mine).start()

    def attend(layer, b):
        base = 1 + 6 * layer
        if layer > 0:
            n_forward(layer, b, theirs).wait_recv()
        normed = n_prev[layer, b]
        pair[layer, b, 0, rows : 2 * rows] = nn(normed, w_cols(base + 1, mine)).astype(BF16)
        pair[layer, b, 1, rows : 2 * rows] = nn(normed, w_cols(base + 2, mine)).astype(BF16)
        keys, values, queries = pair[layer, b, 0], pair[layer, b, 1], query[layer, b]
        out = jnp.zeros((rows, cols), F32)
        for head in range(sz.near):
            score = nt(queries * mask_low[head], keys) * scale + edge_bias[...]
            expo = jnp.exp(score - jnp.max(score, axis=-1, keepdims=True))
            weight = (expo * (1.0 / jnp.sum(expo, axis=-1, keepdims=True))).astype(BF16)
            prob[layer, b, head] = weight
            out = out + nn(weight, values) * mask_full[head]
        mixed[layer, b, j] = out.astype(BF16)
        mix_copy(layer, b).start()

    def mlp(layer, b):
        base = 1 + 6 * layer
        mix_wait(layer, b)
        mid = (
            entry(layer, b)
            + nn(mixed[layer, b, 0], w_rows(base + 3, 0))
            + nn(mixed[layer, b, 1], w_rows(base + 3, 1))
        )
        middle[spot(layer, b)] = mid
        hat, _ = norm_parts(mid)
        normed = (hat * gain_row(2 * layer + 1)).astype(BF16)
        pre = nn(normed, w_full(base + 4)) + bias_row(1 + 2 * layer)
        pre_mlp[spot(layer, b)] = pre
        act = (pre * sigmoid(pre)).astype(BF16)
        state[layer, b] = mid + nn(act, w_full(base + 5)) + bias_row(2 + 2 * layer)

    last = sz.layers - 1
    lane_out = lax.broadcasted_iota(jnp.int32, (1, 128), 1)
    row_index = lax.broadcasted_iota(jnp.int32, (rows, 1), 0)
    own_row = jnp.logical_and(row_index >= j * half, row_index < (j + 1) * half).astype(F32)
    real_lane = (lane_out < sz.c_out).astype(F32)

    def decode(b):
        gain = gain_row(2 * sz.layers)
        dec = (nn(m_row[...], state[last, b].astype(BF16)) * (1.0 / k_m)).astype(BF16).astype(F32)
        hat, inv = norm_parts(dec)
        normed = (hat * gain).astype(BF16)
        final[b] = normed
        weights = aux(out_cols, 128)
        goal = rows_in[b, :, :, 256:384].reshape(rows, 128).astype(F32)
        error = (nn(normed, weights) - goal) * real_lane
        weight = goal[:, 125:126] + goal[:, 126:127] + goal[:, 127:128]
        loss_acc[...] = loss_acc[...] + jnp.sum(
            jnp.sum((weight * own_row) * error * error, axis=1, keepdims=True), axis=0, keepdims=True
        )
        pred_low = (2.0 * weight * error / scalars[1, 0:1, 0:1]).astype(BF16)
        grad_pred[b] = pred_low
        back = nt(pred_low, weights)
        add_affine(2 * sz.layers, column_sum(back * hat))
        dec_low = norm_back(back, hat, inv, gain).astype(BF16)
        state[last, b] = (nn(m_col[...], dec_low) * (1.0 / k_m)).astype(BF16).astype(F32)

    if sz.fused:
        lane_a = pl.ds(0, cols // 2)
        lane_b = pl.ds(cols // 2, cols // 2)
        lanes = (lane_a, lane_b)
        top = 32767.0

        def encoded(value, code_ref, scale_ref):
            size = jnp.max(jnp.abs(value), axis=tuple(range(value.ndim - 1)), keepdims=True)
            size = size.reshape(1, size.shape[-1])
            inverse = jnp.where(size > 1e-30, top / jnp.maximum(size, 1e-30), 0.0)
            code_ref[...] = jnp.round(value * inverse).astype(jnp.int32).astype(jnp.int16)
            scale_ref[...] = jnp.broadcast_to(size * (1.0 / top), scale_ref.shape)

        def decoded(code, scale_row):
            return code.astype(jnp.int32).astype(F32) * scale_row

        def over(unit, body):
            first, count = sz.units[unit]

            def wrapped(m, carry):
                body(m)
                return carry

            lax.fori_loop(first, first + count, wrapped, 0)

        def send_codes(unit, stage, side, device):
            span = pl.ds(*sz.units[unit])
            codes_out, codes_in = ((code_one, got_one), (code_two, got_two))[stage]

            def make_codes():
                k = 2 * stage
                return remote(
                    codes_out.at[side, span], codes_in.at[side, span], rr_s.at[unit, k, side], rr_r.at[unit, k, side], device
                )

            def make_scales():
                k = 2 * stage + 1
                return remote(
                    size_out.at[stage, side, span],
                    size_in.at[stage, side, span],
                    rr_s.at[unit, k, side],
                    rr_r.at[unit, k, side],
                    device,
                )

            return make_codes, make_scales

        def reduce_one(unit):
            def body(m):
                encoded(total[m, :, 1 - x, :, :, :, lane_a], code_one.at[0, m], size_out.at[0, 0, m])
                encoded(total[m, :, :, :, 1 - y, :, lane_b], code_one.at[1, m], size_out.at[0, 1, m])

            over(unit, body)
            for side, device in ((0, x_dev), (1, y_dev)):
                for make in send_codes(unit, 0, side, device):
                    push(make)

        def reduce_two(unit):
            for side, device in ((0, x_dev), (1, y_dev)):
                for make in send_codes(unit, 0, side, device):
                    make().wait_recv()

            def body(m):
                row_a = size_in[0, 0, m, 0:1, :]
                row_b = size_in[0, 1, m, 0:1, :]
                total[m, :, x, :, :, :, lane_a] = total[m, :, x, :, :, :, lane_a] + decoded(got_one[0, m], row_a)
                total[m, :, :, :, y, :, lane_b] = total[m, :, :, :, y, :, lane_b] + decoded(got_one[1, m], row_b)
                encoded(total[m, :, x, :, 1 - y, :, lane_a], code_two.at[0, m], size_out.at[1, 0, m])
                encoded(total[m, :, 1 - x, :, y, :, lane_b], code_two.at[1, m], size_out.at[1, 1, m])

            over(unit, body)
            for side, device in ((0, y_dev), (1, x_dev)):
                for make in send_codes(unit, 1, side, device):
                    push(make)

        def send_z(unit, step):
            span = pl.ds(*sz.units[unit])

            def make_codes():
                return remote(
                    code_z.at[span, lax.rem(z + step, depth)],
                    got_z.at[step - 1, span],
                    rz_s.at[unit, 0, step - 1],
                    rz_r.at[unit, 0, step - 1],
                    z_devs[step - 1],
                )

            def make_scales():
                return remote(
                    size_z.at[span],
                    size_z_in.at[step - 1, span],
                    rz_s.at[unit, 1, step - 1],
                    rz_r.at[unit, 1, step - 1],
                    z_devs[step - 1],
                )

            return make_codes, make_scales

        def reduce_three(unit):
            for side, device in ((0, y_dev), (1, x_dev)):
                for make in send_codes(unit, 1, side, device):
                    make().wait_recv()

            def body(m):
                for side in range(2):
                    row = size_in[1, side, m, 0:1, :]
                    total[m, :, x, :, y, :, lanes[side]] = total[m, :, x, :, y, :, lanes[side]] + decoded(
                        got_two[side, m], row
                    )
                encoded(total[m, :, x, :, y], code_z.at[m], size_z.at[m])

            over(unit, body)
            for step in range(1, depth):
                for make in send_z(unit, step):
                    push(make)

        def core_copy(unit):
            span = pl.ds(*sz.units[unit])
            return remote(total.at[span, z, x, 1 - c, y], got_c.at[span], rc_s.at[unit], rc_r.at[unit], partner)

        def reduce_four(unit):
            for step in range(1, depth):
                for make in send_z(unit, step):
                    make().wait_recv()

            def body(m):
                acc = total[m, z, x, :, y]
                for step in range(1, depth):
                    acc = acc + decoded(got_z[step - 1, m], size_z_in[step - 1, m, 0:1, :])
                total[m, z, x, :, y] = acc
                square_acc[...] = square_acc[...] + jnp.sum(acc * acc, axis=(0, 1)).reshape(1, cols)

            over(unit, body)
            push(lambda: core_copy(unit))

        def reduce_done(unit):
            core_copy(unit).wait_recv()

            def body(m):
                share[m, :, mine] = total[m, z, x, c, y]
                share[m, :, theirs] = got_c[m]

            over(unit, body)

        stages = (None, reduce_one, reduce_two, reduce_three, reduce_four, reduce_done)

    def summed(stage, unit):
        if sz.fused:
            stages[stage](unit)

    def far_copy(layer, b):
        return remote(d_own.at[b], d_far.at[b], s_far.at[layer, b], r_far.at[layer, b], partner)

    def dn_copy(layer, b):
        return remote(
            dn_out.at[layer - 1, b],
            dn_in.at[layer - 1, b, :, mine],
            s_dn.at[layer, b],
            r_dn.at[layer, b],
            before,
        )

    def dn_forward(layer, b, which):
        there = dn_in.at[layer - 1, b, :, which]
        return remote(there, there, s_df.at[layer, b], r_df.at[layer, b], partner)

    def mlp_back(layer, b):
        base = 1 + 6 * layer
        grad = state[last, b]
        grad_low = grad.astype(BF16)
        low[b] = grad_low
        add_affine(8 + 2 + 2 * layer, column_sum(grad))
        pre = pre_mlp[spot(layer, b)]
        gate = sigmoid(pre)
        hidden[b] = (pre * gate).astype(BF16)
        back = (nt(grad_low, w_full(base + 5)) * (gate * (1.0 + pre * (1.0 - gate)))).astype(BF16)
        pre_low[b] = back
        add_affine(8 + 1 + 2 * layer, column_sum(back.astype(F32)))
        back = nt(back, w_full(base + 4))
        gain = gain_row(2 * layer + 1)
        hat, inv = norm_parts(middle[spot(layer, b)])
        n_two[b] = (hat * gain).astype(BF16)
        add_affine(2 * layer + 1, column_sum(back * hat))
        grad = grad + norm_back(back, hat, inv, gain)
        state[last, b] = grad
        mid_low[b] = grad.astype(BF16)

    def attend_back(layer, b):
        base = 1 + 6 * layer
        grad_out = nt(mid_low[b], w_rows(base + 3, j)).astype(BF16)
        keys, values, queries = pair[layer, b, 0], pair[layer, b, 1], query[layer, b]
        d_query = jnp.zeros((rows, cols), F32)
        d_keys = jnp.zeros((2 * rows, cols), F32)
        d_values = jnp.zeros((2 * rows, cols), F32)
        for head in range(sz.near):
            weight_low = prob[layer, b, head]
            out_head = grad_out * mask_low[head]
            weight = weight_low.astype(F32)
            part = weight * nt(out_head, values)
            score = (part - weight * jnp.sum(part, axis=-1, keepdims=True)).astype(BF16)
            d_query = d_query + nn(score, keys) * mask_full[head]
            d_keys = d_keys + tn(score, queries * mask_low[head])
            d_values = d_values + tn(weight_low, out_head)
        d_keys = (d_keys * scale).astype(BF16)
        d_values = d_values.astype(BF16)
        d_own[b, :, 0:cols] = (d_query * scale).astype(BF16)
        d_own[b, :, cols : 2 * cols] = d_keys[0:rows]
        d_own[b, :, 2 * cols : 3 * cols] = d_values[0:rows]
        d_own[b, :, 3 * cols : 4 * cols] = d_keys[rows:]
        d_own[b, :, 4 * cols : 5 * cols] = d_values[rows:]
        if layer < last:
            pl.semaphore_wait(far_free, 1)
        far_copy(layer, b).start()

    def send_prev(layer, b):
        base = 1 + 6 * layer
        far_copy(layer, b).wait()
        back = jnp.zeros((rows, cols), F32)
        for which in (1, 2):
            part = pl.ds((which + 2) * cols, cols)
            back = back + nt(d_own[b, :, part], w_block(base + which, j, mine))
            back = back + nt(d_far[b, :, part], w_block(base + which, j, theirs))
        dn_out[layer - 1, b] = back.astype(BF16)
        dn_copy(layer, b).start()

    def take_next(layer, b):
        dn_copy(layer, b).wait_recv()
        dn_forward(layer, b, mine).start()

    def join(layer, b):
        base = 1 + 6 * layer
        if layer > 0:
            dn_forward(layer, b, theirs).wait_recv()
            back = dn_in[layer - 1, b].astype(F32)
        else:
            far_copy(layer, b).wait()
            back = jnp.zeros((rows, width), F32)
        for which in range(3):
            part = pl.ds(which * cols, cols)
            back = back + nt(d_own[b, :, part], w_cols(base + which, mine))
            back = back + nt(d_far[b, :, part], w_cols(base + which, theirs))
        if layer > 0:
            pl.semaphore_signal(far_free, inc=1, device_id=partner, device_id_type=MESH)
        gain = gain_row(2 * layer)
        hat, inv = norm_parts(entry(layer, b))
        add_affine(2 * layer, column_sum(back * hat))
        state[last, b] = state[last, b] + norm_back(back, hat, inv, gain)

    many = nb * rows

    def outer_mlp(layer):
        base = 1 + 6 * layer
        put_total(base + 5, tn(hidden[...].reshape(many, width), low[:, :, mine].reshape(many, cols)))
        put_total(base + 4, tn(n_two[...].reshape(many, width), pre_low[:, :, mine].reshape(many, cols)))

    def outer_mixed(layer):
        base = 1 + 6 * layer
        grad_mid = mid_low[:, :, mine].reshape(many, cols)
        put_total(
            base + 3,
            jnp.concatenate(
                [
                    tn(mixed[layer, :, 0].reshape(many, cols), grad_mid),
                    tn(mixed[layer, :, 1].reshape(many, cols), grad_mid),
                ],
                axis=0,
            ),
        )

    def outer_pair(layer):
        base = 1 + 6 * layer
        near = tn(n_own[layer].reshape(many, width), d_own[:, :, 0 : 3 * cols].reshape(many, 3 * cols))
        put_total(base, near[:, 0:cols])
        away = tn(n_prev[layer].reshape(many, width), d_own[:, :, 3 * cols : 5 * cols].reshape(many, 2 * cols))
        put_total(base + 1, near[:, cols : 2 * cols] + away[:, 0:cols])
        put_total(base + 2, near[:, 2 * cols : 3 * cols] + away[:, cols : 2 * cols])

    def encode_back(b):
        back = nn(g_col[...], state[last, b].astype(BF16)) * (1.0 / k_g)
        back = (back.astype(BF16).astype(F32) * silu_slope(pre_encode(rows_in, b))).astype(BF16)
        low[b] = back
        add_affine(8, column_sum(back.astype(F32)))
        back = jnp.zeros((rows, width), F32)
        for which in (1, 2):
            part = pl.ds((which + 2) * cols, cols)
            back = back + nt(d_own[b, :, part], w_cols(1 + which, mine))
            back = back + nt(d_far[b, :, part], w_cols(1 + which, theirs))
        gain = gain_row(0)
        hat, inv = norm_parts(start_prev[b].astype(F32))
        add_affine(0, column_sum(back * hat))
        back = nn(gp_col[...], norm_back(back, hat, inv, gain).astype(BF16)) * (1.0 / k_g)
        back = (back.astype(BF16).astype(F32) * silu_slope(pre_encode(rows_prev, b))).astype(BF16)
        mid_low[b] = back
        add_affine(8, column_sum(back.astype(F32)))

    each(encode, hooks=(None, lambda: gather_step(4)))
    gather_step(5)

    def first_project(b):
        project(0, b)

    each(first_project)
    gather_step(6)
    done = 7
    for layer in range(last):

        def attend_this(b, layer=layer):
            attend(layer, b)

        def take_first(b, layer=layer):
            take_prev(layer, b)

        def mlp_this(b, layer=layer):
            mlp(layer, b)

        def project_next(b, layer=layer):
            project(layer + 1, b)

        if layer > 0:
            each(take_first)
        staggered(
            attend_this,
            mlp_this,
            project_next,
            hooks=(None, lambda k=done: gather_step(k), lambda k=done + 1: gather_step(k)),
        )
        gather_step(done + 2)
        done = done + 3

    def ready_last():
        for step in range(done, len(sz.groups) + 3):
            gather_step(step)
        scalars[1] = tile_end(0) if sz.fused else jnp.broadcast_to(weight_ref[...], (8, 128))

    def take_last(b):
        take_prev(last, b)

    def attend_last(b):
        attend(last, b)

    def turn(b):
        mlp(last, b)
        decode(b)
        mlp_back(last, b)
        attend_back(last, b)

    def send_last(b):
        if last > 0:
            send_prev(last, b)

    staggered(take_last, attend_last, turn, send_last, hooks=(None, None, ready_last))
    outer_mlp(last)
    outer_mixed(last)
    summed(1, 2 * last + 2)
    outer_pair(last)
    summed(1, 2 * last + 1)
    for layer in reversed(range(last)):

        def take_this(b, layer=layer):
            take_next(layer + 1, b)

        def back_this(b, layer=layer):
            join(layer + 1, b)
            mlp_back(layer, b)

        def pair_this(b, layer=layer):
            attend_back(layer, b)

        def send_this(b, layer=layer):
            if layer > 0:
                send_prev(layer, b)

        u = 2 * layer
        staggered(
            take_this, back_this, hooks=(None, None, lambda u=u: summed(2, u + 4), lambda u=u: summed(2, u + 3))
        )
        outer_mlp(layer)
        outer_mixed(layer)
        summed(1, u + 2)
        summed(3, u + 4)
        hooks = (None, lambda u=u: summed(2, u + 2), lambda u=u: summed(3, u + 3))
        if layer > 0:
            staggered(pair_this, send_this, hooks=hooks)
        else:
            each(pair_this, hooks=hooks)
        outer_pair(layer)
        summed(1, u + 1)
        summed(4, u + 4)
        if layer > 0:
            summed(4, u + 3)

    def last_back(b):
        join(0, b)
        encode_back(b)

    each(last_back, hooks=(None, lambda: summed(3, 2)))
    wide = jnp.concatenate([affine_grad[...], jnp.zeros((112, width), F32)], axis=0)

    @pl.when(j == 0)
    def _():
        put_total(
            0,
            tn(low[...].reshape(many, width), rows_in[:, :, :, 0:256].reshape(many, 256))
            + tn(mid_low[...].reshape(many, width), rows_prev[...].reshape(many, 256)),
        )

    @pl.when(j == 1)
    def _():
        put_total(
            0,
            jnp.concatenate(
                [
                    jnp.transpose(wide),
                    tn(final[...].reshape(many, width), grad_pred[...].reshape(many, 128)),
                ],
                axis=1,
            ),
        )

    if sz.fused:
        reduce_one(0)
        if sz.layers > 1:
            reduce_four(3)
        reduce_two(1)
        reduce_two(0)
        reduce_four(2)
        reduce_three(1)
        reduce_three(0)
        for unit in range(2, len(sz.units)):
            reduce_done(unit)
        reduce_four(1)
        reduce_four(0)
        squares = jnp.sum(square_acc[...], axis=1, keepdims=True)
        sub = lax.broadcasted_iota(jnp.int32, (8, 128), 0)
        tile[1, 0] = jnp.where(sub == 0, squares, loss_acc[0:1, 0:1])
        tile_start(1)
        reduce_done(1)
        reduce_done(0)
        result = tile_end(1)
        scalars[0] = jnp.broadcast_to(result[1:2, :], (8, 128))
        scalars[2] = jnp.broadcast_to(jnp.sqrt(result[0:1, :]), (8, 128))
    else:
        scalars[0] = loss_acc[...]
        scalars[2] = loss_acc[...]

    for make in waits:
        make().wait_send()
    for layer in range(sz.layers):
        for b in range(nb):
            mix_copy(layer, b).wait_send()
            if layer > 0:
                n_copy(layer, b).wait_send()
                n_forward(layer, b, mine).wait_send()
                dn_copy(layer, b).wait_send()
                dn_forward(layer, b, mine).wait_send()


def dma(*shape):
    return pltpu.SemaphoreType.DMA(shape)


def train_kernel(sz, operands):
    nb, rows, half, width, cols = sz.batches, sz.rows, sz.half, sz.width, sz.cols
    layers = sz.layers
    scratch = []
    if sz.fused:
        out_shape = (
            jax.ShapeDtypeStruct((sz.mats, sz.shard, width), F32),
            jax.ShapeDtypeStruct((3, 8, 128), F32),
        )
        scratch += [
            pltpu.VMEM((sz.mats, sz.depth, 2, 2, 2, sz.shard, width), BF16),
            pltpu.VMEM((sz.mats, sz.depth, 2, 2, 2, sz.shard, cols), F32),
        ]
        scratch += [pltpu.VMEM(value.shape, value.dtype) for value in operands]
        scratch += [dma(len(operands))]
    else:
        out_shape = (
            jax.ShapeDtypeStruct((sz.mats, width, cols), F32),
            jax.ShapeDtypeStruct((3, 8, 128), F32),
        )
    scratch += [
        pltpu.VMEM((nb, half, 384), BF16),
        pltpu.VMEM((nb, 2, half, 384), BF16),
        pltpu.VMEM((nb, 2, half, 256), BF16),
        pltpu.VMEM((3, 32, rows), jnp.int32),
        pltpu.VMEM((nb, rows, width), BF16),
        pltpu.VMEM((nb, rows, width), BF16),
        pltpu.VMEM((layers, nb, rows, width), F32),
        pltpu.VMEM(((layers - 1) * nb + 1, rows, width), F32),
        pltpu.VMEM(((layers - 1) * nb + 1, rows, width), F32),
        pltpu.VMEM((layers, nb, 2, rows, cols), BF16),
        pltpu.VMEM((layers, nb, rows, cols), BF16),
        pltpu.VMEM((layers, nb, 2, 2 * rows, cols), BF16),
        pltpu.VMEM((layers, nb, sz.near, rows, 2 * rows), BF16),
        pltpu.VMEM((rows, 2 * rows), F32),
    ]
    scratch += [pltpu.VMEM((rows, rows), BF16)] * 6
    scratch += [pltpu.VMEM((16, width), F32)] * 2
    scratch += [
        pltpu.VMEM((nb, rows, width), BF16),
        pltpu.VMEM((nb, rows, 128), BF16),
        pltpu.VMEM((nb, rows, width), BF16),
        pltpu.VMEM((nb, rows, width), BF16),
        pltpu.VMEM((nb, rows, width), BF16),
        pltpu.VMEM((layers, nb, rows, width), BF16),
        pltpu.VMEM((layers, nb, rows, width), BF16),
        pltpu.VMEM((nb, rows, width), BF16),
        pltpu.VMEM((nb, rows, width), BF16),
        pltpu.VMEM((nb, rows, 5 * cols), BF16),
        pltpu.VMEM((nb, rows, 5 * cols), BF16),
        pltpu.VMEM((max(layers - 1, 1), nb, rows, cols), BF16),
        pltpu.VMEM((max(layers - 1, 1), nb, rows, width), BF16),
        pltpu.VMEM((8, 128), F32),
        pltpu.VMEM((1, cols), F32),
    ]
    scratch += [dma(3), dma(3), dma(2), dma(2), dma(2), dma(2)] + [dma(layers, nb)] * 12
    scratch += [pltpu.SemaphoreType.REGULAR]
    if sz.fused:
        depth, groups, units = sz.depth, len(sz.groups), len(sz.units)
        lane = cols // 2
        one_shape = (2, sz.mats, depth, 2, 2, sz.shard, lane)
        two_shape = (2, sz.mats, depth, 2, sz.shard, lane)
        scratch += [pltpu.VMEM(one_shape, jnp.int16)] * 2 + [pltpu.VMEM(two_shape, jnp.int16)] * 2
        scratch += [
            pltpu.VMEM((sz.mats, depth, 2, sz.shard, cols), jnp.int16),
            pltpu.VMEM((depth - 1, sz.mats, 2, sz.shard, cols), jnp.int16),
            pltpu.VMEM((sz.mats, sz.shard, cols), F32),
            pltpu.VMEM((2, 2, sz.mats, 8, lane), F32),
            pltpu.VMEM((2, 2, sz.mats, 8, lane), F32),
            pltpu.VMEM((sz.mats, 8, cols), F32),
            pltpu.VMEM((depth - 1, sz.mats, 8, cols), F32),
            pltpu.VMEM((2, 2, 8, 128), F32),
            pltpu.VMEM((2, 8, 128), F32),
            pltpu.VMEM((2, 4 * depth, 8, 128), F32),
        ]
        far = [dma(groups, depth - 1)] * 2
        scratch += far + [dma(groups, 2)] * 4 + [dma(groups)] * 2
        scratch += [dma(units, 4, 2)] * 2 + [dma(units, 2, depth - 1)] * 2 + [dma(units)] * 2
        scratch += [dma(2)] * 2 + [dma(2, 4 * depth - 1)] * 2
    return pl.pallas_call(
        functools.partial(step_kernel, sz),
        out_shape=out_shape,
        in_specs=[pl.BlockSpec(memory_space=pl.ANY if sz.fused else pltpu.VMEM)] * len(operands),
        out_specs=(pl.BlockSpec(memory_space=pltpu.VMEM),) * 2,
        scratch_shapes=scratch,
        compiler_params=pltpu.CompilerParams(
            collective_id=0, has_side_effects=True, vmem_limit_bytes=60 * 1024 * 1024
        ),
    )(*operands)


def adam(weight, first, second, grad):
    first_new = BETA_ONE * first + (1.0 - BETA_ONE) * grad
    second_new = BETA_TWO * second + (1.0 - BETA_TWO) * grad * grad
    first_hat = first_new / (1.0 - BETA_ONE**STEP)
    second_hat = second_new / (1.0 - BETA_TWO**STEP)
    weight_new = weight - RATE * (first_hat / (jnp.sqrt(second_hat) + ADAM_EPS) + DECAY * weight)
    return (weight_new, first_new, second_new, weight_new.astype(BF16))


def adam_kernel(sz, share, scalars, *refs):
    masters = refs[:15]
    outs = refs[15:35]
    for index, ref in enumerate(refs[35:38]):
        ref[...] = scalars[index, 0:1, 0:1]
    mat, inp, out, gain, bias = [masters[3 * k : 3 * k + 3] for k in range(5)]
    factor = jnp.minimum(1.0, CLIP / (scalars[2, 0:1, 0:1] + 1e-06))

    def put(k, values):
        for ref, value in zip(outs[4 * k : 4 * k + 4], values):
            ref[...] = value

    for index in range(sz.mats - 1):
        values = adam(mat[0][index], mat[1][index], mat[2][index], factor * share[1 + index])
        for ref, value in zip(outs[0:4], values):
            ref[index] = value
    last = share[0]
    put(1, adam(inp[0][...], inp[1][...], inp[2][...], factor * last[:, 0 : sz.c_in]))
    put(2, adam(out[0][...], out[1][...], out[2][...], factor * last[:, 384 : 384 + sz.c_out]))
    small = jnp.concatenate([last[:, 256:384], jnp.zeros((128 - sz.shard, 128), F32)], axis=0)
    small = jnp.transpose(small)[:, 0 : sz.shard]
    count = gain[0].shape[0]
    put(3, adam(gain[0][...], gain[1][...], gain[2][...], factor * small[0:count]))
    put(4, adam(bias[0][...], bias[1][...], bias[2][...], factor * small[8 : 8 + count]))


def update(sz, share, scalars, groups):
    operands = [share, scalars]
    out_shape = []
    for triple in groups:
        operands += list(triple)
        shape = triple[0].shape
        out_shape += [jax.ShapeDtypeStruct(shape, F32)] * 3 + [jax.ShapeDtypeStruct(shape, BF16)]
    out_shape += [jax.ShapeDtypeStruct((1, 1), F32)] * 3
    return pl.pallas_call(
        functools.partial(adam_kernel, sz),
        out_shape=tuple(out_shape),
        in_specs=[pl.BlockSpec(memory_space=pltpu.VMEM)] * len(operands),
        out_specs=(pl.BlockSpec(memory_space=pltpu.VMEM),) * len(out_shape),
    )(*operands)


def per_device(
    grid_in, targets, area, row_count, g2m, m2g, senders, edge_count,
    mat_w, mat_m, mat_v, in_w, in_m, in_v, out_w, out_m, out_v,
    gain_w, gain_m, gain_v, bias_w, bias_m, bias_v,
):
    axes = ("node", "feat")
    sz = Sizes(
        lax.axis_size("node"),
        lax.axis_size("feat"),
        grid_in.shape[0],
        grid_in.shape[1],
        mat_w.shape[2],
        mat_w.shape[0] // 6,
        HEADS,
        senders.shape[1],
        grid_in.shape[2],
        targets.shape[2],
    )
    operands = [
        jnp.swapaxes(grid_in, 1, 2),
        jnp.swapaxes(targets, 1, 2),
        area.reshape(1, -1),
        row_count.T,
        g2m.T,
        m2g.T,
        senders.T,
        edge_count.reshape(1, -1),
    ]
    if sz.fused:
        operands += [mat_w, in_w.T, out_w, gain_w, bias_w]
        share, scalars = train_kernel(sz, operands)
        groups = (
            (mat_w, mat_m, mat_v),
            (in_w.T, in_m.T, in_v.T),
            (out_w, out_m, out_v),
            (gain_w, gain_m, gain_v),
            (bias_w, bias_m, bias_v),
        )
        outs = list(update(sz, share, scalars, groups))
        for index in range(4, 8):
            outs[index] = outs[index].T
        for index in range(20, 23):
            outs[index] = outs[index].reshape(())
        return tuple(outs)

    width, shard = sz.width, sz.shard

    def pad(value, size):
        return jnp.pad(value, ((0, 0), (0, size - value.shape[1])))

    def pack(square, inp, out, gain, bias):
        small = jnp.concatenate([pad(gain.T, 8), pad(bias.T, 120)], axis=1)
        first = jnp.concatenate([pad(inp.T, 256), small, pad(out, 128)], axis=1)
        return jnp.concatenate([first[None], square], axis=0)

    packed = pack(mat_w, in_w, out_w, gain_w, bias_w).astype(BF16)
    full = lax.all_gather(packed, axes, axis=1, tiled=True).reshape(sz.mats, 2, width // 2, width)
    live = (jnp.arange(sz.half)[None, :] < row_count).astype(F32)
    weight_total = lax.psum(jnp.sum(area[None, :] * live) * targets.shape[2], axes)
    operands += [full, weight_total.reshape(1, 1)]
    part, scalars = train_kernel(sz, operands)
    feat = lax.axis_index("feat")
    spread = lax.dynamic_update_slice(
        jnp.zeros((sz.mats, width, width), F32), part, (0, 0, feat * sz.cols)
    )
    share = lax.psum_scatter(spread, axes, scatter_dimension=1, tiled=True)
    square_sum, loss_sum = lax.psum((jnp.sum(share * share), scalars[0, 0, 0]), axes)
    grad_norm = jnp.sqrt(square_sum)
    share = jnp.minimum(1.0, CLIP / (grad_norm + 1e-06)) * share
    count = gain_w.shape[0]
    last = share[0]
    outs = adam(mat_w, mat_m, mat_v, share[1:])
    outs += adam(in_w, in_m, in_v, last[:, 0 : sz.c_in].T)
    outs += adam(out_w, out_m, out_v, last[:, 384 : 384 + sz.c_out])
    outs += adam(gain_w, gain_m, gain_v, last[:, 256 : 256 + count].T)
    outs += adam(bias_w, bias_m, bias_v, last[:, 264 : 264 + count].T)
    return outs + (loss_sum, weight_total, grad_norm)


def solution(mesh):
    both = ("node", "feat")
    rows_three = P(None, both, None)
    second = P(None, both)
    first = P(both, None)
    placed = (
        rows_three, rows_three, P(both), second,
        P("node", None), P("node", None), P("node", None), P("node"),
    )
    placed += (rows_three,) * 3 + (second,) * 3 + (first,) * 3 + (second,) * 6
    outs = (rows_three,) * 4 + (second,) * 4 + (first,) * 4 + (second,) * 8 + (P(), P(), P())
    return jax.shard_map(per_device, mesh=mesh, in_specs=placed, out_specs=outs, check_vma=False)
```

```python
import functools

import jax
import jax.numpy as jnp
from jax import lax
from jax.experimental import pallas as pl
from jax.experimental.pallas import tpu as pltpu
from jax.sharding import PartitionSpec as P

HEADS = 8
STEP = 5
NORM_EPS = 1e-05
CLIP = 0.05
RATE = 0.02
BETA_ONE = 0.5
BETA_TWO = 0.5
DECAY = 0.01
ADAM_EPS = 1e-08
DEAD = -1e30
MESH = pl.DeviceIdType.MESH
F32 = jnp.float32
BF16 = jnp.bfloat16


def nn(left, right):
    return jnp.dot(left, right, preferred_element_type=F32)


def nt(left, right):
    return lax.dot_general(left, right, (((1,), (1,)), ((), ())), preferred_element_type=F32)


def tn(left, right):
    return lax.dot_general(left, right, (((0,), (0,)), ((), ())), preferred_element_type=F32)


def norm_parts(state):
    centre = state - jnp.mean(state, axis=-1, keepdims=True)
    spread = jnp.mean(centre * centre, axis=-1, keepdims=True)
    scale = lax.rsqrt(spread + NORM_EPS)
    return centre * scale, scale


def norm_back(grad, hat, scale, gain):
    inner = grad * gain
    mean_inner = jnp.mean(inner, axis=-1, keepdims=True)
    mean_hat = jnp.mean(inner * hat, axis=-1, keepdims=True)
    return scale * (inner - mean_inner - hat * mean_hat)


def column_sum(value):
    return jnp.sum(value, axis=0, keepdims=True)


def sigmoid(value):
    return 0.5 * jnp.tanh(0.5 * value) + 0.5


def silu_slope(value):
    gate = sigmoid(value)
    return gate * (1.0 + value * (1.0 - gate))


class Sizes:
    def __init__(self, node, feat, batches, half, width, layers, heads, slots, c_in, c_out):
        self.node, self.feat = node, feat
        self.batches, self.half, self.width = batches, half, width
        self.rows = 2 * half
        self.layers, self.heads, self.slots = layers, heads, slots
        self.c_in, self.c_out = c_in, c_out
        self.shard = width // (node * feat)
        self.depth = node // 4
        self.mats = 6 * layers + 1
        self.cols = width // feat
        self.near = heads // feat
        self.fused = self.shard % 16 == 0 and node % 4 == 0
        self.groups = [(0, 1)] + [(first, 2) for first in range(1, self.mats, 2)]
        self.units = [(0, 1)]
        for layer in range(layers):
            self.units += [(1 + 6 * layer, 3), (4 + 6 * layer, 3)]


def step_kernel(sz, *refs):
    refs = list(refs)

    def take(count):
        out = refs[:count]
        del refs[:count]
        return out

    grid_ref, target_ref, area_ref, count_ref, g2m_ref, m2g_ref, send_ref, edge_ref = take(8)
    if sz.fused:
        mat_ref, in_ref, out_ref, gain_ref, bias_ref = take(5)
        share, scalars = take(2)
        full, total = take(2)
        held = take(13)
        (in_sems,) = take(1)
        incoming = [
            pltpu.make_async_copy(src, dst, in_sems.at[k])
            for k, (src, dst) in enumerate(
                zip(
                    (grid_ref, target_ref, area_ref, count_ref, g2m_ref, m2g_ref, send_ref, edge_ref)
                    + (mat_ref, in_ref, out_ref, gain_ref, bias_ref),
                    held,
                )
            )
        ]
        grid_ref, target_ref, area_ref, count_ref, g2m_ref, m2g_ref, send_ref, edge_ref = held[:8]
        mat_ref, in_ref, out_ref, gain_ref, bias_ref = held[8:]
    else:
        full, weight_ref = take(2)
        total, scalars = take(2)
    (
        rows_own,
        rows_in,
        rows_prev,
        indices,
        start,
        start_prev,
        state,
        middle,
        pre_mlp,
        mixed,
        query,
        pair,
        prob,
        edge_bias,
        g_row,
        g_col,
        gp_row,
        gp_col,
        m_row,
        m_col,
        affine,
        affine_grad,
        final,
        grad_pred,
        low,
        pre_low,
        mid_low,
        n_own,
        n_prev,
        n_two,
        hidden,
        d_own,
        d_far,
        dn_out,
        dn_in,
        loss_acc,
        square_acc,
    ) = take(37)
    (s_rows, r_rows, s_idx, r_idx, s_prev, r_prev) = take(6)
    (s_n, r_n, s_nf, r_nf, s_mix, r_mix, s_dn, r_dn, s_df, r_df, s_far, r_far) = take(12)
    (far_free,) = take(1)
    if sz.fused:
        (code_one, got_one, code_two, got_two, code_z, got_z, got_c) = take(7)
        (size_out, size_in, size_z, size_z_in, tile, tile_far, tile_all) = take(7)
        (gz_s, gz_r, g2_s, g2_r, g3_s, g3_r, g4_s, g4_r) = take(8)
        (rr_s, rr_r, rz_s, rz_r, rc_s, rc_r) = take(6)
        (t_s, t_r, tz_s, tz_r) = take(4)

    nb, rows, half, width, cols = sz.batches, sz.rows, sz.half, sz.width, sz.cols
    node = lax.axis_index("node")
    y = lax.axis_index("feat")
    waits = []
    if sz.fused:
        depth = sz.depth
        c = lax.rem(node, 2)
        x = lax.rem(node // 2, 2)
        z = node // 4
        j = c

        def device_of(zz, xx, cc, yy):
            return (zz * 4 + xx * 2 + cc, yy)

        def holder(block):
            return device_of(block // 4, lax.rem(block // 2, 2), c, lax.rem(block, 2))

        block = z * 4 + x * 2 + y
        after = holder(lax.rem(block + 1, sz.node))
        before = holder(lax.rem(block + sz.node - 1, sz.node))
        partner = device_of(z, x, 1 - c, y)
        x_dev = device_of(z, 1 - x, c, y)
        y_dev = device_of(z, x, c, 1 - y)
        z_devs = [device_of(lax.rem(z + step, depth), x, c, y) for step in range(1, depth)]

        def chip_at(dz, dx, dy):
            return device_of(lax.rem(z + dz, depth), lax.rem(x + dx, 2), c, lax.rem(y + dy, 2))

        offsets = [(k // 4, (k // 2) % 2, k % 2) for k in range(1, 4 * depth)]
        greet = [after, before, partner] + [chip_at(*offset) for offset in offsets]
    else:
        j = y
        after = (lax.rem(node + 1, sz.node), j)
        before = (lax.rem(node + sz.node - 1, sz.node), j)
        partner = (node, 1 - j)
        greet = [after, before, partner]
    other = 1 - j
    mine = pl.ds(pl.multiple_of(j * cols, cols), cols)
    theirs = pl.ds(pl.multiple_of(other * cols, cols), cols)

    def remote(src, dst, s_sem, r_sem, device):
        return pltpu.make_async_remote_copy(
            src_ref=src, dst_ref=dst, send_sem=s_sem, recv_sem=r_sem, device_id=device, device_id_type=MESH
        )

    def push(make):
        make().start()
        waits.append(make)

    barrier = pltpu.get_barrier_semaphore()
    for device in greet:
        pl.semaphore_signal(barrier, inc=1, device_id=device, device_id_type=MESH)
    if sz.fused:
        for copy in incoming:
            copy.start()
        for copy in incoming:
            copy.wait()

    lanes_c = lax.broadcasted_iota(jnp.int32, (1, cols), 1) // (width // sz.heads)
    mask_low = [(lanes_c == head).astype(F32).astype(BF16) for head in range(sz.near)]
    mask_full = [(lanes_c == head).astype(F32) for head in range(sz.near)]

    def w_full(index):
        return full[index].reshape(width, width)

    def w_cols(index, which):
        if sz.fused:
            return full[index, :, :, :, :, :, which].reshape(width, cols)
        return full[index, :, :, which].reshape(width, cols)

    def w_rows(index, which):
        if sz.fused:
            count = sz.depth // 2
            return full[index, pl.ds(which * count, count)].reshape(width // 2, width)
        return full[index, which]

    def w_block(index, rows_half, which):
        if sz.fused:
            count = sz.depth // 2
            return full[index, pl.ds(rows_half * count, count), :, :, :, :, which].reshape(width // 2, cols)
        return full[index, rows_half, :, which]

    def put_total(index, value):
        total[index] = value.reshape(total.shape[1:])

    cell = lax.broadcasted_iota(jnp.int32, (1, half), 1)
    for b in range(nb):
        block_in = jnp.concatenate([grid_ref[b].astype(F32), jnp.zeros((256 - sz.c_in, half), F32)], axis=0)
        rows_own[b, :, 0:256] = jnp.transpose(block_in).astype(BF16)
        weight = jnp.where(cell < count_ref[0:1, b : b + 1], area_ref[...], 0.0)
        first = weight.astype(BF16).astype(F32)
        second = (weight - first).astype(BF16).astype(F32)
        third = weight - first - second
        block_in = jnp.concatenate(
            [target_ref[b].astype(F32), jnp.zeros((125 - sz.c_out, half), F32), first, second, third], axis=0
        )
        rows_own[b, :, 256:384] = jnp.transpose(block_in).astype(BF16)
    slot = c if sz.fused else 0
    k_g = g2m_ref.shape[0]
    k_m = m2g_ref.shape[0]
    receiver = lax.broadcasted_iota(jnp.int32, (1, rows), 1)
    indices[slot, 0:k_g] = g2m_ref[...]
    indices[slot, 8 : 8 + k_m] = m2g_ref[...]
    indices[slot, 15:16] = jnp.where(receiver < rows // 2, edge_ref[0:1, 0:1], edge_ref[0:1, 1:2])
    indices[slot, 16 : 16 + sz.slots] = send_ref[...]
    if sz.fused:
        n_groups = len(sz.groups)
        packed = jnp.concatenate(
            [
                in_ref[...],
                jnp.zeros((sz.shard, 256 - sz.c_in), F32),
                jnp.zeros((sz.shard, 128), F32),
                out_ref[...],
                jnp.zeros((sz.shard, 128 - sz.c_out), F32),
            ],
            axis=1,
        )
        small = jnp.concatenate(
            [
                gain_ref[...],
                jnp.zeros((3, sz.shard), F32),
                bias_ref[...],
                jnp.zeros((3, sz.shard), F32),
            ],
            axis=0,
        )
        small = jnp.concatenate([small, jnp.zeros((16, 128 - sz.shard), F32)], axis=1)
        small = jnp.concatenate([small, jnp.zeros((112, 128), F32)], axis=0)
        small = jnp.transpose(small)[0 : sz.shard, :]
        full[0, z, x, c, y] = jnp.concatenate([packed[:, 0:256], small, packed[:, 384:512]], axis=1).astype(BF16)
        for index in range(sz.mats - 1):
            full[1 + index, z, x, c, y] = mat_ref[index].astype(BF16)

    pl.semaphore_wait(barrier, len(greet))

    here = rows_in.at[:, y]
    there = rows_in.at[:, 1 - y]
    if sz.fused:
        push(lambda: remote(indices.at[c], indices.at[c], s_idx.at[0], r_idx.at[0], partner))
        to_partner = remote(rows_own, here, s_rows.at[0], r_rows.at[0], partner)
        to_chip = remote(rows_own, here, s_rows.at[1], r_rows.at[1], y_dev)
        forward = remote(there, there, s_rows.at[2], r_rows.at[1], partner)

        @pl.when(c == y)
        def _():
            to_partner.start()
            rows_in[:, y] = rows_own[...]

        @pl.when(c != y)
        def _():
            to_chip.start()

    else:
        push(lambda: remote(rows_own, here, s_rows.at[0], r_rows.at[0], partner))
        rows_in[:, y] = rows_own[...]

    if sz.fused:

        def gather_one(g):
            first, count = sz.groups[g]
            for step in range(1, depth):

                def make(g=g, first=first, count=count, step=step):
                    own = full.at[pl.ds(first, count), z, x, c, y]
                    return remote(own, own, gz_s.at[g, step - 1], gz_r.at[g, step - 1], z_devs[step - 1])

                push(make)

        gather_one(0)
        gather_one(1)

    if sz.fused:
        weight_sum = jnp.zeros((1, 1), F32)
        for b in range(nb):
            weight = jnp.where(cell < count_ref[0:1, b : b + 1], area_ref[...], 0.0)
            weight_sum = weight_sum + jnp.sum(weight, axis=1, keepdims=True)
        tile[0, 0] = jnp.broadcast_to(weight_sum * float(sz.c_out), (8, 128))

        def tile_core(slot):
            return remote(tile.at[slot, 0], tile_far.at[slot], t_s.at[slot], t_r.at[slot], partner)

        def tile_chip(slot, k, place):
            return remote(
                tile.at[slot, 1], tile_all.at[slot, place], tz_s.at[slot, k], tz_r.at[slot, k], chip_at(*offsets[k])
            )

        def tile_start(slot):
            tile_core(slot).start()
            tile_core(slot).wait()
            tile[slot, 1] = tile[slot, 0] + tile_far[slot]
            spot = z * 4 + x * 2 + y
            tile_all[slot, spot] = tile[slot, 1]
            for k in range(len(offsets)):
                tile_chip(slot, k, spot).start()

        def tile_end(slot):
            for k, (dz, dx, dy) in enumerate(offsets):
                source = (
                    lax.rem(z + depth - dz, depth) * 4 + lax.rem(x + 2 - dx, 2) * 2 + lax.rem(y + 2 - dy, 2)
                )
                tile_chip(slot, k, source).wait()
            result = tile_all[slot, 0]
            for index in range(1, 4 * depth):
                result = result + tile_all[slot, index]
            return result

        tile_start(0)

    if sz.fused:
        remote(indices.at[1 - c], indices.at[1 - c], s_idx.at[0], r_idx.at[0], partner).wait_recv()
        slot = y
    push(lambda: remote(indices.at[slot], indices.at[2], s_idx.at[1], r_idx.at[1], after))

    affine_grad[...] = jnp.zeros_like(affine_grad)
    loss_acc[...] = jnp.zeros_like(loss_acc)
    square_acc[...] = jnp.zeros_like(square_acc)

    if sz.fused:
        side_a = pl.ds(0, width // 2)
        side_b = pl.ds(width // 2, width // 2)

        def gather_part(g, stage, which):
            span = pl.ds(*sz.groups[g])
            if stage == 2:
                return full.at[span, :, x, c, y, :, which]
            if which is side_a:
                return full.at[span, :, :, c, y, :, which]
            return full.at[span, :, x, c, :, :, which]

        def gather_push(g, stage, side, sems, device):
            which = (side_a, side_b)[side]

            def make():
                part = gather_part(g, stage, which)
                return remote(part, part, sems[0].at[g, side], sems[1].at[g, side], device)

            push(make)

        def arrived(part, s_sem, r_sem, device):
            remote(part, part, s_sem, r_sem, device).wait_recv()

        def gather_two(g):
            span = pl.ds(*sz.groups[g])
            for step in range(1, depth):
                there = full.at[span, lax.rem(z + depth - step, depth), x, c, y]
                arrived(there, gz_s.at[g, step - 1], gz_r.at[g, step - 1], z_devs[step - 1])
            gather_push(g, 2, 0, (g2_s, g2_r), x_dev)
            gather_push(g, 2, 1, (g2_s, g2_r), y_dev)

        def gather_three(g):
            span = pl.ds(*sz.groups[g])
            arrived(full.at[span, :, 1 - x, c, y, :, side_a], g2_s.at[g, 0], g2_r.at[g, 0], x_dev)
            gather_push(g, 3, 0, (g3_s, g3_r), y_dev)
            arrived(full.at[span, :, x, c, 1 - y, :, side_b], g2_s.at[g, 1], g2_r.at[g, 1], y_dev)
            gather_push(g, 3, 1, (g3_s, g3_r), x_dev)

        def gather_four(g):
            span = pl.ds(*sz.groups[g])
            arrived(full.at[span, :, :, c, 1 - y, :, side_a], g3_s.at[g, 0], g3_r.at[g, 0], y_dev)
            arrived(full.at[span, :, 1 - x, c, :, :, side_b], g3_s.at[g, 1], g3_r.at[g, 1], x_dev)

            def make():
                part = full.at[span, :, :, c]
                return remote(part, part, g4_s.at[g], g4_r.at[g], partner)

            push(make)

        def gather_done(g):
            span = pl.ds(*sz.groups[g])
            arrived(full.at[span, :, :, 1 - c], g4_s.at[g], g4_r.at[g], partner)

    def gather_step(step):
        if not sz.fused:
            return
        for stage, move in enumerate((gather_two, gather_three, gather_four, gather_done)):
            if 0 <= step - stage < len(sz.groups):
                move(step - stage)
        if 2 <= step + 2 < len(sz.groups):
            gather_one(step + 2)

    in_cols = pl.ds(0, 256)
    small_cols = pl.ds(256, 128)
    out_cols = pl.ds(384, 128)

    def aux(which, size):
        if sz.fused:
            return full[0, :, :, :, :, :, which].reshape(width, size)
        return full[0, :, :, which].reshape(width, size)

    gather_step(0)
    if sz.fused:

        @pl.when(c == y)
        def _():
            remote(there, there, s_rows.at[1], r_rows.at[1], y_dev).wait_recv()
            forward.start()
            to_partner.wait_send()
            forward.wait_send()

        @pl.when(c != y)
        def _():
            to_chip.wait_send()
            remote(here, here, s_rows.at[0], r_rows.at[0], partner).wait_recv()
            remote(there, there, s_rows.at[2], r_rows.at[1], partner).wait_recv()

    else:
        remote(there, there, s_rows.at[0], r_rows.at[0], partner).wait_recv()

    push(lambda: remote(rows_in.at[:, j, :, 0:256], rows_prev.at[:, j], s_prev.at[0], r_prev.at[0], after))

    gather_step(1)
    def counts(place, first, slots, origin, live=None):
        wide = lax.broadcasted_iota(jnp.int32, (rows, rows), 0) + origin
        acc = jnp.zeros((rows, rows), F32)
        for k in range(slots):
            hit = wide == indices[place, first + k : first + k + 1, :]
            if live is not None:
                hit = jnp.logical_and(hit, live > k)
            acc = acc + jnp.where(hit, 1.0, 0.0)
        return acc

    live = indices[slot, 15:16, :]
    for part in range(2):
        acc = jnp.transpose(counts(slot, 16, sz.slots, part * rows, live))
        edge_bias[:, part * rows : (part + 1) * rows] = jnp.where(acc > 0.5, jnp.log(jnp.maximum(acc, 1.0)), DEAD)
    table = counts(slot, 0, k_g, 0)
    g_col[...] = table.astype(BF16)
    g_row[...] = jnp.transpose(table).astype(BF16)
    table = counts(slot, 8, k_m, 0)
    m_col[...] = table.astype(BF16)
    m_row[...] = jnp.transpose(table).astype(BF16)
    gather_step(2)
    remote(rows_prev.at[:, j], rows_prev.at[:, j], s_prev.at[0], r_prev.at[0], after).wait_recv()
    push(lambda: remote(rows_prev.at[:, j], rows_prev.at[:, j], s_prev.at[1], r_prev.at[1], partner))
    remote(indices.at[slot], indices.at[2], s_idx.at[1], r_idx.at[1], after).wait_recv()
    table = counts(2, 0, k_g, 0)
    gp_col[...] = table.astype(BF16)
    gp_row[...] = jnp.transpose(table).astype(BF16)
    gather_step(3)
    remote(rows_prev.at[:, other], rows_prev.at[:, other], s_prev.at[1], r_prev.at[1], partner).wait_recv()

    affine[...] = jnp.transpose(aux(small_cols, 128).astype(F32))[0:16, :]

    def gain_row(index):
        return affine[pl.ds(index, 1), :]

    def bias_row(index):
        return affine[pl.ds(8 + index, 1), :]

    def add_affine(index, value):
        affine_grad[pl.ds(index, 1), :] = affine_grad[pl.ds(index, 1), :] + value

    def staggered(*bodies, hooks=()):
        def wrapped(t, carry):
            for step, hook in enumerate(hooks):
                if hook is not None:
                    pl.when(t == step)(hook)
            for late in reversed(range(len(bodies))):

                @pl.when(jnp.logical_and(t >= late, t < nb + late))
                def _(late=late):
                    bodies[late](t - late)

            return carry

        lax.fori_loop(0, nb + len(bodies) - 1, wrapped, 0)

    def each(body, hooks=()):
        def wrapped(b, carry):
            for step, hook in enumerate(hooks):
                if hook is not None:
                    pl.when(b == step)(hook)
            body(b)
            return carry

        lax.fori_loop(0, nb, wrapped, 0)

    def pre_encode(ref, b):
        return nt(ref[b, :, :, 0:256].reshape(rows, 256), aux(in_cols, 256)) + bias_row(0)

    def encode(b):
        gain = gain_row(0)
        for ref, table, keep, normed in (
            (rows_in, g_row, start, n_own),
            (rows_prev, gp_row, start_prev, n_prev),
        ):
            pre = pre_encode(ref, b)
            enc = (pre * sigmoid(pre)).astype(BF16)
            first = (nn(table[...], enc) * (1.0 / k_g)).astype(BF16)
            keep[b] = first
            hat, _ = norm_parts(first.astype(F32))
            normed[0, b] = (hat * gain).astype(BF16)

    def n_copy(layer, b):
        return remote(
            n_own.at[layer, b, :, mine], n_prev.at[layer, b, :, mine], s_n.at[layer, b], r_n.at[layer, b], after
        )

    def n_forward(layer, b, which):
        there = n_prev.at[layer, b, :, which]
        return remote(there, there, s_nf.at[layer, b], r_nf.at[layer, b], partner)

    def mix_copy(layer, b):
        return remote(
            mixed.at[layer, b, j], mixed.at[layer, b, j], s_mix.at[layer, b], r_mix.at[layer, b], partner
        )

    def mix_wait(layer, b):
        there = mixed.at[layer, b, other]
        remote(there, there, s_mix.at[layer, b], r_mix.at[layer, b], partner).wait_recv()

    scale = float(width // sz.heads) ** -0.5

    def spot(layer, b):
        return layer * nb + (b if layer < sz.layers - 1 else 0)

    def entry(layer, b):
        if layer == 0:
            return start[b].astype(F32)
        return state[layer - 1, b]

    def project(layer, b):
        base = 1 + 6 * layer
        if layer > 0:
            hat, _ = norm_parts(state[layer - 1, b])
            n_own[layer, b] = (hat * gain_row(2 * layer)).astype(BF16)
            n_copy(layer, b).start()
        normed = n_own[layer, b]
        query[layer, b] = nn(normed, w_cols(base, mine)).astype(BF16)
        pair[layer, b, 0, 0:rows] = nn(normed, w_cols(base + 1, mine)).astype(BF16)
        pair[layer, b, 1, 0:rows] = nn(normed, w_cols(base + 2, mine)).astype(BF16)

    def take_prev(layer, b):
        if layer > 0:
            n_copy(layer, b).wait_recv()
            n_forward(layer, b, mine).start()

    def attend(layer, b):
        base = 1 + 6 * layer
        if layer > 0:
            n_forward(layer, b, theirs).wait_recv()
        normed = n_prev[layer, b]
        pair[layer, b, 0, rows : 2 * rows] = nn(normed, w_cols(base + 1, mine)).astype(BF16)
        pair[layer, b, 1, rows : 2 * rows] = nn(normed, w_cols(base + 2, mine)).astype(BF16)
        keys, values, queries = pair[layer, b, 0], pair[layer, b, 1], query[layer, b]
        out = jnp.zeros((rows, cols), F32)
        for head in range(sz.near):
            score = nt(queries * mask_low[head], keys) * scale + edge_bias[...]
            expo = jnp.exp(score - jnp.max(score, axis=-1, keepdims=True))
            weight = (expo * (1.0 / jnp.sum(expo, axis=-1, keepdims=True))).astype(BF16)
            prob[spot(layer, b), head] = weight
            out = out + nn(weight, values) * mask_full[head]
        mixed[layer, b, j] = out.astype(BF16)
        mix_copy(layer, b).start()

    def mlp(layer, b):
        base = 1 + 6 * layer
        mix_wait(layer, b)
        mid = (
            entry(layer, b)
            + nn(mixed[layer, b, 0], w_rows(base + 3, 0))
            + nn(mixed[layer, b, 1], w_rows(base + 3, 1))
        )
        middle[spot(layer, b)] = mid
        hat, _ = norm_parts(mid)
        normed = (hat * gain_row(2 * layer + 1)).astype(BF16)
        pre = nn(normed, w_full(base + 4)) + bias_row(1 + 2 * layer)
        pre_mlp[spot(layer, b)] = pre
        act = (pre * sigmoid(pre)).astype(BF16)
        state[layer, b] = mid + nn(act, w_full(base + 5)) + bias_row(2 + 2 * layer)

    last = sz.layers - 1
    lane_out = lax.broadcasted_iota(jnp.int32, (1, 128), 1)
    row_index = lax.broadcasted_iota(jnp.int32, (rows, 1), 0)
    own_row = jnp.logical_and(row_index >= j * half, row_index < (j + 1) * half).astype(F32)
    real_lane = (lane_out < sz.c_out).astype(F32)

    def decode(b):
        gain = gain_row(2 * sz.layers)
        dec = (nn(m_row[...], state[last, b].astype(BF16)) * (1.0 / k_m)).astype(BF16).astype(F32)
        hat, inv = norm_parts(dec)
        normed = (hat * gain).astype(BF16)
        final[b] = normed
        weights = aux(out_cols, 128)
        goal = rows_in[b, :, :, 256:384].reshape(rows, 128).astype(F32)
        error = (nn(normed, weights) - goal) * real_lane
        weight = goal[:, 125:126] + goal[:, 126:127] + goal[:, 127:128]
        loss_acc[...] = loss_acc[...] + jnp.sum(
            jnp.sum((weight * own_row) * error * error, axis=1, keepdims=True), axis=0, keepdims=True
        )
        pred_low = (2.0 * weight * error / scalars[1, 0:1, 0:1]).astype(BF16)
        grad_pred[b] = pred_low
        back = nt(pred_low, weights)
        add_affine(2 * sz.layers, column_sum(back * hat))
        dec_low = norm_back(back, hat, inv, gain).astype(BF16)
        state[last, b] = (nn(m_col[...], dec_low) * (1.0 / k_m)).astype(BF16).astype(F32)

    if sz.fused:
        lane_a = pl.ds(0, cols // 2)
        lane_b = pl.ds(cols // 2, cols // 2)
        lanes = (lane_a, lane_b)
        top = 32767.0

        def encoded(value, code_ref, scale_ref):
            size = jnp.max(jnp.abs(value), axis=tuple(range(value.ndim - 1)), keepdims=True)
            size = size.reshape(1, size.shape[-1])
            inverse = jnp.where(size > 1e-30, top / jnp.maximum(size, 1e-30), 0.0)
            code_ref[...] = jnp.round(value * inverse).astype(jnp.int32).astype(jnp.int16)
            scale_ref[...] = jnp.broadcast_to(size * (1.0 / top), scale_ref.shape)

        def decoded(code, scale_row):
            return code.astype(jnp.int32).astype(F32) * scale_row

        def over(unit, body):
            first, count = sz.units[unit]

            def wrapped(m, carry):
                body(m)
                return carry

            lax.fori_loop(first, first + count, wrapped, 0)

        def send_codes(unit, stage, side, device):
            span = pl.ds(*sz.units[unit])
            codes_out, codes_in = ((code_one, got_one), (code_two, got_two))[stage]

            def make_codes():
                k = 2 * stage
                return remote(
                    codes_out.at[side, span], codes_in.at[side, span], rr_s.at[unit, k, side], rr_r.at[unit, k, side], device
                )

            def make_scales():
                k = 2 * stage + 1
                return remote(
                    size_out.at[stage, side, span],
                    size_in.at[stage, side, span],
                    rr_s.at[unit, k, side],
                    rr_r.at[unit, k, side],
                    device,
                )

            return make_codes, make_scales

        def reduce_one(unit):
            def body(m):
                encoded(total[m, :, 1 - x, :, :, :, lane_a], code_one.at[0, m], size_out.at[0, 0, m])
                encoded(total[m, :, :, :, 1 - y, :, lane_b], code_one.at[1, m], size_out.at[0, 1, m])

            over(unit, body)
            for side, device in ((0, x_dev), (1, y_dev)):
                for make in send_codes(unit, 0, side, device):
                    push(make)

        def reduce_two(unit):
            for side, device in ((0, x_dev), (1, y_dev)):
                for make in send_codes(unit, 0, side, device):
                    make().wait_recv()

            def body(m):
                row_a = size_in[0, 0, m, 0:1, :]
                row_b = size_in[0, 1, m, 0:1, :]
                total[m, :, x, :, :, :, lane_a] = total[m, :, x, :, :, :, lane_a] + decoded(got_one[0, m], row_a)
                total[m, :, :, :, y, :, lane_b] = total[m, :, :, :, y, :, lane_b] + decoded(got_one[1, m], row_b)
                encoded(total[m, :, x, :, 1 - y, :, lane_a], code_two.at[0, m], size_out.at[1, 0, m])
                encoded(total[m, :, 1 - x, :, y, :, lane_b], code_two.at[1, m], size_out.at[1, 1, m])

            over(unit, body)
            for side, device in ((0, y_dev), (1, x_dev)):
                for make in send_codes(unit, 1, side, device):
                    push(make)

        def send_z(unit, step):
            span = pl.ds(*sz.units[unit])

            def make_codes():
                return remote(
                    code_z.at[span, lax.rem(z + step, depth)],
                    got_z.at[step - 1, span],
                    rz_s.at[unit, 0, step - 1],
                    rz_r.at[unit, 0, step - 1],
                    z_devs[step - 1],
                )

            def make_scales():
                return remote(
                    size_z.at[span],
                    size_z_in.at[step - 1, span],
                    rz_s.at[unit, 1, step - 1],
                    rz_r.at[unit, 1, step - 1],
                    z_devs[step - 1],
                )

            return make_codes, make_scales

        def reduce_three(unit):
            for side, device in ((0, y_dev), (1, x_dev)):
                for make in send_codes(unit, 1, side, device):
                    make().wait_recv()

            def body(m):
                for side in range(2):
                    row = size_in[1, side, m, 0:1, :]
                    total[m, :, x, :, y, :, lanes[side]] = total[m, :, x, :, y, :, lanes[side]] + decoded(
                        got_two[side, m], row
                    )
                encoded(total[m, :, x, :, y], code_z.at[m], size_z.at[m])

            over(unit, body)
            for step in range(1, depth):
                for make in send_z(unit, step):
                    push(make)

        def core_copy(unit):
            span = pl.ds(*sz.units[unit])
            return remote(total.at[span, z, x, 1 - c, y], got_c.at[span], rc_s.at[unit], rc_r.at[unit], partner)

        def reduce_four(unit):
            for step in range(1, depth):
                for make in send_z(unit, step):
                    make().wait_recv()

            def body(m):
                acc = total[m, z, x, :, y]
                for step in range(1, depth):
                    acc = acc + decoded(got_z[step - 1, m], size_z_in[step - 1, m, 0:1, :])
                total[m, z, x, :, y] = acc
                square_acc[...] = square_acc[...] + jnp.sum(acc * acc, axis=(0, 1)).reshape(1, cols)

            over(unit, body)
            push(lambda: core_copy(unit))

        def reduce_done(unit):
            core_copy(unit).wait_recv()

            def body(m):
                share[m, :, mine] = total[m, z, x, c, y]
                share[m, :, theirs] = got_c[m]

            over(unit, body)

        stages = (None, reduce_one, reduce_two, reduce_three, reduce_four, reduce_done)

    def summed(stage, unit):
        if sz.fused:
            stages[stage](unit)

    def far_copy(layer, b):
        return remote(d_own.at[b], d_far.at[b], s_far.at[layer, b], r_far.at[layer, b], partner)

    def dn_copy(layer, b):
        return remote(
            dn_out.at[layer - 1, b],
            dn_in.at[layer - 1, b, :, mine],
            s_dn.at[layer, b],
            r_dn.at[layer, b],
            before,
        )

    def dn_forward(layer, b, which):
        there = dn_in.at[layer - 1, b, :, which]
        return remote(there, there, s_df.at[layer, b], r_df.at[layer, b], partner)

    def mlp_back(layer, b):
        base = 1 + 6 * layer
        grad = state[last, b]
        grad_low = grad.astype(BF16)
        low[b] = grad_low
        add_affine(8 + 2 + 2 * layer, column_sum(grad))
        pre = pre_mlp[spot(layer, b)]
        gate = sigmoid(pre)
        hidden[b] = (pre * gate).astype(BF16)
        back = (nt(grad_low, w_full(base + 5)) * (gate * (1.0 + pre * (1.0 - gate)))).astype(BF16)
        pre_low[b] = back
        add_affine(8 + 1 + 2 * layer, column_sum(back.astype(F32)))
        back = nt(back, w_full(base + 4))
        gain = gain_row(2 * layer + 1)
        hat, inv = norm_parts(middle[spot(layer, b)])
        n_two[b] = (hat * gain).astype(BF16)
        add_affine(2 * layer + 1, column_sum(back * hat))
        grad = grad + norm_back(back, hat, inv, gain)
        state[last, b] = grad
        mid_low[b] = grad.astype(BF16)

    def attend_back(layer, b):
        base = 1 + 6 * layer
        grad_out = nt(mid_low[b], w_rows(base + 3, j)).astype(BF16)
        keys, values, queries = pair[layer, b, 0], pair[layer, b, 1], query[layer, b]
        d_query = jnp.zeros((rows, cols), F32)
        scores = []
        out_heads = jnp.concatenate([grad_out * mask for mask in mask_low], axis=0)
        query_heads = jnp.concatenate([queries * mask for mask in mask_low], axis=0)
        for head in range(sz.near):
            weight_low = prob[spot(layer, b), head]
            out_head = out_heads[head * rows : (head + 1) * rows]
            weight = weight_low.astype(F32)
            part = weight * nt(out_head, values)
            score = (part - weight * jnp.sum(part, axis=-1, keepdims=True)).astype(BF16)
            d_query = d_query + nn(score, keys) * mask_full[head]
            scores.append(score)
        d_keys = tn(jnp.concatenate(scores, axis=0), query_heads)
        d_values = tn(prob[spot(layer, b)].reshape(sz.near * rows, 2 * rows), out_heads)
        d_keys = (d_keys * scale).astype(BF16)
        d_values = d_values.astype(BF16)
        d_own[b, :, 0:cols] = (d_query * scale).astype(BF16)
        d_own[b, :, cols : 2 * cols] = d_keys[0:rows]
        d_own[b, :, 2 * cols : 3 * cols] = d_values[0:rows]
        d_own[b, :, 3 * cols : 4 * cols] = d_keys[rows:]
        d_own[b, :, 4 * cols : 5 * cols] = d_values[rows:]
        if layer < last:
            pl.semaphore_wait(far_free, 1)
        far_copy(layer, b).start()

    def send_prev(layer, b):
        base = 1 + 6 * layer
        far_copy(layer, b).wait()
        back = jnp.zeros((rows, cols), F32)
        for which in (1, 2):
            part = pl.ds((which + 2) * cols, cols)
            back = back + nt(d_own[b, :, part], w_block(base + which, j, mine))
            back = back + nt(d_far[b, :, part], w_block(base + which, j, theirs))
        dn_out[layer - 1, b] = back.astype(BF16)
        dn_copy(layer, b).start()

    def take_next(layer, b):
        dn_copy(layer, b).wait_recv()
        dn_forward(layer, b, mine).start()

    def join(layer, b):
        base = 1 + 6 * layer
        if layer > 0:
            dn_forward(layer, b, theirs).wait_recv()
            back = dn_in[layer - 1, b].astype(F32)
        else:
            far_copy(layer, b).wait()
            back = jnp.zeros((rows, width), F32)
        for which in range(3):
            part = pl.ds(which * cols, cols)
            back = back + nt(d_own[b, :, part], w_cols(base + which, mine))
            back = back + nt(d_far[b, :, part], w_cols(base + which, theirs))
        if layer > 0:
            pl.semaphore_signal(far_free, inc=1, device_id=partner, device_id_type=MESH)
        gain = gain_row(2 * layer)
        hat, inv = norm_parts(entry(layer, b))
        add_affine(2 * layer, column_sum(back * hat))
        state[last, b] = state[last, b] + norm_back(back, hat, inv, gain)

    many = nb * rows

    def outer_mlp(layer):
        base = 1 + 6 * layer
        put_total(base + 5, tn(hidden[...].reshape(many, width), low[:, :, mine].reshape(many, cols)))
        put_total(base + 4, tn(n_two[...].reshape(many, width), pre_low[:, :, mine].reshape(many, cols)))

    def outer_mixed(layer):
        base = 1 + 6 * layer
        grad_mid = mid_low[:, :, mine].reshape(many, cols)
        put_total(
            base + 3,
            jnp.concatenate(
                [
                    tn(mixed[layer, :, 0].reshape(many, cols), grad_mid),
                    tn(mixed[layer, :, 1].reshape(many, cols), grad_mid),
                ],
                axis=0,
            ),
        )

    def outer_pair(layer):
        base = 1 + 6 * layer
        near = tn(n_own[layer].reshape(many, width), d_own[:, :, 0 : 3 * cols].reshape(many, 3 * cols))
        put_total(base, near[:, 0:cols])
        away = tn(n_prev[layer].reshape(many, width), d_own[:, :, 3 * cols : 5 * cols].reshape(many, 2 * cols))
        put_total(base + 1, near[:, cols : 2 * cols] + away[:, 0:cols])
        put_total(base + 2, near[:, 2 * cols : 3 * cols] + away[:, cols : 2 * cols])

    def encode_back(b):
        back = nn(g_col[...], state[last, b].astype(BF16)) * (1.0 / k_g)
        back = (back.astype(BF16).astype(F32) * silu_slope(pre_encode(rows_in, b))).astype(BF16)
        low[b] = back
        add_affine(8, column_sum(back.astype(F32)))
        back = jnp.zeros((rows, width), F32)
        for which in (1, 2):
            part = pl.ds((which + 2) * cols, cols)
            back = back + nt(d_own[b, :, part], w_cols(1 + which, mine))
            back = back + nt(d_far[b, :, part], w_cols(1 + which, theirs))
        gain = gain_row(0)
        hat, inv = norm_parts(start_prev[b].astype(F32))
        add_affine(0, column_sum(back * hat))
        back = nn(gp_col[...], norm_back(back, hat, inv, gain).astype(BF16)) * (1.0 / k_g)
        back = (back.astype(BF16).astype(F32) * silu_slope(pre_encode(rows_prev, b))).astype(BF16)
        mid_low[b] = back
        add_affine(8, column_sum(back.astype(F32)))

    each(encode, hooks=(None, lambda: gather_step(4)))
    gather_step(5)

    def first_project(b):
        project(0, b)

    each(first_project)
    gather_step(6)
    done = 7
    for layer in range(last):

        def attend_this(b, layer=layer):
            attend(layer, b)

        def take_first(b, layer=layer):
            take_prev(layer, b)

        def mlp_this(b, layer=layer):
            mlp(layer, b)

        def project_next(b, layer=layer):
            project(layer + 1, b)

        if layer > 0:
            each(take_first)
        staggered(
            attend_this,
            mlp_this,
            project_next,
            hooks=(None, lambda k=done: gather_step(k), lambda k=done + 1: gather_step(k)),
        )
        gather_step(done + 2)
        done = done + 3

    def ready_last():
        for step in range(done, len(sz.groups) + 3):
            gather_step(step)
        scalars[1] = tile_end(0) if sz.fused else jnp.broadcast_to(weight_ref[...], (8, 128))

    def take_last(b):
        take_prev(last, b)

    def attend_last(b):
        attend(last, b)

    def turn(b):
        mlp(last, b)
        decode(b)
        mlp_back(last, b)
        attend_back(last, b)

    def send_last(b):
        if last > 0:
            send_prev(last, b)

    staggered(take_last, attend_last, turn, send_last, hooks=(None, None, ready_last))
    outer_mlp(last)
    outer_mixed(last)
    summed(1, 2 * last + 2)
    outer_pair(last)
    summed(1, 2 * last + 1)
    for layer in reversed(range(last)):

        def take_this(b, layer=layer):
            take_next(layer + 1, b)

        def back_this(b, layer=layer):
            join(layer + 1, b)
            mlp_back(layer, b)

        def pair_this(b, layer=layer):
            attend_back(layer, b)

        def send_this(b, layer=layer):
            if layer > 0:
                send_prev(layer, b)

        u = 2 * layer
        staggered(
            take_this, back_this, hooks=(None, None, None, lambda u=u: summed(2, u + 4))
        )
        outer_mlp(layer)
        outer_mixed(layer)
        summed(1, u + 2)
        summed(2, u + 3)
        hooks = (None, lambda u=u: summed(3, u + 4), lambda u=u: summed(2, u + 2))
        if layer > 0:
            staggered(pair_this, send_this, hooks=hooks)
        else:
            each(pair_this, hooks=hooks)
        outer_pair(layer)
        summed(1, u + 1)
        summed(3, u + 3)
        summed(4, u + 4)
        if layer > 0:
            summed(4, u + 3)

    def last_back(b):
        join(0, b)
        encode_back(b)

    each(last_back, hooks=(None, lambda: summed(3, 2)))
    wide = jnp.concatenate([affine_grad[...], jnp.zeros((112, width), F32)], axis=0)

    @pl.when(j == 0)
    def _():
        put_total(
            0,
            tn(low[...].reshape(many, width), rows_in[:, :, :, 0:256].reshape(many, 256))
            + tn(mid_low[...].reshape(many, width), rows_prev[...].reshape(many, 256)),
        )

    @pl.when(j == 1)
    def _():
        put_total(
            0,
            jnp.concatenate(
                [
                    jnp.transpose(wide),
                    tn(final[...].reshape(many, width), grad_pred[...].reshape(many, 128)),
                ],
                axis=1,
            ),
        )

    if sz.fused:
        reduce_one(0)
        reduce_two(1)
        reduce_two(0)
        if sz.layers > 1:
            reduce_four(3)
        reduce_three(1)
        reduce_three(0)
        reduce_four(2)
        for unit in range(2, len(sz.units)):
            reduce_done(unit)
        reduce_four(1)
        reduce_four(0)
        squares = jnp.sum(square_acc[...], axis=1, keepdims=True)
        sub = lax.broadcasted_iota(jnp.int32, (8, 128), 0)
        tile[1, 0] = jnp.where(sub == 0, squares, loss_acc[0:1, 0:1])
        tile_start(1)
        reduce_done(1)
        reduce_done(0)
        result = tile_end(1)
        scalars[0] = jnp.broadcast_to(result[1:2, :], (8, 128))
        scalars[2] = jnp.broadcast_to(jnp.sqrt(result[0:1, :]), (8, 128))
    else:
        scalars[0] = loss_acc[...]
        scalars[2] = loss_acc[...]

    for make in waits:
        make().wait_send()
    for layer in range(sz.layers):
        for b in range(nb):
            mix_copy(layer, b).wait_send()
            if layer > 0:
                n_copy(layer, b).wait_send()
                n_forward(layer, b, mine).wait_send()
                dn_copy(layer, b).wait_send()
                dn_forward(layer, b, mine).wait_send()


def dma(*shape):
    return pltpu.SemaphoreType.DMA(shape)


def train_kernel(sz, operands):
    nb, rows, half, width, cols = sz.batches, sz.rows, sz.half, sz.width, sz.cols
    layers = sz.layers
    scratch = []
    if sz.fused:
        out_shape = (
            jax.ShapeDtypeStruct((sz.mats, sz.shard, width), F32),
            jax.ShapeDtypeStruct((3, 8, 128), F32),
        )
        scratch += [
            pltpu.VMEM((sz.mats, sz.depth, 2, 2, 2, sz.shard, width), BF16),
            pltpu.VMEM((sz.mats, sz.depth, 2, 2, 2, sz.shard, cols), F32),
        ]
        scratch += [pltpu.VMEM(value.shape, value.dtype) for value in operands]
        scratch += [dma(len(operands))]
    else:
        out_shape = (
            jax.ShapeDtypeStruct((sz.mats, width, cols), F32),
            jax.ShapeDtypeStruct((3, 8, 128), F32),
        )
    scratch += [
        pltpu.VMEM((nb, half, 384), BF16),
        pltpu.VMEM((nb, 2, half, 384), BF16),
        pltpu.VMEM((nb, 2, half, 256), BF16),
        pltpu.VMEM((3, 32, rows), jnp.int32),
        pltpu.VMEM((nb, rows, width), BF16),
        pltpu.VMEM((nb, rows, width), BF16),
        pltpu.VMEM((layers, nb, rows, width), F32),
        pltpu.VMEM(((layers - 1) * nb + 1, rows, width), F32),
        pltpu.VMEM(((layers - 1) * nb + 1, rows, width), F32),
        pltpu.VMEM((layers, nb, 2, rows, cols), BF16),
        pltpu.VMEM((layers, nb, rows, cols), BF16),
        pltpu.VMEM((layers, nb, 2, 2 * rows, cols), BF16),
        pltpu.VMEM(((layers - 1) * nb + 1, sz.near, rows, 2 * rows), BF16),
        pltpu.VMEM((rows, 2 * rows), F32),
    ]
    scratch += [pltpu.VMEM((rows, rows), BF16)] * 6
    scratch += [pltpu.VMEM((16, width), F32)] * 2
    scratch += [
        pltpu.VMEM((nb, rows, width), BF16),
        pltpu.VMEM((nb, rows, 128), BF16),
        pltpu.VMEM((nb, rows, width), BF16),
        pltpu.VMEM((nb, rows, width), BF16),
        pltpu.VMEM((nb, rows, width), BF16),
        pltpu.VMEM((layers, nb, rows, width), BF16),
        pltpu.VMEM((layers, nb, rows, width), BF16),
        pltpu.VMEM((nb, rows, width), BF16),
        pltpu.VMEM((nb, rows, width), BF16),
        pltpu.VMEM((nb, rows, 5 * cols), BF16),
        pltpu.VMEM((nb, rows, 5 * cols), BF16),
        pltpu.VMEM((max(layers - 1, 1), nb, rows, cols), BF16),
        pltpu.VMEM((max(layers - 1, 1), nb, rows, width), BF16),
        pltpu.VMEM((8, 128), F32),
        pltpu.VMEM((1, cols), F32),
    ]
    scratch += [dma(3), dma(3), dma(2), dma(2), dma(2), dma(2)] + [dma(layers, nb)] * 12
    scratch += [pltpu.SemaphoreType.REGULAR]
    if sz.fused:
        depth, groups, units = sz.depth, len(sz.groups), len(sz.units)
        lane = cols // 2
        one_shape = (2, sz.mats, depth, 2, 2, sz.shard, lane)
        two_shape = (2, sz.mats, depth, 2, sz.shard, lane)
        scratch += [pltpu.VMEM(one_shape, jnp.int16)] * 2 + [pltpu.VMEM(two_shape, jnp.int16)] * 2
        scratch += [
            pltpu.VMEM((sz.mats, depth, 2, sz.shard, cols), jnp.int16),
            pltpu.VMEM((depth - 1, sz.mats, 2, sz.shard, cols), jnp.int16),
            pltpu.VMEM((sz.mats, sz.shard, cols), F32),
            pltpu.VMEM((2, 2, sz.mats, 8, lane), F32),
            pltpu.VMEM((2, 2, sz.mats, 8, lane), F32),
            pltpu.VMEM((sz.mats, 8, cols), F32),
            pltpu.VMEM((depth - 1, sz.mats, 8, cols), F32),
            pltpu.VMEM((2, 2, 8, 128), F32),
            pltpu.VMEM((2, 8, 128), F32),
            pltpu.VMEM((2, 4 * depth, 8, 128), F32),
        ]
        far = [dma(groups, depth - 1)] * 2
        scratch += far + [dma(groups, 2)] * 4 + [dma(groups)] * 2
        scratch += [dma(units, 4, 2)] * 2 + [dma(units, 2, depth - 1)] * 2 + [dma(units)] * 2
        scratch += [dma(2)] * 2 + [dma(2, 4 * depth - 1)] * 2
    return pl.pallas_call(
        functools.partial(step_kernel, sz),
        out_shape=out_shape,
        in_specs=[pl.BlockSpec(memory_space=pl.ANY if sz.fused else pltpu.VMEM)] * len(operands),
        out_specs=(pl.BlockSpec(memory_space=pltpu.VMEM),) * 2,
        scratch_shapes=scratch,
        compiler_params=pltpu.CompilerParams(
            collective_id=0, has_side_effects=True, vmem_limit_bytes=60 * 1024 * 1024
        ),
    )(*operands)


def adam(weight, first, second, grad):
    first_new = BETA_ONE * first + (1.0 - BETA_ONE) * grad
    second_new = BETA_TWO * second + (1.0 - BETA_TWO) * grad * grad
    first_hat = first_new / (1.0 - BETA_ONE**STEP)
    second_hat = second_new / (1.0 - BETA_TWO**STEP)
    weight_new = weight - RATE * (first_hat / (jnp.sqrt(second_hat) + ADAM_EPS) + DECAY * weight)
    return (weight_new, first_new, second_new, weight_new.astype(BF16))


def adam_kernel(sz, share, scalars, *refs):
    masters = refs[:15]
    outs = refs[15:35]
    for index, ref in enumerate(refs[35:38]):
        ref[...] = scalars[index, 0:1, 0:1]
    mat, inp, out, gain, bias = [masters[3 * k : 3 * k + 3] for k in range(5)]
    factor = jnp.minimum(1.0, CLIP / (scalars[2, 0:1, 0:1] + 1e-06))

    def put(k, values):
        for ref, value in zip(outs[4 * k : 4 * k + 4], values):
            ref[...] = value

    for index in range(sz.mats - 1):
        values = adam(mat[0][index], mat[1][index], mat[2][index], factor * share[1 + index])
        for ref, value in zip(outs[0:4], values):
            ref[index] = value
    last = share[0]
    put(1, adam(inp[0][...], inp[1][...], inp[2][...], factor * last[:, 0 : sz.c_in]))
    put(2, adam(out[0][...], out[1][...], out[2][...], factor * last[:, 384 : 384 + sz.c_out]))
    small = jnp.concatenate([last[:, 256:384], jnp.zeros((128 - sz.shard, 128), F32)], axis=0)
    small = jnp.transpose(small)[:, 0 : sz.shard]
    count = gain[0].shape[0]
    put(3, adam(gain[0][...], gain[1][...], gain[2][...], factor * small[0:count]))
    put(4, adam(bias[0][...], bias[1][...], bias[2][...], factor * small[8 : 8 + count]))


def update(sz, share, scalars, groups):
    operands = [share, scalars]
    out_shape = []
    for triple in groups:
        operands += list(triple)
        shape = triple[0].shape
        out_shape += [jax.ShapeDtypeStruct(shape, F32)] * 3 + [jax.ShapeDtypeStruct(shape, BF16)]
    out_shape += [jax.ShapeDtypeStruct((1, 1), F32)] * 3
    return pl.pallas_call(
        functools.partial(adam_kernel, sz),
        out_shape=tuple(out_shape),
        in_specs=[pl.BlockSpec(memory_space=pltpu.VMEM)] * len(operands),
        out_specs=(pl.BlockSpec(memory_space=pltpu.VMEM),) * len(out_shape),
    )(*operands)


def per_device(
    grid_in, targets, area, row_count, g2m, m2g, senders, edge_count,
    mat_w, mat_m, mat_v, in_w, in_m, in_v, out_w, out_m, out_v,
    gain_w, gain_m, gain_v, bias_w, bias_m, bias_v,
):
    axes = ("node", "feat")
    sz = Sizes(
        lax.axis_size("node"),
        lax.axis_size("feat"),
        grid_in.shape[0],
        grid_in.shape[1],
        mat_w.shape[2],
        mat_w.shape[0] // 6,
        HEADS,
        senders.shape[1],
        grid_in.shape[2],
        targets.shape[2],
    )
    operands = [
        jnp.swapaxes(grid_in, 1, 2),
        jnp.swapaxes(targets, 1, 2),
        area.reshape(1, -1),
        row_count.T,
        g2m.T,
        m2g.T,
        senders.T,
        edge_count.reshape(1, -1),
    ]
    if sz.fused:
        operands += [mat_w, in_w.T, out_w, gain_w, bias_w]
        share, scalars = train_kernel(sz, operands)
        groups = (
            (mat_w, mat_m, mat_v),
            (in_w.T, in_m.T, in_v.T),
            (out_w, out_m, out_v),
            (gain_w, gain_m, gain_v),
            (bias_w, bias_m, bias_v),
        )
        outs = list(update(sz, share, scalars, groups))
        for index in range(4, 8):
            outs[index] = outs[index].T
        for index in range(20, 23):
            outs[index] = outs[index].reshape(())
        return tuple(outs)

    width, shard = sz.width, sz.shard

    def pad(value, size):
        return jnp.pad(value, ((0, 0), (0, size - value.shape[1])))

    def pack(square, inp, out, gain, bias):
        small = jnp.concatenate([pad(gain.T, 8), pad(bias.T, 120)], axis=1)
        first = jnp.concatenate([pad(inp.T, 256), small, pad(out, 128)], axis=1)
        return jnp.concatenate([first[None], square], axis=0)

    packed = pack(mat_w, in_w, out_w, gain_w, bias_w).astype(BF16)
    full = lax.all_gather(packed, axes, axis=1, tiled=True).reshape(sz.mats, 2, width // 2, width)
    live = (jnp.arange(sz.half)[None, :] < row_count).astype(F32)
    weight_total = lax.psum(jnp.sum(area[None, :] * live) * targets.shape[2], axes)
    operands += [full, weight_total.reshape(1, 1)]
    part, scalars = train_kernel(sz, operands)
    feat = lax.axis_index("feat")
    spread = lax.dynamic_update_slice(
        jnp.zeros((sz.mats, width, width), F32), part, (0, 0, feat * sz.cols)
    )
    share = lax.psum_scatter(spread, axes, scatter_dimension=1, tiled=True)
    square_sum, loss_sum = lax.psum((jnp.sum(share * share), scalars[0, 0, 0]), axes)
    grad_norm = jnp.sqrt(square_sum)
    share = jnp.minimum(1.0, CLIP / (grad_norm + 1e-06)) * share
    count = gain_w.shape[0]
    last = share[0]
    outs = adam(mat_w, mat_m, mat_v, share[1:])
    outs += adam(in_w, in_m, in_v, last[:, 0 : sz.c_in].T)
    outs += adam(out_w, out_m, out_v, last[:, 384 : 384 + sz.c_out])
    outs += adam(gain_w, gain_m, gain_v, last[:, 256 : 256 + count].T)
    outs += adam(bias_w, bias_m, bias_v, last[:, 264 : 264 + count].T)
    return outs + (loss_sum, weight_total, grad_norm)


def solution(mesh):
    both = ("node", "feat")
    rows_three = P(None, both, None)
    second = P(None, both)
    first = P(both, None)
    placed = (
        rows_three, rows_three, P(both), second,
        P("node", None), P("node", None), P("node", None), P("node"),
    )
    placed += (rows_three,) * 3 + (second,) * 3 + (first,) * 3 + (second,) * 6
    outs = (rows_three,) * 4 + (second,) * 4 + (first,) * 4 + (second,) * 8 + (P(), P(), P())
    return jax.shard_map(per_device, mesh=mesh, in_specs=placed, out_specs=outs, check_vma=False)
```
